32 devices in a mesh: stream: 2 (over x), dp: 16 (over z, y, core).
Axes of the slice: x: 2, y: 2, z: 4, core: 2. Of those that a mesh axis runs over, the one named last changes fastest.
Arguments:
- tokens: bfloat16 [2, 16384, 768], P('stream', 'dp'), may hold values from -6 to 6
- lengths: int32 [16, 8], P('dp'), may hold values from 0 to 1024, as said below
- pad_mask: int32 [16384], P('dp'), may hold values 0 or 1
- first_gain: float32 [768], replicated, may hold values from 0.5 to 1.5
- first_bias: float32 [768], replicated, may hold values from -1 to 1
- query_weight: bfloat16 [768, 768], replicated, may hold values from -0.21875 to 0.21875
- key_weight: bfloat16 [768, 768], replicated, may hold values from -0.21875 to 0.21875
- value_weight: bfloat16 [768, 768], replicated, may hold values from -0.21875 to 0.21875
- out_weight: bfloat16 [768, 768], replicated, may hold values from -0.875 to 0.875
- second_gain: float32 [768], replicated, may hold values from 0.5 to 1.5
- second_bias: float32 [768], replicated, may hold values from -1 to 1
- up_weight: bfloat16 [768, 3072], replicated, may hold values from -0.21875 to 0.21875
- down_weight: bfloat16 [3072, 768], replicated, may hold values from -0.109375 to 0.109375
- output_grad: bfloat16 [2, 16384, 768], P('stream', 'dp'), may hold values from -6 to 6
Outputs:
- layer_output: bfloat16 [2, 16384, 768], P('stream', 'dp')
- tokens_grad: float32 [2, 16384, 768], P('stream', 'dp')
- first_grads: float32 [2, 768], P(None, ('stream', 'dp'))
- query_grad: float32 [768, 768], P(('stream', 'dp'))
- key_grad: float32 [768, 768], P(('stream', 'dp'))
- value_grad: float32 [768, 768], P(('stream', 'dp'))
- out_grad: float32 [768, 768], P(None, ('stream', 'dp'))
- second_grads: float32 [2, 768], P(None, ('stream', 'dp'))
- up_grad: float32 [768, 3072], P(('stream', 'dp'))
- down_grad: float32 [3072, 768], P(None, ('stream', 'dp'))
The draws below stay inside these ranges and needn't reach their ends.
Inputs may be any that keep to these rules, and one draw needn't show every extreme that they name: Row i gives, in order, the lengths of the documents of the pack on dp index i: each a multiple of 128, together 1024, zeros after the last one. One row, chosen by the seed, is a single document.
All inputs are finite; a program needn't handle non-finite values. No bound on the sum of `pad_mask` on one device may be relied on, other than what follows from the above.
Results may differ from the reference program's by a relative error of at most 0.012.
Values may be sent and summed in bfloat16 or wider, within the bound.
A program may use at most 384 MiB of HBM per device.

```python
import math
import jax
import jax.numpy as jnp
from jax import lax

H = 12
D = 768
FF = 3072
BLOCK = 16
UNIT = 128
ROWS = 1024
UNITS = 8
TOKENS = 16384
N_DP = 16


def draw_lengths(key, part):
    key = jax.random.fold_in(key, 11)
    cut_key, pick_key = jax.random.split(key)
    slot_count = ROWS // UNIT
    cut_flags = jax.random.randint(cut_key, (N_DP, slot_count), 0, 2)
    chosen = jax.random.randint(pick_key, (), 0, N_DP)
    row_index = jnp.arange(N_DP)[:, None]
    first_slot = (jnp.arange(slot_count) == 0)[None, :]
    cut_flags = jnp.where(first_slot, 1, jnp.where(row_index == chosen, 0, cut_flags))
    doc_index = jnp.cumsum(cut_flags, axis=1) - 1
    one_hot = (doc_index[:, :, None] == jnp.arange(slot_count)[None, None, :]).astype(jnp.int32)
    return (jnp.sum(one_hot, axis=1) * UNIT).astype(jnp.int32)


def plant(entries, own_key, low, top_value):
    spot = [jax.random.randint(jax.random.fold_in(own_key, axis), (), 0, length) for axis, length in enumerate(entries.shape)]
    widest = entries.shape.index(max(entries.shape))
    neighbour = spot[:widest] + [(spot[widest] + 1) % entries.shape[widest]] + spot[widest + 1:]
    return entries.at[tuple(spot)].set(low).at[tuple(neighbour)].set(top_value)


def raised(drawn, key, source, target, blocks, factor):
    def block_of(dim):
        return (jnp.arange(drawn.shape[dim]) // (drawn.shape[dim] // blocks)).reshape((-1,) + (1,) * (drawn.ndim - 1 - dim))

    first = jax.random.permutation(key, blocks)[block_of(target)]
    far = (block_of(target) + blocks // 2) % blocks
    return jnp.where((block_of(source) == first) | (block_of(source) == far), factor * drawn, drawn)


def block_levels(rng, dims, cuts, low, largest):
    def one(dim, parts):
        heights = jax.random.uniform(jax.random.fold_in(jax.random.fold_in(rng, 6), dim), (parts,), jnp.float32, low / len(cuts), largest / len(cuts))
        return jnp.repeat(jnp.exp(heights), dims[dim] // parts).reshape((-1,) + (1,) * (len(dims) - dim - 1))

    gain = one(*cuts[0])
    for cut in cuts[1:]:
        gain = gain * one(*cut)
    return gain


def centred(key, dims, scale, reach, cuts=(), kind=jnp.bfloat16):
    loudness = block_levels(key, dims, cuts, -0.22, 0.18) if cuts else 1.0
    values = jax.random.normal(key, dims, jnp.float32) * scale * loudness
    return jnp.minimum(jnp.maximum(values, -reach), reach).astype(kind)


def noise_with(key, dims, scale, most, cuts, heavy, kind=jnp.bfloat16):
    array = scale * jax.random.normal(key, dims, jnp.float32)
    if cuts:
        array = array * block_levels(key, dims, cuts, -0.22, 0.18)
    return jnp.clip(raised(array, jax.random.fold_in(key, 3), *heavy), -most, most).astype(kind)


def setup_inputs(seed: int = 0) -> dict:
    keys = jax.random.split(jax.random.key(seed), 15)
    tokens = centred(keys[0], (2, TOKENS, D), 1.0, 6.0, ((0, 2), (1, 16)))
    lengths = draw_lengths(jax.random.fold_in(keys[14], 71), 0)
    pad_mask = plant((jax.random.randint(keys[2], (TOKENS,), 0, 8) < 7).astype(jnp.int32), jax.random.fold_in(keys[2], 1), 0, 1)
    first_gain = jnp.clip(1.0 + 0.1 * jax.random.normal(keys[3], (D,), jnp.float32), 0.5, 1.5)
    first_bias = centred(keys[4], (D,), 0.2, 1.0, (), jnp.float32)
    query_weight = centred(keys[5], (D, D), D ** -0.5, 0.21875)
    key_weight = centred(keys[6], (D, D), D ** -0.5, 0.21875)
    value_weight = centred(keys[7], (D, D), D ** -0.5, 0.21875)
    out_weight = centred(keys[8], (D, D), (D // 16) ** -0.5, 0.875)
    second_gain = jnp.clip(1.0 + 0.1 * jax.random.normal(keys[9], (D,), jnp.float32), 0.5, 1.5)
    second_bias = centred(keys[10], (D,), 0.2, 1.0, (), jnp.float32)
    up_weight = centred(keys[11], (D, FF), D ** -0.5, 0.21875)
    down_weight = centred(keys[12], (FF, D), FF ** -0.5, 0.109375)
    output_grad = noise_with(keys[13], (2, TOKENS, D), 1.0, 6.0, ((0, 2), (1, 16)), (1, 2, 16, 2.0))
    return {"tokens": tokens, "lengths": lengths, "pad_mask": pad_mask, "first_gain": first_gain, "first_bias": first_bias, "query_weight": query_weight, "key_weight": key_weight, "value_weight": value_weight, "out_weight": out_weight, "second_gain": second_gain, "second_bias": second_bias, "up_weight": up_weight, "down_weight": down_weight, "output_grad": output_grad}


@jax.custom_vjp
def low(v):
    return lax.optimization_barrier(v.astype(jnp.bfloat16)).astype(jnp.float32)

@jax.custom_vjp
def low_back(v):
    return v

def low_keep(v):
    return (low(v), None)

def low_pass(kept, grad):
    return (grad,)

def back_keep(v):
    return (v, None)

def back_low(kept, grad):
    return (low(grad),)
low.defvjp(low_keep, low_pass)
low_back.defvjp(back_keep, back_low)
epsilon = 1e-05
masked_score = -1e+30
highest = lax.Precision.HIGHEST

def product(left, right):
    return jnp.dot(left, right, precision=highest)

def layer_norm(values, gain_row, bias_row):
    centre = values - lax.optimization_barrier(jnp.mean(values, axis=-1, keepdims=True))
    spread = lax.optimization_barrier(jnp.mean(centre * centre, axis=-1, keepdims=True))
    return centre * lax.rsqrt(spread + epsilon) * gain_row + bias_row

def layout(lengths_row, total_rows, doc_slots):
    places = jnp.arange(total_rows, dtype=jnp.int32)
    end_places = jnp.cumsum(lengths_row).astype(jnp.int32)
    starts = (end_places - lengths_row).astype(jnp.int32)
    document = lax.optimization_barrier(jnp.sum((places[:, None] >= end_places[None, :]).astype(jnp.int32), axis=1)).astype(jnp.int32)
    picked = document[:, None] == jnp.arange(doc_slots, dtype=jnp.int32)[None, :]
    first_place = lax.optimization_barrier(jnp.sum(jnp.where(picked, starts[None, :], 0), axis=1)).astype(jnp.int32)
    return (places, document, (places - first_place).astype(jnp.int32))

def angles(position, head_width):
    half_width = head_width // 2
    freq_index = jnp.arange(half_width).astype(jnp.float32)
    frequency = jnp.exp(freq_index * (-2.0 * math.log(10000.0) / head_width))
    turned = position.astype(jnp.float32)[:, None] * frequency[None, :]
    return (jnp.cos(turned)[:, None, :], jnp.sin(turned)[:, None, :])

def rotate(values, cosine_table, sine_table):
    half_width = values.shape[-1] // 2
    first_half = values[..., :half_width]
    second_half = values[..., half_width:]
    return jnp.concatenate([first_half * cosine_table - second_half * sine_table, second_half * cosine_table + first_half * sine_table], axis=-1)

def attend_block(query_block, query_info, keys_all, values_all, key_info, score_scale):
    query_stream, query_doc, query_blk, query_place = query_info
    key_stream, key_doc, key_blk, key_place, key_pad = key_info
    same_doc = query_doc[:, None] == key_doc[None, :]
    usable = key_pad[None, :] == 1
    kept = usable | (query_place[:, None] == key_place[None, :])
    clean_query = query_stream[:, None] == 0
    noisy_query = query_stream[:, None] == 1
    clean_key = key_stream[None, :] == 0
    noisy_key = key_stream[None, :] == 1
    clean_self = clean_query & clean_key & (key_blk[None, :] <= query_blk[:, None]) & kept
    noisy_self = noisy_query & noisy_key & (key_blk[None, :] == query_blk[:, None]) & kept
    crossing = noisy_query & clean_key & (key_blk[None, :] < query_blk[:, None]) & usable
    allowed = same_doc & (clean_self | noisy_self | crossing)
    raw_scores = jnp.einsum('qhd,khd->hqk', query_block, keys_all, precision=highest) * score_scale
    scores = jnp.where(allowed[None], low_back(raw_scores), masked_score)
    topmost = lax.optimization_barrier(jnp.max(scores, axis=2, keepdims=True))
    weights = jnp.exp(scores - topmost)
    weights = weights / lax.optimization_barrier(jnp.sum(weights, axis=2, keepdims=True))
    return jnp.einsum('hqk,khd->qhd', low(weights), values_all, precision=highest)

def forward(streams, params, document, places, within, padding):
    first_gain, first_bias, query_weight, key_weight, value_weight, out_weight, second_gain, second_bias, up_weight, down_weight = params
    model_width = streams.shape[-1]
    head_width = model_width // H
    double_rows = 2 * ROWS
    rows_all = streams.reshape(double_rows, model_width)
    normed = low(layer_norm(rows_all, first_gain, first_bias))
    position = jnp.concatenate([within, within])
    cosine_table, sine_table = angles(position, head_width)
    queries = low(rotate(low_back(product(normed, query_weight)).reshape(double_rows, H, head_width), cosine_table, sine_table))
    keys_all = low(rotate(low_back(product(normed, key_weight)).reshape(double_rows, H, head_width), cosine_table, sine_table))
    values_all = low(low_back(product(normed, value_weight))).reshape(double_rows, H, head_width)
    stream_ids = jnp.concatenate([jnp.zeros((ROWS,), jnp.int32), jnp.ones((ROWS,), jnp.int32)])
    doc_all = jnp.concatenate([document, document])
    blk_all = jnp.concatenate([places // BLOCK, places // BLOCK]).astype(jnp.int32)
    place_all = jnp.concatenate([places, places])
    pad_all = jnp.concatenate([padding, padding])
    block_rows = min(ROWS, 512)
    block_count = double_rows // block_rows
    key_info = (stream_ids, doc_all, blk_all, place_all, pad_all)
    score_scale = head_width ** (-0.5)

    def one_block(pieces):
        return attend_block(pieces[0], pieces[1:], keys_all, values_all, key_info, score_scale)
    attended = lax.map(jax.checkpoint(one_block), (queries.reshape(block_count, block_rows, H, head_width), stream_ids.reshape(block_count, block_rows), doc_all.reshape(block_count, block_rows), blk_all.reshape(block_count, block_rows), place_all.reshape(block_count, block_rows)))
    mixed = low(low_back(attended.reshape(double_rows, model_width)))
    middle = rows_all + low_back(product(mixed, out_weight))
    normed_second = low(layer_norm(middle, second_gain, second_bias))
    hidden = low_back(product(normed_second, up_weight))
    activated = low(jax.nn.gelu(hidden))
    return (middle + low_back(product(activated, down_weight))).reshape(2, ROWS, model_width)

def reference(tokens, lengths, pad_mask, first_gain, first_bias, query_weight, key_weight, value_weight, out_weight, second_gain, second_bias, up_weight, down_weight, output_grad):
    model_width = tokens.shape[-1]
    params = (first_gain.astype(jnp.float32), first_bias.astype(jnp.float32), query_weight.astype(jnp.float32), key_weight.astype(jnp.float32), value_weight.astype(jnp.float32), out_weight.astype(jnp.float32), second_gain.astype(jnp.float32), second_bias.astype(jnp.float32), up_weight.astype(jnp.float32), down_weight.astype(jnp.float32))
    streams = tokens.astype(jnp.float32).reshape(2, N_DP, ROWS, model_width).transpose(1, 0, 2, 3)
    cotangents = output_grad.astype(jnp.float32).reshape(2, N_DP, ROWS, model_width).transpose(1, 0, 2, 3)
    paddings = pad_mask.reshape(N_DP, ROWS)

    def per_pack(running, pieces):
        stream_pack, cotangent, lengths_row, padding = pieces
        places, document, within = layout(lengths_row, ROWS, UNITS)

        def closed(stream_arg, param_arg):
            return forward(stream_arg, param_arg, document, places, within, padding)
        result, pullback = jax.vjp(closed, stream_pack, params)
        input_grad, param_grads = pullback(cotangent)
        running = jax.tree.map(lambda left, right: left + right, running, param_grads)
        return (running, (result.astype(jnp.bfloat16), input_grad))
    zeros_init = jax.tree.map(jnp.zeros_like, params)
    totals, (results, input_grads) = lax.scan(per_pack, zeros_init, (streams, cotangents, lengths, paddings))
    layer_output = results.transpose(1, 0, 2, 3).reshape(2, TOKENS, model_width)
    tokens_grad = input_grads.transpose(1, 0, 2, 3).reshape(2, TOKENS, model_width)
    return (layer_output, tokens_grad, jnp.stack([totals[0], totals[1]]), totals[2], totals[3], totals[4], totals[5], jnp.stack([totals[6], totals[7]]), totals[8], totals[9])
```

```python
import functools
import math

import jax
import jax.numpy as jnp
from jax import lax
from jax.experimental import pallas as pl
from jax.experimental.pallas import tpu as pltpu
from jax.sharding import PartitionSpec as P

H = 12
BLOCK = 16
TILE = 256
SUB = 128
LANES = 128

epsilon = 1e-05
masked_score = -1e30
MIB = 1024 * 1024


def layer_norm(values, gain_row, bias_row):
    centre = values - jnp.mean(values, axis=-1, keepdims=True)
    spread = jnp.mean(centre * centre, axis=-1, keepdims=True)
    return centre * lax.rsqrt(spread + epsilon) * gain_row + bias_row


def layout(lengths_row, total_rows, doc_slots):
    places = jnp.arange(total_rows, dtype=jnp.int32)
    end_places = jnp.cumsum(lengths_row)
    starts = end_places - lengths_row
    document = jnp.sum((places[:, None] >= end_places[None, :]).astype(jnp.int32), axis=1)
    picked = document[:, None] == jnp.arange(doc_slots, dtype=jnp.int32)[None, :]
    first_place = jnp.sum(jnp.where(picked, starts[None, :], 0), axis=1)
    return (places, first_place)


def angle_tables(position, head_width):
    half_width = head_width // 2
    freq_index = (jnp.arange(half_width)).astype(jnp.float32)
    frequency = jnp.exp(freq_index * (-2.0 * math.log(10000.0) / head_width))
    turned = position.astype(jnp.float32)[:, None] * frequency[None, :]
    cosine, sine = jnp.cos(turned), jnp.sin(turned)
    return (
        jnp.concatenate([cosine] * 4, axis=1),
        jnp.concatenate([-sine, sine, -sine, sine], axis=1),
    )


def turn(values, cosine, sine):
    lane = lax.broadcasted_iota(jnp.int32, values.shape, 1)
    low = lax.rem(lane, 64) < 32
    partner = jnp.where(low, pltpu.roll(values, LANES - 32, 1), pltpu.roll(values, 32, 1))
    return values * cosine + partner * sine


def nt(left, right):
    return lax.dot_general(
        left, right, (((1,), (1,)), ((), ())), preferred_element_type=jnp.float32
    )


def tn(left, right):
    return lax.dot_general(
        left, right, (((0,), (0,)), ((), ())), preferred_element_type=jnp.float32
    )


def nn(left, right):
    return jnp.dot(left, right, preferred_element_type=jnp.float32)


def project_kernel(score_scale, x_ref, gain_ref, bias_ref, cos_ref, sin_ref, *refs):
    count = (len(refs) - 1) // 2
    weights, outs = refs[:count], refs[count:]
    h1 = layer_norm(x_ref[...].astype(jnp.float32), gain_ref[...], bias_ref[...]).astype(
        jnp.bfloat16
    )
    outs[0][...] = h1
    cosine, sine = cos_ref[...], sin_ref[...]
    for index, (weight, out) in enumerate(zip(weights, outs[1:])):
        product = nn(h1, weight[...])
        is_value = index == count - 1
        is_query = count == 3 and index == 0
        if is_value:
            out[...] = product.astype(jnp.bfloat16)
            continue
        for pair in range(product.shape[1] // LANES):
            columns = slice(pair * LANES, (pair + 1) * LANES)
            turned = turn(product[:, columns], cosine, sine)
            if is_query:
                turned = turned * score_scale
            out[:, columns] = turned.astype(jnp.bfloat16)


def project(x, gain, bias, cosine, sine, weights, score_scale):
    rows, width = x.shape
    count = len(weights)
    row_spec = pl.BlockSpec((TILE, width), lambda i: (i, 0))
    table_spec = pl.BlockSpec((TILE, LANES), lambda i: (i, 0))
    whole = pl.BlockSpec((width, width), lambda i: (0, 0))
    line = pl.BlockSpec((1, width), lambda i: (0, 0))
    return pl.pallas_call(
        functools.partial(project_kernel, score_scale),
        grid=(rows // TILE,),
        in_specs=[row_spec, line, line, table_spec, table_spec] + [whole] * count,
        out_specs=[row_spec] * (count + 1),
        out_shape=[jax.ShapeDtypeStruct((rows, width), jnp.bfloat16)] * (count + 1),
        compiler_params=pltpu.CompilerParams(vmem_limit_bytes=40 * MIB),
        cost_estimate=pl.CostEstimate(
            flops=2 * rows * width * width * count,
            bytes_accessed=2 * (rows + count * (width + rows)) * width,
            transcendentals=0,
        ),
        name="project%d" % count,
    )(x, gain, bias, cosine, sine, *weights)


def two_heads(block):
    lane = lax.broadcasted_iota(jnp.int32, block.shape, 1)
    zero = jnp.zeros_like(block)
    return jnp.concatenate(
        [jnp.where(lane < 64, block, zero), jnp.where(lane < 64, zero, block)], axis=0
    )


def one_row(both):
    rows = both.shape[0] // 2
    lane = lax.broadcasted_iota(jnp.int32, (rows, LANES), 1)
    return jnp.where(lane < 64, both[:rows], both[rows:])


def subs(both, sub):
    low = sub * SUB
    return jnp.concatenate([both[low : low + SUB], both[TILE + low : TILE + low + SUB]], axis=0)


def attend_kernel(rows, q_ref, kb_ref, vb_ref, ko_ref, vo_ref, meta_ref, o_ref, lse_ref, bias, diag, lse):
    pair = pl.program_id(0)

    @pl.when(pair == 0)
    def _():
        columns = jnp.transpose(meta_ref[...])
        noisy = columns[:, 3:4]
        for i in range(rows // TILE):
            band = slice(i * TILE, (i + 1) * TILE)
            n = (i + 1) * TILE
            start, limit = columns[band, 0:1], columns[band, 1:2]
            key = lax.broadcasted_iota(jnp.int32, (TILE, n), 1)
            query = lax.broadcasted_iota(jnp.int32, (TILE, n), 0) + i * TILE
            usable = (meta_ref[2:3, :n] == 1.0) | (key == query)
            place = key.astype(jnp.float32)
            seen = (place >= start) & (place < limit) & usable
            bias[band, :n] = jnp.where(seen, 0.0, masked_score)
            for sub in range(TILE // SUB):
                low = i * TILE + sub * SUB
                key = lax.broadcasted_iota(jnp.int32, (SUB, SUB), 1) + low
                query = lax.broadcasted_iota(jnp.int32, (SUB, SUB), 0) + low
                usable = (meta_ref[2:3, low : low + SUB] == 1.0) | (key == query)
                same = (key // BLOCK == query // BLOCK) & (
                    key.astype(jnp.float32) >= columns[low : low + SUB, 0:1]
                )
                seen = same & usable & (noisy[low : low + SUB] == 1.0)
                diag[low : low + SUB, :] = jnp.where(seen, 0.0, masked_score)

    lane = lax.broadcasted_iota(jnp.int32, (TILE, LANES), 1)
    for i in range(rows // TILE):
        band = slice(i * TILE, (i + 1) * TILE)
        n = (i + 1) * TILE
        q2 = two_heads(q_ref[band, :])
        b = bias[band, :n]
        s = nt(q2, kb_ref[:n, :]) + jnp.concatenate([b, b], axis=0)
        d = diag[band, :]
        parts = [
            nt(subs(q2, sub), ko_ref[i * TILE + sub * SUB : i * TILE + (sub + 1) * SUB, :])
            for sub in range(TILE // SUB)
        ]
        sd = jnp.concatenate(
            [parts[0][:SUB], parts[1][:SUB], parts[0][SUB:], parts[1][SUB:]], axis=0
        ) + jnp.concatenate([d, d], axis=0)
        top = jnp.maximum(
            jnp.max(s, axis=1, keepdims=True), jnp.max(sd, axis=1, keepdims=True)
        )
        p = jnp.exp(s - top)
        pd = jnp.exp(sd - top)
        total = jnp.sum(p, axis=1, keepdims=True) + jnp.sum(pd, axis=1, keepdims=True)
        pd_low = pd.astype(jnp.bfloat16)
        o = nn(p.astype(jnp.bfloat16), vb_ref[:n, :])
        parts = [
            nn(subs(pd_low, sub), vo_ref[i * TILE + sub * SUB : i * TILE + (sub + 1) * SUB, :])
            for sub in range(TILE // SUB)
        ]
        o = o + jnp.concatenate(
            [parts[0][:SUB], parts[1][:SUB], parts[0][SUB:], parts[1][SUB:]], axis=0
        )
        o = o * (1.0 / total)
        o_ref[band, :] = one_row(o).astype(o_ref.dtype)
        level = top + jnp.log(total)
        old = lse[band, :]
        lse[band, :] = jnp.where(
            lane == 2 * pair, level[:TILE], jnp.where(lane == 2 * pair + 1, level[TILE:], old)
        )

    @pl.when(pair == pl.num_programs(0) - 1)
    def _():
        lse_ref[...] = jnp.transpose(lse[...])[: lse_ref.shape[0], :]


def attend(q, kb, vb, ko, vo, meta):
    rows, width = q.shape
    pairs = width // LANES
    spec = pl.BlockSpec((rows, LANES), lambda j: (0, j))
    return pl.pallas_call(
        functools.partial(attend_kernel, rows),
        grid=(pairs,),
        in_specs=[spec] * 5 + [pl.BlockSpec(meta.shape, lambda j: (0, 0))],
        out_specs=[spec, pl.BlockSpec((16, rows), lambda j: (0, 0))],
        out_shape=[
            jax.ShapeDtypeStruct((rows, width), jnp.bfloat16),
            jax.ShapeDtypeStruct((16, rows), jnp.float32),
        ],
        scratch_shapes=[
            pltpu.VMEM((rows, rows), jnp.float32),
            pltpu.VMEM((rows, SUB), jnp.float32),
            pltpu.VMEM((rows, LANES), jnp.float32),
        ],
        compiler_params=pltpu.CompilerParams(vmem_limit_bytes=48 * MIB),
        cost_estimate=pl.CostEstimate(
            flops=2 * 2 * rows * rows * width, bytes_accessed=12 * rows * width, transcendentals=0
        ),
        name="attend",
    )(q, kb, vb, ko, vo, meta)


def attend_back_kernel(
    rows, score_scale, q_ref, kb_ref, vb_ref, ko_ref, vo_ref, o_ref, do_ref, lse_ref, meta_ref, cos_ref, sin_ref,
    dq_ref, dkb_ref, dvb_ref, dko_ref, dvo_ref, bias, diag, dk_sum, dv_sum,
):
    pair = pl.program_id(0)

    @pl.when(pair == 0)
    def _():
        columns = jnp.transpose(meta_ref[...])
        for i in range(rows // TILE):
            band = slice(i * TILE, (i + 1) * TILE)
            n = (i + 1) * TILE
            start, limit = meta_ref[0:1, band], meta_ref[1:2, band]
            key = lax.broadcasted_iota(jnp.int32, (n, TILE), 0)
            query = lax.broadcasted_iota(jnp.int32, (n, TILE), 1) + i * TILE
            usable = (columns[:n, 2:3] == 1.0) | (key == query)
            place = key.astype(jnp.float32)
            seen = (place >= start) & (place < limit) & usable
            bias[:n, band] = jnp.where(seen, 0.0, masked_score)
            for sub in range(TILE // SUB):
                low = i * TILE + sub * SUB
                part = slice(low, low + SUB)
                key = lax.broadcasted_iota(jnp.int32, (SUB, SUB), 0) + low
                query = lax.broadcasted_iota(jnp.int32, (SUB, SUB), 1) + low
                usable = (columns[part, 2:3] == 1.0) | (key == query)
                same = (key // BLOCK == query // BLOCK) & (
                    key.astype(jnp.float32) >= meta_ref[0:1, part]
                )
                seen = same & usable & (meta_ref[3:4, part] == 1.0)
                diag[:, part] = jnp.where(seen, 0.0, masked_score)

    head_lane = lax.broadcasted_iota(jnp.int32, (8, LANES), 1)
    head_row = lax.broadcasted_iota(jnp.int32, (8, LANES), 0)
    pick = jnp.where(head_lane // 64 == head_row, 1.0, 0.0).astype(jnp.bfloat16)
    for i in reversed(range(rows // TILE)):
        band = slice(i * TILE, (i + 1) * TILE)
        n = (i + 1) * TILE
        q2 = two_heads(q_ref[band, :])
        do = do_ref[band, :]
        do2 = two_heads(do)
        prod = do.astype(jnp.float32) * o_ref[band, :].astype(jnp.float32)
        high = prod.astype(jnp.bfloat16)
        rest = (prod - high.astype(jnp.float32)).astype(jnp.bfloat16)
        inner = nt(pick, high) + nt(pick, rest)
        inner = jnp.concatenate([inner[0:1], inner[1:2]], axis=1)
        level = jnp.concatenate(
            [lse_ref[pl.ds(2 * pair, 1), band], lse_ref[pl.ds(2 * pair + 1, 1), band]], axis=1
        )
        b = bias[:n, band]
        s = nt(kb_ref[:n, :], q2) + jnp.concatenate([b, b], axis=1)
        p = jnp.exp(s - level)
        dp = nt(vb_ref[:n, :], do2)
        ds = (p * (dp - inner)).astype(jnp.bfloat16)
        dv = nn(p.astype(jnp.bfloat16), do2)
        dk = nn(ds, q2)
        if i == rows // TILE - 1:
            dv_sum[...] = dv
            dk_sum[...] = dk
        else:
            dv_sum[:n, :] += dv
            dk_sum[:n, :] += dk
        dq = tn(ds, kb_ref[:n, :])
        extra = []
        for sub in range(TILE // SUB):
            low = i * TILE + sub * SUB
            part = slice(low, low + SUB)
            qs, dos = subs(q2, sub), subs(do2, sub)
            d = diag[:, part]
            at = slice(sub * SUB, (sub + 1) * SUB)
            at2 = slice(TILE + sub * SUB, TILE + (sub + 1) * SUB)
            lev = jnp.concatenate([level[:, at], level[:, at2]], axis=1)
            inn = jnp.concatenate([inner[:, at], inner[:, at2]], axis=1)
            s = nt(ko_ref[part, :], qs) + jnp.concatenate([d, d], axis=1)
            p = jnp.exp(s - lev)
            dp = nt(vo_ref[part, :], dos)
            ds = (p * (dp - inn)).astype(jnp.bfloat16)
            dvo_ref[part, :] = nn(p.astype(jnp.bfloat16), dos).astype(jnp.bfloat16)
            dko = nn(ds, qs)
            dko_ref[part, :] = turn(dko, cos_ref[part, :], -sin_ref[part, :]).astype(jnp.bfloat16)
            extra.append(tn(ds, ko_ref[part, :]))
        dq = dq + jnp.concatenate(
            [extra[0][:SUB], extra[1][:SUB], extra[0][SUB:], extra[1][SUB:]], axis=0
        )
        dq = one_row(dq) * score_scale
        dq_ref[band, :] = turn(dq, cos_ref[band, :], -sin_ref[band, :]).astype(jnp.bfloat16)
    dvb_ref[...] = dv_sum[...].astype(jnp.bfloat16)
    dkb_ref[...] = turn(dk_sum[...], cos_ref[...], -sin_ref[...]).astype(jnp.bfloat16)


def attend_back(q, kb, vb, ko, vo, o, do, lse, meta, cosine, sine, score_scale):
    rows, width = q.shape
    pairs = width // LANES
    spec = pl.BlockSpec((rows, LANES), lambda j: (0, j))
    whole = lambda a: pl.BlockSpec(a.shape, lambda j: (0, 0))
    return pl.pallas_call(
        functools.partial(attend_back_kernel, rows, score_scale),
        grid=(pairs,),
        in_specs=[spec] * 7 + [whole(lse), whole(meta), whole(cosine), whole(sine)],
        out_specs=[spec] * 5,
        out_shape=[jax.ShapeDtypeStruct((rows, width), jnp.bfloat16)] * 5,
        scratch_shapes=[
            pltpu.VMEM((rows, rows), jnp.float32),
            pltpu.VMEM((SUB, rows), jnp.float32),
            pltpu.VMEM((rows, LANES), jnp.float32),
            pltpu.VMEM((rows, LANES), jnp.float32),
        ],
        compiler_params=pltpu.CompilerParams(vmem_limit_bytes=48 * MIB),
        cost_estimate=pl.CostEstimate(
            flops=5 * 2 * rows * rows * width, bytes_accessed=24 * rows * width, transcendentals=0
        ),
        name="attend_back",
    )(q, kb, vb, ko, vo, o, do, lse, meta, cosine, sine)


def shards(
    tokens,
    lengths,
    pad_mask,
    first_gain,
    first_bias,
    query_weight,
    key_weight,
    value_weight,
    out_weight,
    second_gain,
    second_bias,
    up_weight,
    down_weight,
    output_grad,
):
    total_rows = tokens.shape[1]
    model_width = tokens.shape[2]
    head_width = model_width // H
    score_scale = head_width ** (-0.5)
    is_noisy = lax.axis_index("stream") == 1
    own = tokens[0]
    far = lax.ppermute(own, "stream", [(0, 1)])
    base = jnp.where(is_noisy, far, own)
    places, first_place = layout(lengths[0], total_rows, lengths.shape[1])
    limit = (places // BLOCK + jnp.where(is_noisy, 0, 1)) * BLOCK
    noisy_row = jnp.broadcast_to(jnp.where(is_noisy, 1, 0), places.shape)
    blank = jnp.zeros_like(places)
    meta = jnp.stack(
        [first_place, limit, pad_mask, noisy_row, blank, blank, blank, blank]
    ).astype(jnp.float32)
    cosine, sine = angle_tables(places - first_place, head_width)
    gain1, bias1 = first_gain[None], first_bias[None]
    h1, q, ko, vo = project(
        own, gain1, bias1, cosine, sine, (query_weight, key_weight, value_weight), score_scale
    )
    h1b, kb, vb = project(base, gain1, bias1, cosine, sine, (key_weight, value_weight), score_scale)
    mixed_low, lse = attend(q, kb, vb, ko, vo, meta)

    inputs = own.astype(jnp.float32)
    middle = inputs + nn(mixed_low, out_weight)
    normed_second = layer_norm(middle, second_gain, second_bias)
    second_low = normed_second.astype(jnp.bfloat16)
    hidden = nn(second_low, up_weight)
    activated_low = jax.nn.gelu(hidden).astype(jnp.bfloat16)
    result = middle + nn(activated_low, down_weight)
    layer_output = result.astype(jnp.bfloat16)[None]
    cotangent_low = output_grad[0]
    cotangent = cotangent_low.astype(jnp.float32)
    down_part = tn(cotangent_low, activated_low).astype(jnp.bfloat16)
    act_grad = nt(cotangent_low, down_weight)
    gelu_pull = jax.vjp(jax.nn.gelu, hidden)[1]
    hidden_grad = gelu_pull(act_grad)[0].astype(jnp.bfloat16)
    up_part = tn(second_low, hidden_grad).astype(jnp.bfloat16)
    second_norm_grad = nt(hidden_grad, up_weight)
    second_pull = jax.vjp(layer_norm, middle, second_gain, second_bias)[1]
    middle_part, second_gain_part, second_bias_part = second_pull(second_norm_grad)
    middle_grad = cotangent + middle_part
    middle_low = middle_grad.astype(jnp.bfloat16)
    out_part = tn(middle_low, mixed_low).astype(jnp.bfloat16)
    second_part = jnp.stack([second_gain_part, second_bias_part], axis=1).astype(jnp.bfloat16)
    mixed_grad = nt(middle_low, out_weight).astype(jnp.bfloat16)
    early = jnp.concatenate(
        [up_part, down_part, out_part, jnp.pad(second_part, ((0, 0), (0, LANES - 2)))], axis=1
    )
    early = lax.psum_scatter(early, ("stream", "dp"), scatter_dimension=0, tiled=True)

    dq, dkb, dvb, dko, dvo = attend_back(
        q, kb, vb, ko, vo, mixed_low, mixed_grad, lse, meta, cosine, sine, score_scale
    )
    base_grad = nt(dkb, key_weight) + nt(dvb, value_weight)
    back = lax.ppermute(base_grad.astype(jnp.bfloat16), "stream", [(1, 0)])
    query_part = tn(h1, dq)
    key_part = tn(h1, dko) + tn(h1b, dkb)
    value_part = tn(h1, dvo) + tn(h1b, dvb)
    normed_grad = (
        nt(dq, query_weight)
        + nt(dko, key_weight)
        + nt(dvo, value_weight)
        + jnp.where(is_noisy, 0.0, base_grad + back.astype(jnp.float32))
    )
    first_pull = jax.vjp(layer_norm, inputs, first_gain, first_bias)[1]
    input_part, first_gain_part, first_bias_part = first_pull(normed_grad)
    tokens_grad = (middle_grad + input_part)[None]
    first_part = jnp.stack([first_gain_part, first_bias_part], axis=1)
    late = jnp.concatenate(
        [query_part, key_part, value_part, jnp.pad(first_part, ((0, 0), (0, LANES - 2)))], axis=1
    ).astype(jnp.bfloat16)
    late = lax.psum_scatter(late, ("stream", "dp"), scatter_dimension=0, tiled=True)
    early = early.astype(jnp.float32)
    late = late.astype(jnp.float32)
    hidden_width = up_weight.shape[1]
    up_grad = early[:, :hidden_width]
    down_grad = early[:, hidden_width : 2 * hidden_width].T
    out_grad = early[:, 2 * hidden_width : 2 * hidden_width + model_width].T
    second_grads = early[:, 2 * hidden_width + model_width :][:, :2].T
    query_grad = late[:, :model_width]
    key_grad = late[:, model_width : 2 * model_width]
    value_grad = late[:, 2 * model_width : 3 * model_width]
    first_grads = late[:, 3 * model_width :][:, :2].T
    return (
        layer_output,
        tokens_grad,
        first_grads,
        query_grad,
        key_grad,
        value_grad,
        out_grad,
        second_grads,
        up_grad,
        down_grad,
    )


def solution(mesh):
    placed = (
        P("stream", "dp", None),
        P("dp", None),
        P("dp"),
        P(),
        P(),
        P(),
        P(),
        P(),
        P(),
        P(),
        P(),
        P(),
        P(),
        P("stream", "dp", None),
    )
    return jax.shard_map(
        shards,
        mesh=mesh,
        in_specs=placed,
        out_specs=(
            P("stream", "dp", None),
            P("stream", "dp", None),
            P(None, ("stream", "dp")),
            P(("stream", "dp"), None),
            P(("stream", "dp"), None),
            P(("stream", "dp"), None),
            P(None, ("stream", "dp")),
            P(None, ("stream", "dp")),
            P(("stream", "dp"), None),
            P(None, ("stream", "dp")),
        ),
        check_vma=False,
    )
```

```python
import functools
import math

import jax
import jax.numpy as jnp
from jax import lax
from jax.experimental import pallas as pl
from jax.experimental.pallas import tpu as pltpu
from jax.sharding import PartitionSpec as P

H = 12
BLOCK = 16
TILE = 256
SUB = 128
LANES = 128

epsilon = 1e-05
masked_score = -1e30
MIB = 1024 * 1024


def layer_norm(values, gain_row, bias_row):
    centre = values - jnp.mean(values, axis=-1, keepdims=True)
    spread = jnp.mean(centre * centre, axis=-1, keepdims=True)
    return centre * lax.rsqrt(spread + epsilon) * gain_row + bias_row


def layout(lengths_row, total_rows, doc_slots):
    places = jnp.arange(total_rows, dtype=jnp.int32)
    end_places = jnp.cumsum(lengths_row)
    starts = end_places - lengths_row
    document = jnp.sum((places[:, None] >= end_places[None, :]).astype(jnp.int32), axis=1)
    picked = document[:, None] == jnp.arange(doc_slots, dtype=jnp.int32)[None, :]
    first_place = jnp.sum(jnp.where(picked, starts[None, :], 0), axis=1)
    return (places, first_place)


def angle_tables(position, head_width):
    half_width = head_width // 2
    freq_index = (jnp.arange(half_width)).astype(jnp.float32)
    frequency = jnp.exp(freq_index * (-2.0 * math.log(10000.0) / head_width))
    turned = position.astype(jnp.float32)[:, None] * frequency[None, :]
    cosine, sine = jnp.cos(turned), jnp.sin(turned)
    return (
        jnp.concatenate([cosine] * 4, axis=1),
        jnp.concatenate([-sine, sine, -sine, sine], axis=1),
    )


def turn(values, cosine, sine):
    lane = lax.broadcasted_iota(jnp.int32, values.shape, 1)
    low = lax.rem(lane, 64) < 32
    partner = jnp.where(low, pltpu.roll(values, LANES - 32, 1), pltpu.roll(values, 32, 1))
    return values * cosine + partner * sine


def nt(left, right):
    return lax.dot_general(
        left, right, (((1,), (1,)), ((), ())), preferred_element_type=jnp.float32
    )


def tn(left, right):
    return lax.dot_general(
        left, right, (((0,), (0,)), ((), ())), preferred_element_type=jnp.float32
    )


def nn(left, right):
    return jnp.dot(left, right, preferred_element_type=jnp.float32)


MESH = pl.DeviceIdType.MESH
RUN = 48


class Scatter:
    orders = ("yzx", "zyx", "xyz")

    @staticmethod
    def shapes(widths):
        total = sum(widths)
        shapes = [
            pltpu.VMEM((2, 4, 2, RUN, total), jnp.bfloat16),
            pltpu.VMEM((2, 4, 2, RUN, total), jnp.bfloat16),
            pltpu.VMEM((2, 24, total), jnp.float32),
            pltpu.VMEM((24, total), jnp.float32),
        ]
        count = 0
        for order, width in zip(Scatter.orders, widths):
            dims = {"x": 2, "z": 4, "y": 2}
            count += 1
            for axis in order:
                dims.pop(axis)
                rest = tuple(dims.values()) + (RUN, width)
                if axis == "z":
                    shapes += [pltpu.VMEM((4,) + rest, jnp.bfloat16)] * 2
                    shapes += [pltpu.VMEM(rest, jnp.bfloat16)]
                    count += 8
                else:
                    shapes += [pltpu.VMEM(rest, jnp.bfloat16)]
                    count += 1
        return shapes + [
            pltpu.SemaphoreType.DMA((count + 1,)),
            pltpu.SemaphoreType.DMA((count + 1,)),
            pltpu.SemaphoreType.DMA((1,)),
        ]

    def __init__(self, widths, g_ref, out_ref, refs):
        self.widths, self.g, self.out = widths, g_ref, out_ref
        self.half, self.sib, self.fin, self.other = refs[:4]
        self.bufs = list(refs[4:-3])
        self.send, self.recv, self.local = refs[-3:]
        self.s = lax.axis_index("stream")
        d = lax.axis_index("dp")
        self.z, self.y, self.core = d // 4, d // 2 % 2, d % 2
        self.to = {
            "x": {"stream": 1 - self.s},
            "y": {"dp": d + 2 - 4 * self.y},
            "core": {"dp": d + 1 - 2 * self.core},
            "up": {"dp": lax.rem(d + 4, 16)},
            "down": {"dp": lax.rem(d + 12, 16)},
        }
        self.mine = {"x": self.s, "y": self.y, "z": self.z}
        self.used = 0
        self.streams = []
        low = 0
        for order, width in zip(self.orders, widths):
            self.streams.append(self.stream(order, low, width))
            low += width
        self.last = self.take()

    def take(self, count=1):
        self.used += count
        return self.used - count

    def copy(self, src, dst, k, to):
        return pltpu.make_async_remote_copy(
            src_ref=src,
            dst_ref=dst,
            send_sem=self.send.at[k],
            recv_sem=self.recv.at[k],
            device_id=self.to[to],
            device_id_type=MESH,
        )

    def greet(self):
        barrier = pltpu.get_barrier_semaphore()

        def hello(to):
            pl.semaphore_signal(barrier, inc=1, device_id=self.to[to], device_id_type=MESH)

        hello("x")
        hello("y")
        hello("core")
        pl.when(self.z < 3)(lambda: hello("up"))
        pl.when(self.z > 0)(lambda: hello("down"))
        inner = jnp.where((self.z > 0) & (self.z < 3), 1, 0)
        pl.semaphore_wait(barrier, 4 + inner)

    @staticmethod
    def add(dst, left, right):
        lead = dst.shape[:-2]
        count = math.prod(lead)

        def one(index):
            at = []
            for size in reversed(lead):
                at.append(index % size)
                index = index // size
            at = tuple(reversed(at))
            dst[at] = left[at] + right[at]

        if count == 1:
            one(0)
        else:
            pl.loop(0, count)(one)

    def stream(self, order, low, width):
        cols = pl.ds(low, width)
        steps = []
        k0 = self.take()
        whole = (slice(None), slice(None), slice(None), slice(None), cols)
        src = self.half.at[whole]
        swap = lambda: self.copy(
            self.g.at[(1 - self.core,) + whole], self.sib.at[whole], k0, "core"
        )
        got = lambda: pltpu.make_async_copy(
            self.g.at[(self.core,) + whole], self.half.at[whole], self.local.at[0]
        )
        sib = self.sib.at[whole]
        names = ["x", "z", "y"]
        waits = [swap]

        def opening(src=src):
            swap().wait()
            self.add(src, src, sib)

        pending = opening
        for axis in order:
            place = names.index(axis)
            names.pop(place)
            pick = lambda index, src=src, place=place: src.at[(slice(None),) * place + (index,)]
            if axis == "z":
                right, left, total = self.bufs[:3]
                self.bufs = self.bufs[3:]
                k = self.take(8)
                steps += self.chain(pending, pick, right, left, total, k)
                pending = steps.pop()
                src = total
            else:
                buf = self.bufs.pop(0)
                k = self.take()
                mine = self.mine[axis]
                make = lambda pick=pick, mine=mine, buf=buf, k=k, axis=axis: self.copy(
                    pick(1 - mine), buf, k, axis
                )

                def begin(before=pending, make=make):
                    before()
                    make().start()

                steps.append(begin)

                def end(pick=pick, mine=mine, buf=buf, make=make):
                    make().wait()
                    self.add(buf, buf, pick(mine))

                pending = end
                src = buf

        def close(before=pending, src=src):
            before()
            for core in range(2):
                self.fin[core, :, cols] = src[24 * core : 24 * core + 24, :].astype(jnp.float32)

        steps.append(close)
        return (swap, got, steps)

    def chain(self, before, pick, right, left, total, k):
        z = self.z

        def hop(src, side, zt, wait_only=False):
            buf = (right, left)[side]
            return self.copy(src, buf.at[zt], k + 4 * side + zt, ("up", "down")[side])

        def first():
            before()

            @pl.when(z == 0)
            def _():
                for zt in (3, 2, 1):
                    hop(pick(zt), 0, zt).start()

            @pl.when(z == 3)
            def _():
                for zt in (0, 1, 2):
                    hop(pick(zt), 1, zt).start()

        def relay(at, side, zt):
            buf = (right, left)[side].at[zt]

            @pl.when(z == at)
            def _():
                hop(buf, side, zt).wait_recv()
                self.add(buf, buf, pick(zt))
                hop(buf, side, zt).start()

        def second():
            relay(1, 0, 3)
            relay(2, 1, 0)

        def third():
            relay(1, 0, 2)
            relay(2, 1, 1)

        def fourth():
            relay(2, 0, 3)
            relay(1, 1, 0)

        def final():
            @pl.when(z > 0)
            def _():
                hop(right.at[z], 0, z).wait_recv()
                self.add(total, pick(z), right.at[z])

            @pl.when(z == 0)
            def _():
                hop(left.at[z], 1, z).wait_recv()
                self.add(total, pick(z), left.at[z])

            @pl.when((z > 0) & (z < 3))
            def _():
                hop(left.at[z], 1, z).wait_recv()
                self.add(total, total, left.at[z])

            for at in range(4):
                for zt in range(4):
                    if at < zt:
                        pl.when(z == at)(lambda zt=zt: hop(right.at[zt], 0, zt).wait_send())
                    if at > zt:
                        pl.when(z == at)(lambda zt=zt: hop(left.at[zt], 1, zt).wait_send())

        return [first, second, third, fourth, final]

    def open(self, order=(1, 0, 2)):
        self.greet()
        for index in order:
            self.streams[index][0]().start()
        whole = pltpu.make_async_copy(self.g.at[self.core], self.half, self.local.at[0])
        whole.start()
        whole.wait()

    def step(self, stream, index):
        self.streams[stream][2][index]()

    def finish(self):
        last = self.copy(self.fin.at[1 - self.core], self.other, self.last, "core")
        last.start()
        self.out[self.core] = self.fin[self.core]
        last.wait()
        self.out[1 - self.core] = self.other[...]


def project_kernel(score_scale, x_ref, gain_ref, bias_ref, cos_ref, sin_ref, *refs):
    count = (len(refs) - 1) // 2
    weights, outs = refs[:count], refs[count:]
    h1 = layer_norm(x_ref[...].astype(jnp.float32), gain_ref[...], bias_ref[...]).astype(
        jnp.bfloat16
    )
    outs[0][...] = h1
    cosine, sine = cos_ref[...], sin_ref[...]
    for index, (weight, out) in enumerate(zip(weights, outs[1:])):
        product = nn(h1, weight[...])
        is_value = index == count - 1
        is_query = count == 3 and index == 0
        if is_value:
            out[...] = product.astype(jnp.bfloat16)
            continue
        for pair in range(product.shape[1] // LANES):
            columns = slice(pair * LANES, (pair + 1) * LANES)
            turned = turn(product[:, columns], cosine, sine)
            if is_query:
                turned = turned * score_scale
            out[:, columns] = turned.astype(jnp.bfloat16)


def project(x, gain, bias, cosine, sine, weights, score_scale):
    rows, width = x.shape
    count = len(weights)
    row_spec = pl.BlockSpec((TILE, width), lambda i: (i, 0))
    table_spec = pl.BlockSpec((TILE, LANES), lambda i: (i, 0))
    whole = pl.BlockSpec((width, width), lambda i: (0, 0))
    line = pl.BlockSpec((1, width), lambda i: (0, 0))
    return pl.pallas_call(
        functools.partial(project_kernel, score_scale),
        grid=(rows // TILE,),
        in_specs=[row_spec, line, line, table_spec, table_spec] + [whole] * count,
        out_specs=[row_spec] * (count + 1),
        out_shape=[jax.ShapeDtypeStruct((rows, width), jnp.bfloat16)] * (count + 1),
        compiler_params=pltpu.CompilerParams(vmem_limit_bytes=40 * MIB),
        cost_estimate=pl.CostEstimate(
            flops=2 * rows * width * width * count,
            bytes_accessed=2 * (rows + count * (width + rows)) * width,
            transcendentals=0,
        ),
        name="project%d" % count,
    )(x, gain, bias, cosine, sine, *weights)


def two_heads(block):
    lane = lax.broadcasted_iota(jnp.int32, block.shape, 1)
    zero = jnp.zeros_like(block)
    return jnp.concatenate(
        [jnp.where(lane < 64, block, zero), jnp.where(lane < 64, zero, block)], axis=0
    )


def one_row(both):
    rows = both.shape[0] // 2
    lane = lax.broadcasted_iota(jnp.int32, (rows, LANES), 1)
    return jnp.where(lane < 64, both[:rows], both[rows:])


def subs(both, sub):
    low = sub * SUB
    return jnp.concatenate([both[low : low + SUB], both[TILE + low : TILE + low + SUB]], axis=0)


def attend_kernel(rows, q_ref, kb_ref, vb_ref, ko_ref, vo_ref, meta_ref, o_ref, lse_ref, bias, diag, lse):
    pair = pl.program_id(0)

    @pl.when(pair == 0)
    def _():
        columns = jnp.transpose(meta_ref[...])
        noisy = columns[:, 3:4]
        for i in range(rows // TILE):
            band = slice(i * TILE, (i + 1) * TILE)
            n = (i + 1) * TILE
            start, limit = columns[band, 0:1], columns[band, 1:2]
            key = lax.broadcasted_iota(jnp.int32, (TILE, n), 1)
            query = lax.broadcasted_iota(jnp.int32, (TILE, n), 0) + i * TILE
            usable = (meta_ref[2:3, :n] == 1.0) | (key == query)
            place = key.astype(jnp.float32)
            seen = (place >= start) & (place < limit) & usable
            bias[band, :n] = jnp.where(seen, 0.0, masked_score)
            for sub in range(TILE // SUB):
                low = i * TILE + sub * SUB
                key = lax.broadcasted_iota(jnp.int32, (SUB, SUB), 1) + low
                query = lax.broadcasted_iota(jnp.int32, (SUB, SUB), 0) + low
                usable = (meta_ref[2:3, low : low + SUB] == 1.0) | (key == query)
                same = (key // BLOCK == query // BLOCK) & (
                    key.astype(jnp.float32) >= columns[low : low + SUB, 0:1]
                )
                seen = same & usable & (noisy[low : low + SUB] == 1.0)
                diag[low : low + SUB, :] = jnp.where(seen, 0.0, masked_score)

    lane = lax.broadcasted_iota(jnp.int32, (TILE, LANES), 1)
    for i in range(rows // TILE):
        band = slice(i * TILE, (i + 1) * TILE)
        n = (i + 1) * TILE
        q2 = two_heads(q_ref[band, :])
        b = bias[band, :n]
        s = nt(q2, kb_ref[:n, :]) + jnp.concatenate([b, b], axis=0)
        d = diag[band, :]
        parts = [
            nt(subs(q2, sub), ko_ref[i * TILE + sub * SUB : i * TILE + (sub + 1) * SUB, :])
            for sub in range(TILE // SUB)
        ]
        sd = jnp.concatenate(
            [parts[0][:SUB], parts[1][:SUB], parts[0][SUB:], parts[1][SUB:]], axis=0
        ) + jnp.concatenate([d, d], axis=0)
        top = jnp.maximum(
            jnp.max(s, axis=1, keepdims=True), jnp.max(sd, axis=1, keepdims=True)
        )
        p = jnp.exp(s - top)
        pd = jnp.exp(sd - top)
        total = jnp.sum(p, axis=1, keepdims=True) + jnp.sum(pd, axis=1, keepdims=True)
        pd_low = pd.astype(jnp.bfloat16)
        o = nn(p.astype(jnp.bfloat16), vb_ref[:n, :])
        parts = [
            nn(subs(pd_low, sub), vo_ref[i * TILE + sub * SUB : i * TILE + (sub + 1) * SUB, :])
            for sub in range(TILE // SUB)
        ]
        o = o + jnp.concatenate(
            [parts[0][:SUB], parts[1][:SUB], parts[0][SUB:], parts[1][SUB:]], axis=0
        )
        o = o * (1.0 / total)
        o_ref[band, :] = one_row(o).astype(o_ref.dtype)
        level = top + jnp.log(total)
        old = lse[band, :]
        lse[band, :] = jnp.where(
            lane == 2 * pair, level[:TILE], jnp.where(lane == 2 * pair + 1, level[TILE:], old)
        )

    @pl.when(pair == pl.num_programs(0) - 1)
    def _():
        lse_ref[...] = jnp.transpose(lse[...])[: lse_ref.shape[0], :]


def attend(q, kb, vb, ko, vo, meta):
    rows, width = q.shape
    pairs = width // LANES
    spec = pl.BlockSpec((rows, LANES), lambda j: (0, j))
    return pl.pallas_call(
        functools.partial(attend_kernel, rows),
        grid=(pairs,),
        in_specs=[spec] * 5 + [pl.BlockSpec(meta.shape, lambda j: (0, 0))],
        out_specs=[spec, pl.BlockSpec((16, rows), lambda j: (0, 0))],
        out_shape=[
            jax.ShapeDtypeStruct((rows, width), jnp.bfloat16),
            jax.ShapeDtypeStruct((16, rows), jnp.float32),
        ],
        scratch_shapes=[
            pltpu.VMEM((rows, rows), jnp.float32),
            pltpu.VMEM((rows, SUB), jnp.float32),
            pltpu.VMEM((rows, LANES), jnp.float32),
        ],
        compiler_params=pltpu.CompilerParams(vmem_limit_bytes=48 * MIB),
        cost_estimate=pl.CostEstimate(
            flops=2 * 2 * rows * rows * width, bytes_accessed=12 * rows * width, transcendentals=0
        ),
        name="attend",
    )(q, kb, vb, ko, vo, meta)


def attend_back_kernel(
    rows, score_scale, widths, q_ref, kb_ref, vb_ref, ko_ref, vo_ref, o_ref, do_ref, lse_ref, meta_ref, cos_ref, sin_ref,
    *refs,
):
    pair = pl.program_id(0)
    scatter = None
    if widths:
        g_ref, dq_ref, dkb_ref, dvb_ref, dko_ref, dvo_ref, g_out = refs[:7]
        bias, diag, dk_sum, dv_sum = refs[7:11]
        scatter = Scatter(widths, g_ref, g_out, refs[11:])
    else:
        dq_ref, dkb_ref, dvb_ref, dko_ref, dvo_ref, bias, diag, dk_sum, dv_sum = refs

    def tick(slot):
        if scatter is None:
            return
        for at, moves in TICKS.items():
            if at[1] == slot:
                @pl.when(pair == at[0])
                def _(moves=moves):
                    for stream, index in moves:
                        scatter.step(stream, index)

    if scatter is not None:
        pl.when(pair == 0)(scatter.open)
    tick(0)

    @pl.when(pair == 0)
    def _():
        columns = jnp.transpose(meta_ref[...])
        for i in range(rows // TILE):
            band = slice(i * TILE, (i + 1) * TILE)
            n = (i + 1) * TILE
            start, limit = meta_ref[0:1, band], meta_ref[1:2, band]
            key = lax.broadcasted_iota(jnp.int32, (n, TILE), 0)
            query = lax.broadcasted_iota(jnp.int32, (n, TILE), 1) + i * TILE
            usable = (columns[:n, 2:3] == 1.0) | (key == query)
            place = key.astype(jnp.float32)
            seen = (place >= start) & (place < limit) & usable
            bias[:n, band] = jnp.where(seen, 0.0, masked_score)
            for sub in range(TILE // SUB):
                low = i * TILE + sub * SUB
                part = slice(low, low + SUB)
                key = lax.broadcasted_iota(jnp.int32, (SUB, SUB), 0) + low
                query = lax.broadcasted_iota(jnp.int32, (SUB, SUB), 1) + low
                usable = (columns[part, 2:3] == 1.0) | (key == query)
                same = (key // BLOCK == query // BLOCK) & (
                    key.astype(jnp.float32) >= meta_ref[0:1, part]
                )
                seen = same & usable & (meta_ref[3:4, part] == 1.0)
                diag[:, part] = jnp.where(seen, 0.0, masked_score)

    head_lane = lax.broadcasted_iota(jnp.int32, (8, LANES), 1)
    head_row = lax.broadcasted_iota(jnp.int32, (8, LANES), 0)
    pick = jnp.where(head_lane // 64 == head_row, 1.0, 0.0).astype(jnp.bfloat16)
    for i in reversed(range(rows // TILE)):
        band = slice(i * TILE, (i + 1) * TILE)
        n = (i + 1) * TILE
        q2 = two_heads(q_ref[band, :])
        do = do_ref[band, :]
        do2 = two_heads(do)
        prod = do.astype(jnp.float32) * o_ref[band, :].astype(jnp.float32)
        high = prod.astype(jnp.bfloat16)
        rest = (prod - high.astype(jnp.float32)).astype(jnp.bfloat16)
        inner = nt(pick, high) + nt(pick, rest)
        inner = jnp.concatenate([inner[0:1], inner[1:2]], axis=1)
        level = jnp.concatenate(
            [lse_ref[pl.ds(2 * pair, 1), band], lse_ref[pl.ds(2 * pair + 1, 1), band]], axis=1
        )
        b = bias[:n, band]
        s = nt(kb_ref[:n, :], q2) + jnp.concatenate([b, b], axis=1)
        p = jnp.exp(s - level)
        dp = nt(vb_ref[:n, :], do2)
        ds = (p * (dp - inner)).astype(jnp.bfloat16)
        dv = nn(p.astype(jnp.bfloat16), do2)
        dk = nn(ds, q2)
        if i == rows // TILE - 1:
            dv_sum[...] = dv
            dk_sum[...] = dk
        else:
            dv_sum[:n, :] += dv
            dk_sum[:n, :] += dk
        dq = tn(ds, kb_ref[:n, :])
        extra = []
        for sub in range(TILE // SUB):
            low = i * TILE + sub * SUB
            part = slice(low, low + SUB)
            qs, dos = subs(q2, sub), subs(do2, sub)
            d = diag[:, part]
            at = slice(sub * SUB, (sub + 1) * SUB)
            at2 = slice(TILE + sub * SUB, TILE + (sub + 1) * SUB)
            lev = jnp.concatenate([level[:, at], level[:, at2]], axis=1)
            inn = jnp.concatenate([inner[:, at], inner[:, at2]], axis=1)
            s = nt(ko_ref[part, :], qs) + jnp.concatenate([d, d], axis=1)
            p = jnp.exp(s - lev)
            dp = nt(vo_ref[part, :], dos)
            ds = (p * (dp - inn)).astype(jnp.bfloat16)
            dvo_ref[part, :] = nn(p.astype(jnp.bfloat16), dos).astype(jnp.bfloat16)
            dko = nn(ds, qs)
            dko_ref[part, :] = turn(dko, cos_ref[part, :], -sin_ref[part, :]).astype(jnp.bfloat16)
            extra.append(tn(ds, ko_ref[part, :]))
        dq = dq + jnp.concatenate(
            [extra[0][:SUB], extra[1][:SUB], extra[0][SUB:], extra[1][SUB:]], axis=0
        )
        dq = one_row(dq) * score_scale
        dq_ref[band, :] = turn(dq, cos_ref[band, :], -sin_ref[band, :]).astype(jnp.bfloat16)
        if i > 0:
            tick(rows // TILE - i)
    dvb_ref[...] = dv_sum[...].astype(jnp.bfloat16)
    dkb_ref[...] = turn(dk_sum[...], cos_ref[...], -sin_ref[...]).astype(jnp.bfloat16)
    tick(rows // TILE)
    if scatter is not None:
        pl.when(pair == pl.num_programs(0) - 1)(scatter.finish)


A, B, C = range(3)
TICKS = {
    (0, 2): [(B, 0)],
    (1, 1): [(A, 0)],
    (2, 0): [(C, 0), (B, 1)],
    (3, 1): [(B, 2)],
    (3, 2): [(B, 3)],
    (4, 2): [(B, 4)],
    (4, 3): [(A, 1)],
    (5, 1): [(B, 5)],
    (5, 3): [(C, 1), (A, 2)],
    (5, 4): [
        (B, 6), (A, 3), (A, 4), (C, 2), (A, 5), (C, 3), (C, 4), (C, 5), (A, 6), (C, 6),
    ],
}


def scatter_call(widths, g):
    def kernel(g_ref, out_ref, *refs):
        scatter = Scatter(widths, g_ref, out_ref, refs)
        scatter.open()
        for index in range(7):
            for stream in (B, A, C):
                scatter.step(stream, index)
        scatter.finish()

    total = sum(widths)
    return pl.pallas_call(
        kernel,
        in_specs=[pl.BlockSpec(memory_space=pl.ANY)],
        out_specs=pl.BlockSpec(memory_space=pltpu.VMEM),
        out_shape=jax.ShapeDtypeStruct((2, 24, total), jnp.float32),
        scratch_shapes=Scatter.shapes(widths),
        compiler_params=pltpu.CompilerParams(
            collective_id=1, has_side_effects=True, vmem_limit_bytes=48 * MIB
        ),
        name="scatter",
    )(halves(g, total))


def halves(g, total):
    return jnp.stack([g[:, :total], g[:, total:]]).reshape(2, 2, 4, 2, RUN, total)


def whole_rows(parts):
    return jnp.concatenate([parts[0], parts[1]], axis=1)


def attend_back(q, kb, vb, ko, vo, o, do, lse, meta, cosine, sine, score_scale, g=None, widths=()):
    rows, width = q.shape
    pairs = width // LANES
    total = sum(widths)
    spec = pl.BlockSpec((rows, LANES), lambda j: (0, j))
    whole = lambda a: pl.BlockSpec(a.shape, lambda j: (0, 0))
    in_specs = [spec] * 7 + [whole(lse), whole(meta), whole(cosine), whole(sine)]
    out_specs = [spec] * 5
    out_shape = [jax.ShapeDtypeStruct((rows, width), jnp.bfloat16)] * 5
    scratch = [
        pltpu.VMEM((rows, rows), jnp.float32),
        pltpu.VMEM((SUB, rows), jnp.float32),
        pltpu.VMEM((rows, LANES), jnp.float32),
        pltpu.VMEM((rows, LANES), jnp.float32),
    ]
    operands = [q, kb, vb, ko, vo, o, do, lse, meta, cosine, sine]
    options = {}
    if widths:
        in_specs += [pl.BlockSpec(memory_space=pl.ANY)]
        out_specs += [pl.BlockSpec((2, 24, total), lambda j: (0, 0, 0))]
        out_shape += [jax.ShapeDtypeStruct((2, 24, total), jnp.float32)]
        scratch += Scatter.shapes(widths)
        operands += [halves(g, total)]
        options = {"collective_id": 0, "has_side_effects": True}
    return pl.pallas_call(
        functools.partial(attend_back_kernel, rows, score_scale, widths),
        grid=(pairs,),
        in_specs=in_specs,
        out_specs=out_specs,
        out_shape=out_shape,
        scratch_shapes=scratch,
        compiler_params=pltpu.CompilerParams(vmem_limit_bytes=58 * MIB, **options),
        cost_estimate=pl.CostEstimate(
            flops=5 * 2 * rows * rows * width, bytes_accessed=24 * rows * width, transcendentals=0
        ),
        name="attend_back",
    )(*operands)


def shards(
    tokens,
    lengths,
    pad_mask,
    first_gain,
    first_bias,
    query_weight,
    key_weight,
    value_weight,
    out_weight,
    second_gain,
    second_bias,
    up_weight,
    down_weight,
    output_grad,
):
    total_rows = tokens.shape[1]
    model_width = tokens.shape[2]
    head_width = model_width // H
    score_scale = head_width ** (-0.5)
    is_noisy = lax.axis_index("stream") == 1
    own = tokens[0]
    far = lax.ppermute(own, "stream", [(0, 1)])
    base = jnp.where(is_noisy, far, own)
    places, first_place = layout(lengths[0], total_rows, lengths.shape[1])
    limit = (places // BLOCK + jnp.where(is_noisy, 0, 1)) * BLOCK
    noisy_row = jnp.broadcast_to(jnp.where(is_noisy, 1, 0), places.shape)
    blank = jnp.zeros_like(places)
    meta = jnp.stack(
        [first_place, limit, pad_mask, noisy_row, blank, blank, blank, blank]
    ).astype(jnp.float32)
    cosine, sine = angle_tables(places - first_place, head_width)
    gain1, bias1 = first_gain[None], first_bias[None]
    h1, q, ko, vo = project(
        own, gain1, bias1, cosine, sine, (query_weight, key_weight, value_weight), score_scale
    )
    h1b, kb, vb = project(base, gain1, bias1, cosine, sine, (key_weight, value_weight), score_scale)
    mixed_low, lse = attend(q, kb, vb, ko, vo, meta)

    inputs = own.astype(jnp.float32)
    middle = inputs + nn(mixed_low, out_weight)
    normed_second = layer_norm(middle, second_gain, second_bias)
    second_low = normed_second.astype(jnp.bfloat16)
    hidden = nn(second_low, up_weight)
    activated_low = jax.nn.gelu(hidden).astype(jnp.bfloat16)
    result = middle + nn(activated_low, down_weight)
    layer_output = result.astype(jnp.bfloat16)[None]
    cotangent_low = output_grad[0]
    cotangent = cotangent_low.astype(jnp.float32)
    down_part = tn(cotangent_low, activated_low).astype(jnp.bfloat16)
    act_grad = nt(cotangent_low, down_weight)
    gelu_pull = jax.vjp(jax.nn.gelu, hidden)[1]
    hidden_grad = gelu_pull(act_grad)[0].astype(jnp.bfloat16)
    up_part = tn(second_low, hidden_grad).astype(jnp.bfloat16)
    second_norm_grad = nt(hidden_grad, up_weight)
    second_pull = jax.vjp(layer_norm, middle, second_gain, second_bias)[1]
    middle_part, second_gain_part, second_bias_part = second_pull(second_norm_grad)
    middle_grad = cotangent + middle_part
    middle_low = middle_grad.astype(jnp.bfloat16)
    out_part = tn(middle_low, mixed_low).astype(jnp.bfloat16)
    mixed_grad = nt(middle_low, out_weight).astype(jnp.bfloat16)
    early = jnp.concatenate([up_part, down_part, out_part], axis=1)
    ring = lax.axis_size("dp") == 16 and lax.axis_size("stream") == 2
    back = functools.partial(
        attend_back, q, kb, vb, ko, vo, mixed_low, mixed_grad, lse, meta, cosine, sine, score_scale
    )
    if ring:
        dq, dkb, dvb, dko, dvo, early = back(early, tuple(LANES * t for t in (10, 7, 10)))
        early = whole_rows(early)
    else:
        early = lax.psum_scatter(early, ("stream", "dp"), scatter_dimension=0, tiled=True)
        dq, dkb, dvb, dko, dvo = back()
    base_grad = nt(dkb, key_weight) + nt(dvb, value_weight)
    back = lax.ppermute(base_grad.astype(jnp.bfloat16), "stream", [(1, 0)])
    query_part = tn(h1, dq)
    key_part = tn(h1, dko) + tn(h1b, dkb)
    value_part = tn(h1, dvo) + tn(h1b, dvb)
    normed_grad = (
        nt(dq, query_weight)
        + nt(dko, key_weight)
        + nt(dvo, value_weight)
        + jnp.where(is_noisy, 0.0, base_grad + back.astype(jnp.float32))
    )
    first_pull = jax.vjp(layer_norm, inputs, first_gain, first_bias)[1]
    input_part, first_gain_part, first_bias_part = first_pull(normed_grad)
    tokens_grad = (middle_grad + input_part)[None]
    norm_part = jnp.stack(
        [first_gain_part, first_bias_part, second_gain_part, second_bias_part], axis=1
    )
    late = jnp.concatenate(
        [query_part, key_part, value_part, jnp.pad(norm_part, ((0, 0), (0, 2 * LANES - 4)))], axis=1
    ).astype(jnp.bfloat16)
    if ring:
        late = whole_rows(scatter_call(tuple(LANES * t for t in (4, 2, 4)), late))
    else:
        late = lax.psum_scatter(late, ("stream", "dp"), scatter_dimension=0, tiled=True)
    early = early.astype(jnp.float32)
    late = late.astype(jnp.float32)
    hidden_width = up_weight.shape[1]
    up_grad = early[:, :hidden_width]
    down_grad = early[:, hidden_width : 2 * hidden_width].T
    out_grad = early[:, 2 * hidden_width : 2 * hidden_width + model_width].T
    second_grads = late[:, 3 * model_width + 2 : 3 * model_width + 4].T
    query_grad = late[:, :model_width]
    key_grad = late[:, model_width : 2 * model_width]
    value_grad = late[:, 2 * model_width : 3 * model_width]
    first_grads = late[:, 3 * model_width : 3 * model_width + 2].T
    return (
        layer_output,
        tokens_grad,
        first_grads,
        query_grad,
        key_grad,
        value_grad,
        out_grad,
        second_grads,
        up_grad,
        down_grad,
    )


def solution(mesh):
    placed = (
        P("stream", "dp", None),
        P("dp", None),
        P("dp"),
        P(),
        P(),
        P(),
        P(),
        P(),
        P(),
        P(),
        P(),
        P(),
        P(),
        P("stream", "dp", None),
    )
    return jax.shard_map(
        shards,
        mesh=mesh,
        in_specs=placed,
        out_specs=(
            P("stream", "dp", None),
            P("stream", "dp", None),
            P(None, ("stream", "dp")),
            P(("stream", "dp"), None),
            P(("stream", "dp"), None),
            P(("stream", "dp"), None),
            P(None, ("stream", "dp")),
            P(None, ("stream", "dp")),
            P(("stream", "dp"), None),
            P(None, ("stream", "dp")),
        ),
        check_vma=False,
    )
```

```python
import functools
import math

import jax
import jax.numpy as jnp
from jax import lax
from jax.experimental import pallas as pl
from jax.experimental.pallas import tpu as pltpu
from jax.sharding import PartitionSpec as P

H = 12
BLOCK = 16
TILE = 256
SUB = 128
LANES = 128

epsilon = 1e-05
masked_score = -1e30
MIB = 1024 * 1024


def layer_norm(values, gain_row, bias_row):
    centre = values - jnp.mean(values, axis=-1, keepdims=True)
    spread = jnp.mean(centre * centre, axis=-1, keepdims=True)
    return centre * lax.rsqrt(spread + epsilon) * gain_row + bias_row


def layout(lengths_row, total_rows, doc_slots):
    places = jnp.arange(total_rows, dtype=jnp.int32)
    end_places = jnp.cumsum(lengths_row)
    starts = end_places - lengths_row
    document = jnp.sum((places[:, None] >= end_places[None, :]).astype(jnp.int32), axis=1)
    picked = document[:, None] == jnp.arange(doc_slots, dtype=jnp.int32)[None, :]
    first_place = jnp.sum(jnp.where(picked, starts[None, :], 0), axis=1)
    return (places, first_place)


def angle_tables(position, head_width):
    half_width = head_width // 2
    freq_index = (jnp.arange(half_width)).astype(jnp.float32)
    frequency = jnp.exp(freq_index * (-2.0 * math.log(10000.0) / head_width))
    turned = position.astype(jnp.float32)[:, None] * frequency[None, :]
    cosine, sine = jnp.cos(turned), jnp.sin(turned)
    return (
        jnp.concatenate([cosine] * 4, axis=1),
        jnp.concatenate([-sine, sine, -sine, sine], axis=1),
    )


def turn(values, cosine, sine):
    lane = lax.broadcasted_iota(jnp.int32, values.shape, 1)
    low = lax.rem(lane, 64) < 32
    partner = jnp.where(low, pltpu.roll(values, LANES - 32, 1), pltpu.roll(values, 32, 1))
    return values * cosine + partner * sine


def nt(left, right):
    return lax.dot_general(
        left, right, (((1,), (1,)), ((), ())), preferred_element_type=jnp.float32
    )


def tn(left, right):
    return lax.dot_general(
        left, right, (((0,), (0,)), ((), ())), preferred_element_type=jnp.float32
    )


def nn(left, right):
    return jnp.dot(left, right, preferred_element_type=jnp.float32)


MESH = pl.DeviceIdType.MESH
RUN = 48


class Scatter:
    @staticmethod
    def shapes(streams, far):
        total = sum(width for _, width in streams)
        shapes = [
            pltpu.VMEM((2, 2, 2, 2, RUN, total), jnp.bfloat16),
            pltpu.VMEM((2, 24, total), jnp.float32),
            pltpu.VMEM((24, total), jnp.float32),
        ]
        for number, (order, width) in enumerate(streams):
            if number < far:
                shapes += [pltpu.VMEM((2, 2, 2, 2, RUN, width), jnp.bfloat16)]
            for left in range(len(order) - 1, -1, -1):
                shapes += [pltpu.VMEM((2,) * left + (RUN, width), jnp.bfloat16)]
        count = sum(1 + len(order) for order, _ in streams) + 1
        return shapes + [
            pltpu.SemaphoreType.DMA((count,)),
            pltpu.SemaphoreType.DMA((count,)),
            pltpu.SemaphoreType.DMA((len(streams),)),
        ]

    def __init__(self, streams, sources, out_ref, refs, far):
        self.out, self.far = out_ref, far
        self.sib, self.fin, self.other = refs[:3]
        self.bufs = list(refs[3:-3])
        self.send, self.recv, self.local = refs[-3:]
        s, d = lax.axis_index("stream"), lax.axis_index("dp")
        self.core = d % 2
        self.mine = {"x": s, "y": d // 2 % 2, "l": d // 4 % 2, "h": d // 8}
        self.to = {
            "x": {"stream": 1 - s},
            "y": {"dp": d + 2 - 4 * self.mine["y"]},
            "l": {"dp": d + 4 - 8 * self.mine["l"]},
            "h": {"dp": d + 8 - 16 * self.mine["h"]},
            "core": {"dp": d + 1 - 2 * self.core},
        }
        self.used = 0
        self.streams = []
        place = 0
        for (order, width), (source, low) in zip(streams, sources):
            self.streams.append(self.stream(order, place, width, source, low))
            place += width
        self.last = self.take()

    def take(self):
        self.used += 1
        return self.used - 1

    def copy(self, src, dst, k, to):
        return pltpu.make_async_remote_copy(
            src_ref=src,
            dst_ref=dst,
            send_sem=self.send.at[k],
            recv_sem=self.recv.at[k],
            device_id=self.to[to],
            device_id_type=MESH,
        )

    def greet(self):
        barrier = pltpu.get_barrier_semaphore()
        for to in self.to.values():
            pl.semaphore_signal(barrier, inc=1, device_id=to, device_id_type=MESH)
        pl.semaphore_wait(barrier, len(self.to))

    @staticmethod
    def add(dst, left, right):
        lead = dst.shape[:-2]
        count = math.prod(lead)

        def one(index):
            at = []
            for size in reversed(lead):
                at.append(index % size)
                index = index // size
            at = tuple(reversed(at))
            dst[at] = left[at] + right[at]

        if count == 1:
            one(0)
        else:
            pl.loop(0, count)(one)

    def stream(self, order, place, width, source, low):
        number = len(self.streams)
        cols = pl.ds(place, width)
        every = (slice(None),) * 5
        src = self.sib.at[every + (cols,)]
        k = self.take()
        part = lambda core: source.at[(core,) + every + (pl.ds(low, width),)]
        swap = lambda src=src, k=k: self.copy(part(1 - self.core), src, k, "core")
        near = None
        if number < self.far:
            held = self.bufs.pop(0)
            near = lambda: pltpu.make_async_copy(part(self.core), held, self.local.at[number])

        def opening(src=src):
            swap().wait()
            if near is None:
                self.add(src, src, part(self.core))
            else:
                near().wait()
                self.add(src, src, held)

        steps = []
        pending = opening
        names = ["x", "h", "l", "y"]
        for axis in order:
            at = names.index(axis)
            names.pop(at)
            buf = self.bufs.pop(0)
            k = self.take()
            pick = lambda index, src=src, at=at: src.at[(slice(None),) * at + (index,)]
            make = lambda pick=pick, buf=buf, k=k, axis=axis: self.copy(
                pick(1 - self.mine[axis]), buf, k, axis
            )

            def begin(before=pending, make=make):
                before()
                make().start()

            def end(pick=pick, buf=buf, make=make, axis=axis):
                make().wait()
                self.add(buf, buf, pick(self.mine[axis]))

            steps.append(begin)
            pending = end
            src = buf

        def close(before=pending, src=src):
            before()
            for core in range(2):
                self.fin[core, :, cols] = src[24 * core : 24 * core + 24, :].astype(jnp.float32)

        steps.append(close)
        return (swap, near, steps)

    def open(self, order):
        for index in order:
            swap, near, _ = self.streams[index]
            swap().start()
            if near is not None:
                near().start()

    def step(self, stream, index):
        self.streams[stream][2][index]()

    def finish(self):
        last = self.copy(self.fin.at[1 - self.core], self.other, self.last, "core")
        last.start()
        self.out[self.core] = self.fin[self.core]
        last.wait()
        self.out[1 - self.core] = self.other[...]


def project_kernel(score_scale, x_ref, gain_ref, bias_ref, cos_ref, sin_ref, *refs):
    count = (len(refs) - 1) // 2
    weights, outs = refs[:count], refs[count:]
    h1 = layer_norm(x_ref[...].astype(jnp.float32), gain_ref[...], bias_ref[...]).astype(
        jnp.bfloat16
    )
    outs[0][...] = jnp.transpose(h1)
    cosine, sine = cos_ref[...], sin_ref[...]
    for index, (weight, out) in enumerate(zip(weights, outs[1:])):
        product = nn(h1, weight[...])
        is_value = index == count - 1
        is_query = count == 3 and index == 0
        if is_value:
            out[...] = product.astype(jnp.bfloat16)
            continue
        for pair in range(product.shape[1] // LANES):
            columns = slice(pair * LANES, (pair + 1) * LANES)
            turned = turn(product[:, columns], cosine, sine)
            if is_query:
                turned = turned * score_scale
            out[:, columns] = turned.astype(jnp.bfloat16)


def project(x, gain, bias, cosine, sine, weights, score_scale):
    rows, width = x.shape
    count = len(weights)
    row_spec = pl.BlockSpec((TILE, width), lambda i: (i, 0))
    table_spec = pl.BlockSpec((TILE, LANES), lambda i: (i, 0))
    whole = pl.BlockSpec((width, width), lambda i: (0, 0))
    line = pl.BlockSpec((1, width), lambda i: (0, 0))
    return pl.pallas_call(
        functools.partial(project_kernel, score_scale),
        grid=(rows // TILE,),
        in_specs=[row_spec, line, line, table_spec, table_spec] + [whole] * count,
        out_specs=[pl.BlockSpec((width, TILE), lambda i: (0, i))] + [row_spec] * count,
        out_shape=[jax.ShapeDtypeStruct((width, rows), jnp.bfloat16)]
        + [jax.ShapeDtypeStruct((rows, width), jnp.bfloat16)] * count,
        compiler_params=pltpu.CompilerParams(vmem_limit_bytes=40 * MIB),
        cost_estimate=pl.CostEstimate(
            flops=2 * rows * width * width * count,
            bytes_accessed=2 * (rows + count * (width + rows)) * width,
            transcendentals=0,
        ),
        name="project%d" % count,
    )(x, gain, bias, cosine, sine, *weights)


def two_heads(block):
    lane = lax.broadcasted_iota(jnp.int32, block.shape, 1)
    zero = jnp.zeros_like(block)
    return jnp.concatenate(
        [jnp.where(lane < 64, block, zero), jnp.where(lane < 64, zero, block)], axis=0
    )


def one_row(both):
    rows = both.shape[0] // 2
    lane = lax.broadcasted_iota(jnp.int32, (rows, LANES), 1)
    return jnp.where(lane < 64, both[:rows], both[rows:])


def subs(both, sub):
    low = sub * SUB
    return jnp.concatenate([both[low : low + SUB], both[TILE + low : TILE + low + SUB]], axis=0)


def attend_kernel(rows, q_ref, kb_ref, vb_ref, ko_ref, vo_ref, meta_ref, o_ref, lse_ref, bias, diag, lse):
    pair = pl.program_id(0)

    @pl.when(pair == 0)
    def _():
        columns = jnp.transpose(meta_ref[...])
        noisy = columns[:, 3:4]
        for i in range(rows // TILE):
            band = slice(i * TILE, (i + 1) * TILE)
            n = (i + 1) * TILE
            start, limit = columns[band, 0:1], columns[band, 1:2]
            key = lax.broadcasted_iota(jnp.int32, (TILE, n), 1)
            query = lax.broadcasted_iota(jnp.int32, (TILE, n), 0) + i * TILE
            usable = (meta_ref[2:3, :n] == 1.0) | (key == query)
            place = key.astype(jnp.float32)
            seen = (place >= start) & (place < limit) & usable
            bias[band, :n] = jnp.where(seen, 0.0, masked_score)
            for sub in range(TILE // SUB):
                low = i * TILE + sub * SUB
                key = lax.broadcasted_iota(jnp.int32, (SUB, SUB), 1) + low
                query = lax.broadcasted_iota(jnp.int32, (SUB, SUB), 0) + low
                usable = (meta_ref[2:3, low : low + SUB] == 1.0) | (key == query)
                same = (key // BLOCK == query // BLOCK) & (
                    key.astype(jnp.float32) >= columns[low : low + SUB, 0:1]
                )
                seen = same & usable & (noisy[low : low + SUB] == 1.0)
                diag[low : low + SUB, :] = jnp.where(seen, 0.0, masked_score)

    lane = lax.broadcasted_iota(jnp.int32, (TILE, LANES), 1)
    for i in range(rows // TILE):
        band = slice(i * TILE, (i + 1) * TILE)
        n = (i + 1) * TILE
        q2 = two_heads(q_ref[band, :])
        b = bias[band, :n]
        s = nt(q2, kb_ref[:n, :]) + jnp.concatenate([b, b], axis=0)
        d = diag[band, :]
        parts = [
            nt(subs(q2, sub), ko_ref[i * TILE + sub * SUB : i * TILE + (sub + 1) * SUB, :])
            for sub in range(TILE // SUB)
        ]
        sd = jnp.concatenate(
            [parts[0][:SUB], parts[1][:SUB], parts[0][SUB:], parts[1][SUB:]], axis=0
        ) + jnp.concatenate([d, d], axis=0)
        top = jnp.maximum(
            jnp.max(s, axis=1, keepdims=True), jnp.max(sd, axis=1, keepdims=True)
        )
        p = jnp.exp(s - top)
        pd = jnp.exp(sd - top)
        total = jnp.sum(p, axis=1, keepdims=True) + jnp.sum(pd, axis=1, keepdims=True)
        pd_low = pd.astype(jnp.bfloat16)
        o = nn(p.astype(jnp.bfloat16), vb_ref[:n, :])
        parts = [
            nn(subs(pd_low, sub), vo_ref[i * TILE + sub * SUB : i * TILE + (sub + 1) * SUB, :])
            for sub in range(TILE // SUB)
        ]
        o = o + jnp.concatenate(
            [parts[0][:SUB], parts[1][:SUB], parts[0][SUB:], parts[1][SUB:]], axis=0
        )
        o = o * (1.0 / total)
        o_ref[band, :] = one_row(o).astype(o_ref.dtype)
        level = top + jnp.log(total)
        old = lse[band, :]
        lse[band, :] = jnp.where(
            lane == 2 * pair, level[:TILE], jnp.where(lane == 2 * pair + 1, level[TILE:], old)
        )

    @pl.when(pair == pl.num_programs(0) - 1)
    def _():
        lse_ref[...] = jnp.transpose(lse[...])[: lse_ref.shape[0], :]


def attend(q, kb, vb, ko, vo, meta):
    rows, width = q.shape
    pairs = width // LANES
    spec = pl.BlockSpec((rows, LANES), lambda j: (0, j))
    return pl.pallas_call(
        functools.partial(attend_kernel, rows),
        grid=(pairs,),
        in_specs=[spec] * 5 + [pl.BlockSpec(meta.shape, lambda j: (0, 0))],
        out_specs=[spec, pl.BlockSpec((16, rows), lambda j: (0, 0))],
        out_shape=[
            jax.ShapeDtypeStruct((rows, width), jnp.bfloat16),
            jax.ShapeDtypeStruct((16, rows), jnp.float32),
        ],
        scratch_shapes=[
            pltpu.VMEM((rows, rows), jnp.float32),
            pltpu.VMEM((rows, SUB), jnp.float32),
            pltpu.VMEM((rows, LANES), jnp.float32),
        ],
        compiler_params=pltpu.CompilerParams(vmem_limit_bytes=48 * MIB),
        cost_estimate=pl.CostEstimate(
            flops=2 * 2 * rows * rows * width, bytes_accessed=12 * rows * width, transcendentals=0
        ),
        name="attend",
    )(q, kb, vb, ko, vo, meta)


def mask_back(rows, meta_ref, bias, diag):
    columns = jnp.transpose(meta_ref[...])
    for i in range(rows // TILE):
        band = slice(i * TILE, (i + 1) * TILE)
        n = (i + 1) * TILE
        start, limit = meta_ref[0:1, band], meta_ref[1:2, band]
        key = lax.broadcasted_iota(jnp.int32, (n, TILE), 0)
        query = lax.broadcasted_iota(jnp.int32, (n, TILE), 1) + i * TILE
        usable = (columns[:n, 2:3] == 1.0) | (key == query)
        place = key.astype(jnp.float32)
        seen = (place >= start) & (place < limit) & usable
        bias[i][...] = jnp.where(seen, 0.0, masked_score)
        for sub in range(TILE // SUB):
            low = i * TILE + sub * SUB
            part = slice(low, low + SUB)
            key = lax.broadcasted_iota(jnp.int32, (SUB, SUB), 0) + low
            query = lax.broadcasted_iota(jnp.int32, (SUB, SUB), 1) + low
            usable = (columns[part, 2:3] == 1.0) | (key == query)
            same = (key // BLOCK == query // BLOCK) & (
                key.astype(jnp.float32) >= meta_ref[0:1, part]
            )
            seen = same & usable & (meta_ref[3:4, part] == 1.0)
            diag[:, part] = jnp.where(seen, 0.0, masked_score)


def pair_back(
    rows, score_scale, pair, out_cols, tick, q_ref, kb_ref, vb_ref, ko_ref, vo_ref, o_ref, do_ref, lse_ref,
    cos_ref, sin_ref, dq_ref, dkb_ref, dvb_ref, dko_ref, dvo_ref, bias, diag, dk_sum, dv_sum,
):
    head_lane = lax.broadcasted_iota(jnp.int32, (8, LANES), 1)
    head_row = lax.broadcasted_iota(jnp.int32, (8, LANES), 0)
    pick = jnp.where(head_lane // 64 == head_row, 1.0, 0.0).astype(jnp.bfloat16)
    for i in reversed(range(rows // TILE)):
        band = slice(i * TILE, (i + 1) * TILE)
        n = (i + 1) * TILE
        q2 = two_heads(q_ref[band, :])
        do = do_ref[band, :]
        do2 = two_heads(do)
        prod = do.astype(jnp.float32) * o_ref[band, :].astype(jnp.float32)
        high = prod.astype(jnp.bfloat16)
        rest = (prod - high.astype(jnp.float32)).astype(jnp.bfloat16)
        inner = nt(pick, high) + nt(pick, rest)
        inner = jnp.concatenate([inner[0:1], inner[1:2]], axis=1)
        level = jnp.concatenate(
            [lse_ref[pl.ds(2 * pair, 1), band], lse_ref[pl.ds(2 * pair + 1, 1), band]], axis=1
        )
        b = bias[i][...]
        s = nt(kb_ref[:n, :], q2) + jnp.concatenate([b, b], axis=1)
        p = jnp.exp(s - level)
        dp = nt(vb_ref[:n, :], do2)
        ds = (p * (dp - inner)).astype(jnp.bfloat16)
        dv = nn(p.astype(jnp.bfloat16), do2)
        dk = nn(ds, q2)
        if i == rows // TILE - 1:
            dv_sum[...] = dv
            dk_sum[...] = dk
        else:
            dv_sum[:n, :] += dv
            dk_sum[:n, :] += dk
        dq = tn(ds, kb_ref[:n, :])
        extra = []
        for sub in range(TILE // SUB):
            low = i * TILE + sub * SUB
            part = slice(low, low + SUB)
            qs, dos = subs(q2, sub), subs(do2, sub)
            d = diag[:, part]
            at = slice(sub * SUB, (sub + 1) * SUB)
            at2 = slice(TILE + sub * SUB, TILE + (sub + 1) * SUB)
            lev = jnp.concatenate([level[:, at], level[:, at2]], axis=1)
            inn = jnp.concatenate([inner[:, at], inner[:, at2]], axis=1)
            s = nt(ko_ref[part, :], qs) + jnp.concatenate([d, d], axis=1)
            p = jnp.exp(s - lev)
            dp = nt(vo_ref[part, :], dos)
            ds = (p * (dp - inn)).astype(jnp.bfloat16)
            dvo_ref[part, out_cols] = nn(p.astype(jnp.bfloat16), dos).astype(jnp.bfloat16)
            dko = nn(ds, qs)
            dko_ref[part, out_cols] = turn(dko, cos_ref[part, :], -sin_ref[part, :]).astype(jnp.bfloat16)
            extra.append(tn(ds, ko_ref[part, :]))
        dq = dq + jnp.concatenate(
            [extra[0][:SUB], extra[1][:SUB], extra[0][SUB:], extra[1][SUB:]], axis=0
        )
        dq = one_row(dq) * score_scale
        dq_ref[band, out_cols] = turn(dq, cos_ref[band, :], -sin_ref[band, :]).astype(jnp.bfloat16)
        tick(rows // TILE - i)
    dvb_ref[:, out_cols] = dv_sum[...].astype(jnp.bfloat16)
    dkb_ref[:, out_cols] = turn(dk_sum[...], cos_ref[...], -sin_ref[...]).astype(jnp.bfloat16)


def attend_back_kernel(
    rows, score_scale, q_ref, kb_ref, vb_ref, ko_ref, vo_ref, o_ref, do_ref, lse_ref, meta_ref, cos_ref, sin_ref,
    *refs,
):
    pair = pl.program_id(0)
    dq_ref, dkb_ref, dvb_ref, dko_ref, dvo_ref, *bias, diag, dk_sum, dv_sum = refs
    pl.when(pair == 0)(lambda: mask_back(rows, meta_ref, bias, diag))
    pair_back(
        rows, score_scale, pair, slice(None), lambda slot: None, q_ref, kb_ref, vb_ref, ko_ref, vo_ref, o_ref,
        do_ref, lse_ref, cos_ref, sin_ref, dq_ref, dkb_ref, dvb_ref, dko_ref, dvo_ref, bias, diag, dk_sum,
        dv_sum,
    )


def back_scratch(rows):
    return [pltpu.VMEM(((i + 1) * TILE, TILE), jnp.float32) for i in range(rows // TILE)] + [
        pltpu.VMEM((SUB, rows), jnp.float32),
        pltpu.VMEM((rows, LANES), jnp.float32),
        pltpu.VMEM((rows, LANES), jnp.float32),
    ]


def attend_back(q, kb, vb, ko, vo, o, do, lse, meta, cosine, sine, score_scale):
    rows, width = q.shape
    pairs = width // LANES
    spec = pl.BlockSpec((rows, LANES), lambda j: (0, j))
    whole = lambda a: pl.BlockSpec(a.shape, lambda j: (0, 0))
    return pl.pallas_call(
        functools.partial(attend_back_kernel, rows, score_scale),
        grid=(pairs,),
        in_specs=[spec] * 7 + [whole(lse), whole(meta), whole(cosine), whole(sine)],
        out_specs=[spec] * 5,
        out_shape=[jax.ShapeDtypeStruct((rows, width), jnp.bfloat16)] * 5,
        scratch_shapes=back_scratch(rows),
        compiler_params=pltpu.CompilerParams(vmem_limit_bytes=48 * MIB),
        cost_estimate=pl.CostEstimate(
            flops=5 * 2 * rows * rows * width, bytes_accessed=24 * rows * width, transcendentals=0
        ),
        name="attend_back",
    )(q, kb, vb, ko, vo, o, do, lse, meta, cosine, sine)


F1, OUT, F2, P0, P1, P2, N = range(7)
TAIL_STREAMS = (
    ("yxlh", 1024), ("ylhx", 384), ("xylh", 1024), ("lhyx", 384), ("xylh", 384), ("ylhx", 384), ("xylh", 128),
)
TAIL_FAR = 3
TAIL_TICKS = {
    (0, 3): [(OUT, 0)],
    (1, 2): [(F2, 0)],
    (1, 4): [(F1, 0)],
    (1, 5): [(OUT, 1)],
    (2, 2): [(P0, 0)],
    (2, 4): [(OUT, 2)],
    (3, 5): [(P0, 1), (F2, 1)],
    (4, 1): [(OUT, 3), (F1, 1)],
    (4, 2): [(P1, 0)],
    (4, 4): [(OUT, 4)],
    (5, 2): [(P0, 2)],
    (5, 3): [(F2, 2)],
    (5, 5): [(F1, 2), (P0, 3)],
}
TAIL_POST = {
    0: [(P2, 0)],
    1: [(F2, 3)],
    2: [(P1, 1), (P0, 4)],
    3: [(F1, 3)],
    5: [(N, 0), (P2, 1), (F2, 4)],
    6: [(P1, 2), (F1, 4), (P2, 2), (N, 1), (P1, 3), (N, 2)],
    7: [(P2, 3), (N, 3), (P1, 4), (P2, 4), (N, 4)],
}


def normalized(x):
    x = x.astype(jnp.float32)
    centre = x - jnp.mean(x, axis=-1, keepdims=True)
    inverse = lax.rsqrt(jnp.mean(centre * centre, axis=-1, keepdims=True) + epsilon)
    return centre * inverse, inverse


def normal_back(grad, gain, n, inverse):
    e = grad * gain
    return inverse * (
        e - jnp.mean(e, axis=-1, keepdims=True) - n * jnp.mean(e * n, axis=-1, keepdims=True)
    )


def tail_kernel(
    rows, score_scale, q_ref, kb_ref, vb_ref, ko_ref, vo_ref, o_ref, do_ref, lse_ref, meta_ref, cos_ref, sin_ref,
    h1t_ref, h1bt_ref, gain_ref, norm_ref, *refs,
):
    pair = pl.program_id(0)
    hbm, refs = refs[:6], refs[6:]
    ff_ref, go_ref, refs = refs[0], refs[1], refs[2:]
    out_ref, g_out, refs = refs[0], refs[1], refs[2:]
    scratch, refs = refs[:7], refs[7:]
    bias, (diag, dk_sum, dv_sum) = scratch[:4], scratch[4:]
    dq, dkb, dvb, dko, dvo, refs = *refs[:5], refs[5:]
    held, refs = refs[:5], refs[5:]
    wq, wk, wv, x, base = held
    coming, pair_sums, norm_sums, refs = refs[0], refs[1:4], refs[4], refs[5:]
    load_sem, send_sem, recv_sem, refs = refs[0], refs[1], refs[2], refs[3:]
    sources = [(ff_ref.at[1], 0), (go_ref, 0), (ff_ref.at[2], 0)]
    sources += [(ref, 0) for ref in (*pair_sums, norm_sums)]
    scatter = Scatter(TAIL_STREAMS, sources, g_out, refs, TAIL_FAR)
    stream = lax.axis_index("stream")
    tiles = rows // TILE
    width = x.shape[1]
    loads = [
        pltpu.make_async_copy(src, dst, load_sem.at[i])
        for i, (src, dst) in enumerate(zip(hbm, (*held, out_ref)))
    ]

    def tick(slot):
        for at, moves in TAIL_TICKS.items():
            if at[1] == slot:
                @pl.when(pair == at[0])
                def _(moves=moves):
                    for number, index in moves:
                        scatter.step(number, index)

    def post(slot):
        for number, index in TAIL_POST.get(slot, ()):
            scatter.step(number, index)

    @pl.when(pair == 0)
    def _():
        scatter.greet()
        scatter.open((OUT, F2, F1))
        for load in loads:
            load.start()
        mask_back(rows, meta_ref, bias, diag)

    cols = pl.ds(pl.multiple_of(pair * LANES, LANES), LANES)
    pair_back(
        rows, score_scale, pair, cols, tick, q_ref, kb_ref, vb_ref, ko_ref, vo_ref, o_ref,
        do_ref, lse_ref, cos_ref, sin_ref, dq, dkb, dvb, dko, dvo, bias, diag, dk_sum, dv_sum,
    )

    for number, sums in enumerate(pair_sums):
        @pl.when(pair == 2 * number + 1)
        def _(number=number, sums=sums):
            both = slice(2 * number * LANES, (2 * number + 2) * LANES)
            for at, block in enumerate((
                nn(h1t_ref[...], dq[:, both]),
                nn(h1t_ref[...], dko[:, both]) + nn(h1bt_ref[...], dkb[:, both]),
                nn(h1t_ref[...], dvo[:, both]) + nn(h1bt_ref[...], dvb[:, both]),
            )):
                block = block.astype(jnp.bfloat16)
                for half in range(2):
                    sums[half, :, :, :, :, :, at * LANES : (at + 1) * LANES] = block[
                        :, half * LANES : (half + 1) * LANES
                    ].reshape(2, 2, 2, 2, RUN, LANES)
            scatter.open((P0 + number,))

    tick(tiles + 1)

    @pl.when(pair == pl.num_programs(0) - 1)
    def _():
        for load in loads:
            load.wait()
        gain = gain_ref[...]

        def band(r):
            return slice(r * TILE, (r + 1) * TILE)

        def move(r):
            return pltpu.make_async_remote_copy(
                src_ref=dkb.at[band(r)],
                dst_ref=coming.at[band(r)],
                send_sem=send_sem.at[r],
                recv_sem=recv_sem.at[r],
                device_id=scatter.to["x"],
                device_id_type=MESH,
            )

        gain_sum = jnp.zeros((1, width), jnp.float32)
        bias_sum = jnp.zeros((1, width), jnp.float32)
        for r in range(tiles):
            at = band(r)
            grad = nt(dkb[at, :], wk[...]) + nt(dvb[at, :], wv[...])
            dkb[at, :] = grad.astype(jnp.bfloat16)
            pl.when(stream == 1)(lambda r=r: move(r).start())
            n, _ = normalized(base[at, :])
            gain_sum += jnp.sum(grad * n, axis=0, keepdims=True)
            bias_sum += jnp.sum(grad, axis=0, keepdims=True)
        post(0)
        for r in range(tiles):
            at = band(r)
            grad = nt(dq[at, :], wq[...]) + nt(dko[at, :], wk[...]) + nt(dvo[at, :], wv[...])
            n, inverse = normalized(x[at, :])
            gain_sum += jnp.sum(grad * n, axis=0, keepdims=True)
            bias_sum += jnp.sum(grad, axis=0, keepdims=True)
            grad = grad + jnp.where(stream == 0, dkb[at, :].astype(jnp.float32), 0.0)
            out_ref[at, :] += normal_back(grad, gain, n, inverse)
            post(r + 1)
        eye = jnp.where(
            lax.broadcasted_iota(jnp.int32, (8, LANES), 0)
            == lax.broadcasted_iota(jnp.int32, (8, LANES), 1),
            1.0,
            0.0,
        ).astype(jnp.bfloat16)
        zero = jnp.zeros((6, width), jnp.float32)
        for half, sums in enumerate((
            jnp.concatenate([gain_sum, bias_sum, zero], axis=0), norm_ref[...]
        )):
            block = tn(sums.astype(jnp.bfloat16), eye).astype(jnp.bfloat16)
            norm_sums[half] = block.reshape(2, 2, 2, 2, RUN, LANES)
        scatter.open((N,))
        post(tiles + 1)
        for r in range(tiles):
            at = band(r)

            @pl.when(stream == 1)
            def _(r=r):
                move(r).wait_send()

            @pl.when(stream == 0)
            def _(r=r, at=at):
                move(r).wait_recv()
                n, inverse = normalized(x[at, :])
                out_ref[at, :] += normal_back(coming[at, :].astype(jnp.float32), gain, n, inverse)

            post(tiles + 2 + r)
        scatter.finish()


def tail(operands, h1t, h1bt, gain, norm, weights, x, base, middle_grad, ff, go, score_scale):
    rows, width = x.shape
    pairs = width // LANES
    total = sum(part for _, part in TAIL_STREAMS)
    spec = pl.BlockSpec((rows, LANES), lambda j: (0, j))
    once = pl.Buffered(1)
    whole = lambda shape: pl.BlockSpec(shape, lambda j: (0,) * len(shape), pipeline_mode=once)
    flat, square = (rows, width), (width, width)
    low = jnp.bfloat16
    scratch = back_scratch(rows)
    scratch += [pltpu.VMEM(flat, low)] * 5
    scratch += [pltpu.VMEM(square, low)] * 3 + [pltpu.VMEM(flat, low)] * 2
    scratch += [pltpu.VMEM(flat, low)]
    scratch += [pltpu.VMEM((2, 2, 2, 2, 2, RUN, 3 * LANES), low)] * 3
    scratch += [pltpu.VMEM((2, 2, 2, 2, 2, RUN, LANES), low)]
    scratch += [pltpu.SemaphoreType.DMA((6,))]
    scratch += [pltpu.SemaphoreType.DMA((rows // TILE,))] * 2
    scratch += Scatter.shapes(TAIL_STREAMS, TAIL_FAR)
    return pl.pallas_call(
        functools.partial(tail_kernel, rows, score_scale),
        grid=(pairs,),
        in_specs=[spec] * 7
        + [whole(a.shape) for a in (*operands[7:], h1t, h1bt, gain, norm)]
        + [pl.BlockSpec(memory_space=pl.ANY)] * 8,
        out_specs=[whole(flat), whole((2, 24, total))],
        out_shape=[
            jax.ShapeDtypeStruct(flat, jnp.float32),
            jax.ShapeDtypeStruct((2, 24, total), jnp.float32),
        ],
        scratch_shapes=scratch,
        compiler_params=pltpu.CompilerParams(
            collective_id=0, has_side_effects=True, vmem_limit_bytes=63 * MIB
        ),
        cost_estimate=pl.CostEstimate(
            flops=10 * rows * rows * width + 20 * rows * width * width,
            bytes_accessed=40 * MIB,
            transcendentals=0,
        ),
        name="tail",
    )(*operands, h1t, h1bt, gain, norm, *weights, x, base, middle_grad, ff, go)


FEED_TILE = 1024
FEED_STREAMS = (("yxlh", 512), ("xylh", 512))
FEED_TICKS = {
    (1, 1): [(0, 0), (1, 0)], (1, 5): [(0, 1), (1, 1)], (2, 1): [(0, 2), (1, 2)], (2,5): [(0, 3), (1, 3)], (2,6): [(0, 4), (1, 4)],
}


def feed_kernel(
    streams, x_ref, o_ref, dy_ref, wo_ref, gain_ref, bias_ref, wu_ref, wd_ref,
    y_ref, do_ref, dx_ref, norm_ref, ff_ref, go_ref, *refs,
):
    f = pl.program_id(0)
    rows, width = x_ref.shape
    scatter = None
    if streams:
        out_ref, refs = refs[0], refs[1:]
    total, normal, scale, h2s, h2t, dyt, gs, dus = refs[:8]
    if streams:
        first = refs[8]
        sources, low = [], 0
        for _, part in streams:
            sources.append((first, low))
            low += part
        scatter = Scatter(streams, sources, out_ref, refs[9:], 0)

    def tick(slot):
        if scatter is None:
            return
        for at, moves in FEED_TICKS.items():
            if at[1] == slot:
                @pl.when(f == at[0])
                def _(moves=moves):
                    for stream, index in moves:
                        scatter.step(stream, index)

    def band(r):
        return pl.ds(pl.multiple_of(r * TILE, TILE), TILE)

    @pl.when(f == 0)
    def _():
        if scatter is not None:
            scatter.greet()
        norm_ref[...] = jnp.zeros_like(norm_ref)

        @pl.loop(0, rows // TILE)
        def _(r):
            at = band(r)
            x1 = x_ref[at, :].astype(jnp.float32) + nn(o_ref[at, :], wo_ref[...])
            centre = x1 - jnp.mean(x1, axis=-1, keepdims=True)
            inverse = lax.rsqrt(jnp.mean(centre * centre, axis=-1, keepdims=True) + epsilon)
            n = centre * inverse
            h2 = (n * gain_ref[...] + bias_ref[...]).astype(jnp.bfloat16)
            total[at, :] = x1
            normal[at, :] = n
            scale[at, :] = jnp.broadcast_to(inverse, (TILE, LANES))
            h2s[at, :] = h2
            h2t[:, at] = jnp.transpose(h2)
            dyt[:, at] = jnp.transpose(dy_ref[at, :])
            dx_ref[at, :] = jnp.zeros((TILE, width), jnp.float32)

    for r in range(rows // TILE):
        at = band(r)
        u = nn(h2s[at, :], wu_ref[...])
        square = u * u
        curve = jnp.tanh(0.7978845608028654 * u * (1.0 + 0.044715 * square))
        upper = 0.5 * (1.0 + curve)
        g = (u * upper).astype(jnp.bfloat16)
        slope = upper + u * upper * (1.0 - curve) * (
            0.7978845608028654 + 3 * 0.044715 * 0.7978845608028654 * square
        )
        gs[at, :] = g
        total[at, :] += nn(g, wd_ref[...])
        du = (nt(dy_ref[at, :], wd_ref[...]) * slope).astype(jnp.bfloat16)
        dus[at, :] = du
        dx_ref[at, :] += nt(du, wu_ref[...])
        tick(r)
    slot = rows // TILE
    for half, (left, right) in enumerate(((h2t, dus), (dyt, gs))):
        for c in range(right.shape[1] // TILE):
            cols = pl.ds(c * TILE, TILE)
            block = nn(left[...], right[:, cols]).astype(jnp.bfloat16)
            block = block.reshape(2, 2, 2, 2, RUN, TILE)
            ff_ref[0, half, :, :, :, :, :, cols] = block
        tick(slot + half)
    if scatter is not None:
        @pl.when(f == 0)
        def _():
            @pl.loop(0, 32)
            def _(i):
                at = (i // 16, i // 8 % 2, i // 4 % 2, i // 2 % 2, i % 2)
                first[at] = ff_ref[(0,) + at]

            scatter.open(range(len(streams)))

    @pl.when(f == pl.num_programs(0) - 1)
    def _():
        @pl.loop(0, rows // TILE)
        def _(r):
            at = band(r)
            y_ref[at, :] = total[at, :].astype(jnp.bfloat16)
            n = normal[at, :]
            dh2 = dx_ref[at, :]
            norm_ref[0:1, :] += jnp.sum(dh2 * n, axis=0, keepdims=True)
            norm_ref[1:2, :] += jnp.sum(dh2, axis=0, keepdims=True)
            e = dh2 * gain_ref[...]
            e = (
                e
                - jnp.mean(e, axis=-1, keepdims=True)
                - n * jnp.mean(e * n, axis=-1, keepdims=True)
            )
            dx = dy_ref[at, :].astype(jnp.float32) + scale[at, 0:1] * e
            dx_ref[at, :] = dx
            da = dx.astype(jnp.bfloat16)
            dyt[:, at] = jnp.transpose(da)
            do_ref[at, :] = nt(da, wo_ref[...]).astype(jnp.bfloat16)

        middle = width // 2
        for half in range(2):
            block = nn(dyt[...], o_ref[:, half * middle : (half + 1) * middle])
            go_ref[half] = block.astype(jnp.bfloat16).reshape(2, 2, 2, 2, RUN, middle)
        tick(slot + 2)
        if scatter is not None:
            scatter.finish()


def feed(x, o, dy, wo, gain, bias, wu, wd, streams):
    rows, width = x.shape
    tiles = wu.shape[1] // FEED_TILE
    once = pl.Buffered(1)
    whole = lambda shape: pl.BlockSpec(shape, lambda f: (0,) * len(shape), pipeline_mode=once)
    flat, line, square = (rows, width), (1, width), (width, width)
    parts = (2, 2, 2, 2, RUN)
    out_specs = [
        whole(flat),
        whole(flat),
        whole(flat),
        whole((8, width)),
        pl.BlockSpec((1, 2) + parts + (FEED_TILE,), lambda f: (f,) + (0,) * 7),
        whole((2,) + parts + (width // 2,)),
    ]
    out_shape = [
        jax.ShapeDtypeStruct(flat, jnp.bfloat16),
        jax.ShapeDtypeStruct(flat, jnp.bfloat16),
        jax.ShapeDtypeStruct(flat, jnp.float32),
        jax.ShapeDtypeStruct((8, width), jnp.float32),
        jax.ShapeDtypeStruct((tiles, 2) + parts + (FEED_TILE,), jnp.bfloat16),
        jax.ShapeDtypeStruct((2,) + parts + (width // 2,), jnp.bfloat16),
    ]
    scratch = [
        pltpu.VMEM(flat, jnp.float32),
        pltpu.VMEM(flat, jnp.float32),
        pltpu.VMEM((rows, LANES), jnp.float32),
        pltpu.VMEM(flat, jnp.bfloat16),
        pltpu.VMEM((width, rows), jnp.bfloat16),
        pltpu.VMEM((width, rows), jnp.bfloat16),
        pltpu.VMEM((rows, FEED_TILE), jnp.bfloat16),
        pltpu.VMEM((rows, FEED_TILE), jnp.bfloat16),
    ]
    options = {}
    if streams:
        out_specs += [whole((2, 24, FEED_TILE))]
        out_shape += [jax.ShapeDtypeStruct((2, 24, FEED_TILE), jnp.float32)]
        scratch += [pltpu.VMEM((2,) + parts + (FEED_TILE,), jnp.bfloat16)]
        scratch += Scatter.shapes(streams, 0)
        options = {"collective_id": 2, "has_side_effects": True}
    return pl.pallas_call(
        functools.partial(feed_kernel, streams),
        grid=(tiles,),
        in_specs=[
            whole(flat),
            whole(flat),
            whole(flat),
            whole(square),
            whole(line),
            whole(line),
            pl.BlockSpec((width, FEED_TILE), lambda f: (0, f)),
            pl.BlockSpec((FEED_TILE, width), lambda f: (f, 0)),
        ],
        out_specs=out_specs,
        out_shape=out_shape,
        scratch_shapes=scratch,
        compiler_params=pltpu.CompilerParams(vmem_limit_bytes=62 * MIB, **options),
        cost_estimate=pl.CostEstimate(
            flops=12 * rows * width * wu.shape[1] + 6 * rows * width * width,
            bytes_accessed=30 * MIB,
            transcendentals=0,
        ),
        name="feed",
    )(x, o, dy, wo, gain, bias, wu, wd)


def shards(
    tokens,
    lengths,
    pad_mask,
    first_gain,
    first_bias,
    query_weight,
    key_weight,
    value_weight,
    out_weight,
    second_gain,
    second_bias,
    up_weight,
    down_weight,
    output_grad,
):
    total_rows = tokens.shape[1]
    model_width = tokens.shape[2]
    head_width = model_width // H
    score_scale = head_width ** (-0.5)
    is_noisy = lax.axis_index("stream") == 1
    own = tokens[0]
    far = lax.ppermute(own, "stream", [(0, 1)])
    base = jnp.where(is_noisy, far, own)
    places, first_place = layout(lengths[0], total_rows, lengths.shape[1])
    limit = (places // BLOCK + jnp.where(is_noisy, 0, 1)) * BLOCK
    noisy_row = jnp.broadcast_to(jnp.where(is_noisy, 1, 0), places.shape)
    blank = jnp.zeros_like(places)
    meta = jnp.stack(
        [first_place, limit, pad_mask, noisy_row, blank, blank, blank, blank]
    ).astype(jnp.float32)
    cosine, sine = angle_tables(places - first_place, head_width)
    gain1, bias1 = first_gain[None], first_bias[None]
    h1t, q, ko, vo = project(
        own, gain1, bias1, cosine, sine, (query_weight, key_weight, value_weight), score_scale
    )
    h1bt, kb, vb = project(base, gain1, bias1, cosine, sine, (key_weight, value_weight), score_scale)
    mixed_low, lse = attend(q, kb, vb, ko, vo, meta)

    ring = lax.axis_size("dp") == 16 and lax.axis_size("stream") == 2
    fed = feed(
        own, mixed_low, output_grad[0], out_weight, second_gain[None], second_bias[None],
        up_weight, down_weight, FEED_STREAMS if ring else (),
    )
    layer_output, mixed_grad, middle_grad, norm_sums, ff_part, out_part = fed[:6]
    layer_output = layer_output[None]
    operands = (q, kb, vb, ko, vo, mixed_low, mixed_grad, lse, meta, cosine, sine)
    weights = (query_weight, key_weight, value_weight)
    if ring:
        tokens_grad, parts = tail(
            operands, h1t, h1bt, gain1, norm_sums, weights, own, base, middle_grad, ff_part, out_part,
            score_scale,
        )
        tokens_grad = tokens_grad[None]
        places, low = [], 0
        for _, part in TAIL_STREAMS:
            places.append(parts[:, :, low : low + part])
            low += part
        up_grad, down_grad = (
            jnp.concatenate([fed[6][i], places[F1][i], places[F2][i]], axis=1) for i in range(2)
        )
        out_grad = jnp.concatenate([places[OUT][0], places[OUT][1]], axis=1)
        query_grad, key_grad, value_grad = (
            jnp.concatenate(
                [
                    places[p][half, :, at * LANES : (at + 1) * LANES]
                    for p in (P0, P1, P2)
                    for half in range(2)
                ],
                axis=1,
            )
            for at in range(3)
        )
        first_grads, second_grads = places[N][0, :, :2].T, places[N][1, :, :2].T
    else:
        dq, dkb, dvb, dko, dvo = attend_back(*operands, score_scale)
        base_grad = nt(dkb, key_weight) + nt(dvb, value_weight)
        back = lax.ppermute(base_grad.astype(jnp.bfloat16), "stream", [(1, 0)])
        normed_grad = (
            nt(dq, query_weight)
            + nt(dko, key_weight)
            + nt(dvo, value_weight)
            + jnp.where(is_noisy, 0.0, base_grad + back.astype(jnp.float32))
        )
        inputs = own.astype(jnp.float32)
        first_pull = jax.vjp(layer_norm, inputs, first_gain, first_bias)[1]
        input_part, first_gain_part, first_bias_part = first_pull(normed_grad)
        tokens_grad = (middle_grad + input_part)[None]
        ff_part = ff_part.reshape(-1, 2, model_width, FEED_TILE)
        out_part = out_part.reshape(2, model_width, model_width // 2)
        norm_part = jnp.stack(
            [first_gain_part, first_bias_part, norm_sums[0], norm_sums[1]], axis=1
        )
        part = jnp.concatenate(
            [ff_part[f, i] for i in range(2) for f in range(ff_part.shape[0])]
            + [out_part[0], out_part[1], nn(h1t, dq).astype(jnp.bfloat16)]
            + [(nn(h1t, dko) + nn(h1bt, dkb)).astype(jnp.bfloat16)]
            + [(nn(h1t, dvo) + nn(h1bt, dvb)).astype(jnp.bfloat16)]
            + [jnp.pad(norm_part, ((0, 0), (0, LANES - 4))).astype(jnp.bfloat16)],
            axis=1,
        )
        part = lax.psum_scatter(part, ("stream", "dp"), scatter_dimension=0, tiled=True)
        part = part.astype(jnp.float32)
        hidden_width = up_weight.shape[1]
        cuts = (hidden_width, hidden_width) + (model_width,) * 4 + (LANES,)
        pieces, low = [], 0
        for cut in cuts:
            pieces.append(part[:, low : low + cut])
            low += cut
        up_grad, down_grad, out_grad, query_grad, key_grad, value_grad, norms = pieces
        first_grads, second_grads = norms[:, :2].T, norms[:, 2:4].T
    return (
        layer_output,
        tokens_grad,
        first_grads,
        query_grad,
        key_grad,
        value_grad,
        out_grad.T,
        second_grads,
        up_grad,
        down_grad.T,
    )


def solution(mesh):
    placed = (
        P("stream", "dp", None),
        P("dp", None),
        P("dp"),
        P(),
        P(),
        P(),
        P(),
        P(),
        P(),
        P(),
        P(),
        P(),
        P(),
        P("stream", "dp", None),
    )
    return jax.shard_map(
        shards,
        mesh=mesh,
        in_specs=placed,
        out_specs=(
            P("stream", "dp", None),
            P("stream", "dp", None),
            P(None, ("stream", "dp")),
            P(("stream", "dp"), None),
            P(("stream", "dp"), None),
            P(("stream", "dp"), None),
            P(None, ("stream", "dp")),
            P(None, ("stream", "dp")),
            P(("stream", "dp"), None),
            P(None, ("stream", "dp")),
        ),
        check_vma=False,
    )
```

```python
import functools
import math

import jax
import jax.numpy as jnp
from jax import lax
from jax.experimental import pallas as pl
from jax.experimental.pallas import tpu as pltpu
from jax.sharding import PartitionSpec as P

H = 12
BLOCK = 16
TILE = 256
SUB = 128
LANES = 128

epsilon = 1e-05
masked_score = -1e30
MIB = 1024 * 1024


def layer_norm(values, gain_row, bias_row):
    centre = values - jnp.mean(values, axis=-1, keepdims=True)
    spread = jnp.mean(centre * centre, axis=-1, keepdims=True)
    return centre * lax.rsqrt(spread + epsilon) * gain_row + bias_row


def layout(lengths_row, total_rows, doc_slots):
    places = jnp.arange(total_rows, dtype=jnp.int32)
    end_places = jnp.cumsum(lengths_row)
    starts = end_places - lengths_row
    document = jnp.sum((places[:, None] >= end_places[None, :]).astype(jnp.int32), axis=1)
    picked = document[:, None] == jnp.arange(doc_slots, dtype=jnp.int32)[None, :]
    first_place = jnp.sum(jnp.where(picked, starts[None, :], 0), axis=1)
    return (places, first_place)


def angle_tables(position, head_width):
    half_width = head_width // 2
    freq_index = (jnp.arange(half_width)).astype(jnp.float32)
    frequency = jnp.exp(freq_index * (-2.0 * math.log(10000.0) / head_width))
    turned = position.astype(jnp.float32)[:, None] * frequency[None, :]
    cosine, sine = jnp.cos(turned), jnp.sin(turned)
    return (
        jnp.concatenate([cosine] * 4, axis=1),
        jnp.concatenate([-sine, sine, -sine, sine], axis=1),
    )


def turn(values, cosine, sine):
    lane = lax.broadcasted_iota(jnp.int32, values.shape, 1)
    low = lax.rem(lane, 64) < 32
    partner = jnp.where(low, pltpu.roll(values, LANES - 32, 1), pltpu.roll(values, 32, 1))
    return values * cosine + partner * sine


def nt(left, right):
    return lax.dot_general(
        left, right, (((1,), (1,)), ((), ())), preferred_element_type=jnp.float32
    )


def tn(left, right):
    return lax.dot_general(
        left, right, (((0,), (0,)), ((), ())), preferred_element_type=jnp.float32
    )


def nn(left, right):
    return jnp.dot(left, right, preferred_element_type=jnp.float32)


MESH = pl.DeviceIdType.MESH
RUN = 48


class Scatter:
    @staticmethod
    def shapes(streams, far):
        total = sum(width for _, width in streams)
        shapes = [
            pltpu.VMEM((2, 2, 2, 2, RUN, total), jnp.bfloat16),
            pltpu.VMEM((2, 24, total), jnp.float32),
            pltpu.VMEM((24, total), jnp.float32),
        ]
        for number, (order, width) in enumerate(streams):
            if number < far:
                shapes += [pltpu.VMEM((2, 2, 2, 2, RUN, width), jnp.bfloat16)]
            for left in range(len(order) - 1, -1, -1):
                shapes += [pltpu.VMEM((2,) * left + (RUN, width), jnp.bfloat16)]
        count = sum(1 + len(order) for order, _ in streams) + 1
        return shapes + [
            pltpu.SemaphoreType.DMA((count,)),
            pltpu.SemaphoreType.DMA((count,)),
            pltpu.SemaphoreType.DMA((len(streams),)),
        ]

    def __init__(self, streams, sources, refs, far):
        self.far = far
        self.sib, self.fin, self.other = refs[:3]
        self.bufs = list(refs[3:-3])
        self.send, self.recv, self.local = refs[-3:]
        s, d = lax.axis_index("stream"), lax.axis_index("dp")
        self.core = d % 2
        self.mine = {"x": s, "y": d // 2 % 2, "l": d // 4 % 2, "h": d // 8}
        self.to = {
            "x": {"stream": 1 - s},
            "y": {"dp": d + 2 - 4 * self.mine["y"]},
            "l": {"dp": d + 4 - 8 * self.mine["l"]},
            "h": {"dp": d + 8 - 16 * self.mine["h"]},
            "core": {"dp": d + 1 - 2 * self.core},
        }
        self.used = 0
        self.streams = []
        place = 0
        for (order, width), (source, low) in zip(streams, sources):
            self.streams.append(self.stream(order, place, width, source, low))
            place += width
        self.last = self.take()

    def take(self):
        self.used += 1
        return self.used - 1

    def copy(self, src, dst, k, to):
        return pltpu.make_async_remote_copy(
            src_ref=src,
            dst_ref=dst,
            send_sem=self.send.at[k],
            recv_sem=self.recv.at[k],
            device_id=self.to[to],
            device_id_type=MESH,
        )

    def greet(self):
        barrier = pltpu.get_barrier_semaphore()
        for to in self.to.values():
            pl.semaphore_signal(barrier, inc=1, device_id=to, device_id_type=MESH)
        pl.semaphore_wait(barrier, len(self.to))

    @staticmethod
    def add(dst, left, right):
        lead = dst.shape[:-2]
        count = math.prod(lead)

        def one(index):
            at = []
            for size in reversed(lead):
                at.append(index % size)
                index = index // size
            at = tuple(reversed(at))
            dst[at] = left[at] + right[at]

        if count == 1:
            one(0)
        else:
            pl.loop(0, count)(one)

    def stream(self, order, place, width, source, low):
        number = len(self.streams)
        cols = pl.ds(place, width)
        every = (slice(None),) * 5
        src = self.sib.at[every + (cols,)]
        k = self.take()
        part = lambda core: source.at[(core,) + every + (pl.ds(low, width),)]
        swap = lambda src=src, k=k: self.copy(part(1 - self.core), src, k, "core")
        near = None
        if number < self.far:
            held = self.bufs.pop(0)
            near = lambda: pltpu.make_async_copy(part(self.core), held, self.local.at[number])

        def opening(src=src):
            swap().wait()
            if near is None:
                self.add(src, src, part(self.core))
            else:
                near().wait()
                self.add(src, src, held)

        steps = []
        pending = opening
        names = ["x", "h", "l", "y"]
        for axis in order:
            at = names.index(axis)
            names.pop(at)
            buf = self.bufs.pop(0)
            k = self.take()
            pick = lambda index, src=src, at=at: src.at[(slice(None),) * at + (index,)]
            make = lambda pick=pick, buf=buf, k=k, axis=axis: self.copy(
                pick(1 - self.mine[axis]), buf, k, axis
            )

            def begin(before=pending, make=make):
                before()
                make().start()

            def end(pick=pick, buf=buf, make=make, axis=axis):
                make().wait()
                self.add(buf, buf, pick(self.mine[axis]))

            steps.append(begin)
            pending = end
            src = buf

        def close(before=pending, src=src):
            before()
            for core in range(2):
                self.fin[core, :, cols] = src[24 * core : 24 * core + 24, :].astype(jnp.float32)

        steps.append(close)
        return (swap, near, steps)

    def open(self, order):
        for index in order:
            swap, near, _ = self.streams[index]
            swap().start()
            if near is not None:
                near().start()

    def step(self, stream, index):
        self.streams[stream][2][index]()

    def finish(self):
        last = self.copy(self.fin.at[1 - self.core], self.other, self.last, "core")
        last.start()
        last.wait()

    def result(self, half, place, width):
        cols = slice(place, place + width)
        return jnp.where(self.core == half, self.fin[half, :, cols], self.other[:, cols])


def project_kernel(score_scale, x_ref, vectors_ref, cos_ref, sin_ref, *refs):
    count = (len(refs) - 1) // 2
    weights, outs = refs[:count], refs[count:]
    h1 = layer_norm(
        x_ref[...].astype(jnp.float32), vectors_ref[0:1, :], vectors_ref[1:2, :]
    ).astype(jnp.bfloat16)
    outs[0][...] = jnp.transpose(h1)
    cosine, sine = cos_ref[...], sin_ref[...]
    for index, (weight, out) in enumerate(zip(weights, outs[1:])):
        product = nn(h1, weight[...])
        is_value = index == count - 1
        is_query = count == 3 and index == 0
        if is_value:
            out[...] = product.astype(jnp.bfloat16)
            continue
        for pair in range(product.shape[1] // LANES):
            columns = slice(pair * LANES, (pair + 1) * LANES)
            turned = turn(product[:, columns], cosine, sine)
            if is_query:
                turned = turned * score_scale
            out[:, columns] = turned.astype(jnp.bfloat16)


def project(x, vectors, cosine, sine, weights, score_scale):
    rows, width = x.shape
    count = len(weights)
    row_spec = pl.BlockSpec((TILE, width), lambda i: (i, 0))
    table_spec = pl.BlockSpec((TILE, LANES), lambda i: (i, 0))
    whole = pl.BlockSpec((width, width), lambda i: (0, 0))
    lines = pl.BlockSpec(vectors.shape, lambda i: (0, 0))
    return pl.pallas_call(
        functools.partial(project_kernel, score_scale),
        grid=(rows // TILE,),
        in_specs=[row_spec, lines, table_spec, table_spec] + [whole] * count,
        out_specs=[pl.BlockSpec((width, TILE), lambda i: (0, i))] + [row_spec] * count,
        out_shape=[jax.ShapeDtypeStruct((width, rows), jnp.bfloat16)]
        + [jax.ShapeDtypeStruct((rows, width), jnp.bfloat16)] * count,
        compiler_params=pltpu.CompilerParams(vmem_limit_bytes=40 * MIB),
        cost_estimate=pl.CostEstimate(
            flops=2 * rows * width * width * count,
            bytes_accessed=2 * (rows + count * (width + rows)) * width,
            transcendentals=0,
        ),
        name="project%d" % count,
    )(x, vectors, cosine, sine, *weights)


def two_heads(block):
    lane = lax.broadcasted_iota(jnp.int32, block.shape, 1)
    zero = jnp.zeros_like(block)
    return jnp.concatenate(
        [jnp.where(lane < 64, block, zero), jnp.where(lane < 64, zero, block)], axis=0
    )


def one_row(both):
    rows = both.shape[0] // 2
    lane = lax.broadcasted_iota(jnp.int32, (rows, LANES), 1)
    return jnp.where(lane < 64, both[:rows], both[rows:])


def subs(both, sub):
    low = sub * SUB
    return jnp.concatenate([both[low : low + SUB], both[TILE + low : TILE + low + SUB]], axis=0)


def mask_front(rows, meta_ref, bias, diag):
    columns = jnp.transpose(meta_ref[...])
    noisy = columns[:, 3:4]
    for i in range(rows // TILE):
        band = slice(i * TILE, (i + 1) * TILE)
        n = (i + 1) * TILE
        start, limit = columns[band, 0:1], columns[band, 1:2]
        key = lax.broadcasted_iota(jnp.int32, (TILE, n), 1)
        query = lax.broadcasted_iota(jnp.int32, (TILE, n), 0) + i * TILE
        usable = (meta_ref[2:3, :n] == 1.0) | (key == query)
        place = key.astype(jnp.float32)
        seen = (place >= start) & (place < limit) & usable
        bias[i][...] = jnp.where(seen, 0.0, masked_score)
        for sub in range(TILE // SUB):
            low = i * TILE + sub * SUB
            key = lax.broadcasted_iota(jnp.int32, (SUB, SUB), 1) + low
            query = lax.broadcasted_iota(jnp.int32, (SUB, SUB), 0) + low
            usable = (meta_ref[2:3, low : low + SUB] == 1.0) | (key == query)
            same = (key // BLOCK == query // BLOCK) & (
                key.astype(jnp.float32) >= columns[low : low + SUB, 0:1]
            )
            seen = same & usable & (noisy[low : low + SUB] == 1.0)
            diag[low : low + SUB, :] = jnp.where(seen, 0.0, masked_score)


def tile_front(i, pair, cols, q_ref, kb_ref, vb_ref, ko_ref, vo_ref, o_ref, bias, diag, lse):
    band = slice(i * TILE, (i + 1) * TILE)
    n = (i + 1) * TILE
    lane = lax.broadcasted_iota(jnp.int32, (TILE, LANES), 1)
    q2 = two_heads(q_ref[band, cols])
    b = bias[i][...]
    s = nt(q2, kb_ref[:n, cols]) + jnp.concatenate([b, b], axis=0)
    d = diag[band, :]

    def apart(sub):
        return slice(i * TILE + sub * SUB, i * TILE + (sub + 1) * SUB)

    def merge(parts):
        return jnp.concatenate(
            [parts[0][:SUB], parts[1][:SUB], parts[0][SUB:], parts[1][SUB:]], axis=0
        )

    parts = [nt(subs(q2, sub), ko_ref[apart(sub), cols]) for sub in range(TILE // SUB)]
    sd = merge(parts) + jnp.concatenate([d, d], axis=0)
    top = jnp.maximum(jnp.max(s, axis=1, keepdims=True), jnp.max(sd, axis=1, keepdims=True))
    p = jnp.exp(s - top)
    pd = jnp.exp(sd - top)
    total = jnp.sum(p, axis=1, keepdims=True) + jnp.sum(pd, axis=1, keepdims=True)
    pd_low = pd.astype(jnp.bfloat16)
    o = nn(p.astype(jnp.bfloat16), vb_ref[:n, cols])
    parts = [nn(subs(pd_low, sub), vo_ref[apart(sub), cols]) for sub in range(TILE // SUB)]
    o = (o + merge(parts)) * (1.0 / total)
    o_ref[band, cols] = one_row(o).astype(o_ref.dtype)
    level = top + jnp.log(total)
    old = lse[band, :]
    lse[band, :] = jnp.where(
        lane == 2 * pair, level[:TILE], jnp.where(lane == 2 * pair + 1, level[TILE:], old)
    )


def attend_kernel(rows, q_ref, kb_ref, vb_ref, ko_ref, vo_ref, meta_ref, o_ref, lse_ref, *refs):
    bias, diag, lse = refs[:-2], refs[-2], refs[-1]
    pair = pl.program_id(0)
    pl.when(pair == 0)(lambda: mask_front(rows, meta_ref, bias, diag))
    for i in range(rows // TILE):
        tile_front(
            i, pair, slice(None), q_ref, kb_ref, vb_ref, ko_ref, vo_ref, o_ref, bias, diag, lse
        )

    @pl.when(pair == pl.num_programs(0) - 1)
    def _():
        lse_ref[...] = jnp.transpose(lse[...])[: lse_ref.shape[0], :]


def front_scratch(rows):
    return [pltpu.VMEM((TILE, (i + 1) * TILE), jnp.float32) for i in range(rows // TILE)] + [
        pltpu.VMEM((rows, SUB), jnp.float32),
        pltpu.VMEM((rows, LANES), jnp.float32),
    ]


def front_kernel(
    score_scale, x_ref, vectors_ref, cos_ref, sin_ref, wq_ref, wk_ref, wv_ref, meta_ref,
    base_ref, h1t_ref, h1bt_ref, q_ref, kb_ref, vb_ref, ko_ref, vo_ref, o_ref, lse_ref, *refs,
):
    bias, diag, lse = refs[:4], refs[4], refs[5]
    coming, send_sem, recv_sem = refs[6:]
    rows, width = x_ref.shape
    stream = lax.axis_index("stream")
    gain, shift = vectors_ref[0:1, :], vectors_ref[1:2, :]
    partner = {"stream": 1 - stream}

    def move(r):
        return pltpu.make_async_remote_copy(
            src_ref=x_ref.at[r * TILE : (r + 1) * TILE],
            dst_ref=coming.at[r * TILE : (r + 1) * TILE],
            send_sem=send_sem.at[r],
            recv_sem=recv_sem.at[r],
            device_id=partner,
            device_id_type=MESH,
        )

    barrier = pltpu.get_barrier_semaphore()
    pl.semaphore_signal(barrier, inc=1, device_id=partner, device_id_type=MESH)
    pl.semaphore_wait(barrier, 1)
    tiles = rows // TILE

    @pl.when(stream == 0)
    def _():
        for r in range(tiles):
            move(r).start()

    def put(product, out, at, table, scale=None):
        for pair in range(width // LANES):
            cols = slice(pair * LANES, (pair + 1) * LANES)
            turned = turn(product[:, cols], *table)
            if scale is not None:
                turned = turned * scale
            out[at, cols] = turned.astype(jnp.bfloat16)

    def lower(block):
        return layer_norm(block.astype(jnp.float32), gain, shift).astype(jnp.bfloat16)

    @pl.loop(0, tiles)
    def _(r):
        at = pl.ds(pl.multiple_of(r * TILE, TILE), TILE)
        table = cos_ref[at, :], sin_ref[at, :]
        h1 = lower(x_ref[at, :])
        h1t_ref[:, at] = jnp.transpose(h1)
        put(nn(h1, wq_ref[...]), q_ref, at, table, score_scale)
        put(nn(h1, wk_ref[...]), ko_ref, at, table)
        vo_ref[at, :] = nn(h1, wv_ref[...]).astype(jnp.bfloat16)

    mask_front(rows, meta_ref, bias, diag)
    for r in range(tiles):
        at = slice(r * TILE, (r + 1) * TILE)

        @pl.when(stream == 0)
        def _(at=at):
            base_ref[at, :] = x_ref[at, :]

        @pl.when(stream == 1)
        def _(r=r, at=at):
            move(r).wait_recv()
            base_ref[at, :] = coming[at, :]

        h1 = lower(base_ref[at, :])
        h1bt_ref[:, at] = jnp.transpose(h1)
        put(nn(h1, wk_ref[...]), kb_ref, at, (cos_ref[at, :], sin_ref[at, :]))
        vb_ref[at, :] = nn(h1, wv_ref[...]).astype(jnp.bfloat16)

        @pl.loop(0, width // LANES)
        def _(pair, r=r):
            cols = pl.ds(pl.multiple_of(pair * LANES, LANES), LANES)
            tile_front(r, pair, cols, q_ref, kb_ref, vb_ref, ko_ref, vo_ref, o_ref, bias, diag, lse)

    lse_ref[...] = jnp.transpose(lse[...])[: lse_ref.shape[0], :]

    @pl.when(stream == 0)
    def _():
        for r in range(tiles):
            move(r).wait_send()


def front(x, vectors, cosine, sine, weights, meta, score_scale):
    rows, width = x.shape
    low = jnp.bfloat16
    flat = jax.ShapeDtypeStruct((rows, width), low)
    flipped = jax.ShapeDtypeStruct((width, rows), low)
    vmem = pl.BlockSpec(memory_space=pltpu.VMEM)
    return pl.pallas_call(
        functools.partial(front_kernel, score_scale),
        in_specs=[vmem] * 8,
        out_specs=[vmem] * 10,
        out_shape=[flat, flipped, flipped]
        + [flat] * 6
        + [jax.ShapeDtypeStruct((16, rows), jnp.float32)],
        scratch_shapes=front_scratch(rows)
        + [
            pltpu.VMEM((rows, width), low),
            pltpu.SemaphoreType.DMA((rows // TILE,)),
            pltpu.SemaphoreType.DMA((rows // TILE,)),
        ],
        compiler_params=pltpu.CompilerParams(
            collective_id=1, has_side_effects=True, vmem_limit_bytes=62 * MIB
        ),
        cost_estimate=pl.CostEstimate(
            flops=4 * rows * rows * width + 10 * rows * width * width,
            bytes_accessed=20 * MIB,
            transcendentals=0,
        ),
        name="front",
    )(x, vectors, cosine, sine, *weights, meta)


def attend(q, kb, vb, ko, vo, meta):
    rows, width = q.shape
    pairs = width // LANES
    spec = pl.BlockSpec((rows, LANES), lambda j: (0, j))
    return pl.pallas_call(
        functools.partial(attend_kernel, rows),
        grid=(pairs,),
        in_specs=[spec] * 5 + [pl.BlockSpec(meta.shape, lambda j: (0, 0))],
        out_specs=[spec, pl.BlockSpec((16, rows), lambda j: (0, 0))],
        out_shape=[
            jax.ShapeDtypeStruct((rows, width), jnp.bfloat16),
            jax.ShapeDtypeStruct((16, rows), jnp.float32),
        ],
        scratch_shapes=front_scratch(rows),
        compiler_params=pltpu.CompilerParams(vmem_limit_bytes=48 * MIB),
        cost_estimate=pl.CostEstimate(
            flops=2 * 2 * rows * rows * width, bytes_accessed=12 * rows * width, transcendentals=0
        ),
        name="attend",
    )(q, kb, vb, ko, vo, meta)


def mask_back(rows, meta_ref, bias, diag):
    columns = jnp.transpose(meta_ref[...])
    for i in range(rows // TILE):
        band = slice(i * TILE, (i + 1) * TILE)
        n = (i + 1) * TILE
        start, limit = meta_ref[0:1, band], meta_ref[1:2, band]
        key = lax.broadcasted_iota(jnp.int32, (n, TILE), 0)
        query = lax.broadcasted_iota(jnp.int32, (n, TILE), 1) + i * TILE
        usable = (columns[:n, 2:3] == 1.0) | (key == query)
        place = key.astype(jnp.float32)
        seen = (place >= start) & (place < limit) & usable
        bias[i][...] = jnp.where(seen, 0.0, masked_score)
        for sub in range(TILE // SUB):
            low = i * TILE + sub * SUB
            part = slice(low, low + SUB)
            key = lax.broadcasted_iota(jnp.int32, (SUB, SUB), 0) + low
            query = lax.broadcasted_iota(jnp.int32, (SUB, SUB), 1) + low
            usable = (columns[part, 2:3] == 1.0) | (key == query)
            same = (key // BLOCK == query // BLOCK) & (
                key.astype(jnp.float32) >= meta_ref[0:1, part]
            )
            seen = same & usable & (meta_ref[3:4, part] == 1.0)
            diag[:, part] = jnp.where(seen, 0.0, masked_score)


def pair_back(
    rows, score_scale, pair, out_cols, tick, q_ref, kb_ref, vb_ref, ko_ref, vo_ref, o_ref, do_ref, lse_ref,
    cos_ref, sin_ref, dq_ref, dkb_ref, dvb_ref, dko_ref, dvo_ref, bias, diag, dk_sum, dv_sum,
):
    head_lane = lax.broadcasted_iota(jnp.int32, (8, LANES), 1)
    head_row = lax.broadcasted_iota(jnp.int32, (8, LANES), 0)
    pick = jnp.where(head_lane // 64 == head_row, 1.0, 0.0).astype(jnp.bfloat16)
    for i in reversed(range(rows // TILE)):
        band = slice(i * TILE, (i + 1) * TILE)
        n = (i + 1) * TILE
        q2 = two_heads(q_ref[band, :])
        do = do_ref[band, :]
        do2 = two_heads(do)
        prod = do.astype(jnp.float32) * o_ref[band, :].astype(jnp.float32)
        high = prod.astype(jnp.bfloat16)
        rest = (prod - high.astype(jnp.float32)).astype(jnp.bfloat16)
        inner = nt(pick, high) + nt(pick, rest)
        inner = jnp.concatenate([inner[0:1], inner[1:2]], axis=1)
        level = jnp.concatenate(
            [lse_ref[pl.ds(2 * pair, 1), band], lse_ref[pl.ds(2 * pair + 1, 1), band]], axis=1
        )
        b = bias[i][...]
        s = nt(kb_ref[:n, :], q2) + jnp.concatenate([b, b], axis=1)
        p = jnp.exp(s - level)
        dp = nt(vb_ref[:n, :], do2)
        ds = (p * (dp - inner)).astype(jnp.bfloat16)
        dv = nn(p.astype(jnp.bfloat16), do2)
        dk = nn(ds, q2)
        if i == rows // TILE - 1:
            dv_sum[...] = dv
            dk_sum[...] = dk
        else:
            dv_sum[:n, :] += dv
            dk_sum[:n, :] += dk
        dq = tn(ds, kb_ref[:n, :])
        extra = []
        for sub in range(TILE // SUB):
            low = i * TILE + sub * SUB
            part = slice(low, low + SUB)
            qs, dos = subs(q2, sub), subs(do2, sub)
            d = diag[:, part]
            at = slice(sub * SUB, (sub + 1) * SUB)
            at2 = slice(TILE + sub * SUB, TILE + (sub + 1) * SUB)
            lev = jnp.concatenate([level[:, at], level[:, at2]], axis=1)
            inn = jnp.concatenate([inner[:, at], inner[:, at2]], axis=1)
            s = nt(ko_ref[part, :], qs) + jnp.concatenate([d, d], axis=1)
            p = jnp.exp(s - lev)
            dp = nt(vo_ref[part, :], dos)
            ds = (p * (dp - inn)).astype(jnp.bfloat16)
            dvo_ref[part, out_cols] = nn(p.astype(jnp.bfloat16), dos).astype(jnp.bfloat16)
            dko = nn(ds, qs)
            dko_ref[part, out_cols] = turn(dko, cos_ref[part, :], -sin_ref[part, :]).astype(jnp.bfloat16)
            extra.append(tn(ds, ko_ref[part, :]))
        dq = dq + jnp.concatenate(
            [extra[0][:SUB], extra[1][:SUB], extra[0][SUB:], extra[1][SUB:]], axis=0
        )
        dq = one_row(dq) * score_scale
        dq_ref[band, out_cols] = turn(dq, cos_ref[band, :], -sin_ref[band, :]).astype(jnp.bfloat16)
        tick(rows // TILE - i)
    dvb_ref[:, out_cols] = dv_sum[...].astype(jnp.bfloat16)
    dkb_ref[:, out_cols] = turn(dk_sum[...], cos_ref[...], -sin_ref[...]).astype(jnp.bfloat16)


def attend_back_kernel(
    rows, score_scale, q_ref, kb_ref, vb_ref, ko_ref, vo_ref, o_ref, do_ref, lse_ref, meta_ref, cos_ref, sin_ref,
    *refs,
):
    pair = pl.program_id(0)
    dq_ref, dkb_ref, dvb_ref, dko_ref, dvo_ref, *bias, diag, dk_sum, dv_sum = refs
    pl.when(pair == 0)(lambda: mask_back(rows, meta_ref, bias, diag))
    pair_back(
        rows, score_scale, pair, slice(None), lambda slot: None, q_ref, kb_ref, vb_ref, ko_ref, vo_ref, o_ref,
        do_ref, lse_ref, cos_ref, sin_ref, dq_ref, dkb_ref, dvb_ref, dko_ref, dvo_ref, bias, diag, dk_sum,
        dv_sum,
    )


def back_scratch(rows):
    return [pltpu.VMEM(((i + 1) * TILE, TILE), jnp.float32) for i in range(rows // TILE)] + [
        pltpu.VMEM((SUB, rows), jnp.float32),
        pltpu.VMEM((rows, LANES), jnp.float32),
        pltpu.VMEM((rows, LANES), jnp.float32),
    ]


def attend_back(q, kb, vb, ko, vo, o, do, lse, meta, cosine, sine, score_scale):
    rows, width = q.shape
    pairs = width // LANES
    spec = pl.BlockSpec((rows, LANES), lambda j: (0, j))
    whole = lambda a: pl.BlockSpec(a.shape, lambda j: (0, 0))
    return pl.pallas_call(
        functools.partial(attend_back_kernel, rows, score_scale),
        grid=(pairs,),
        in_specs=[spec] * 7 + [whole(lse), whole(meta), whole(cosine), whole(sine)],
        out_specs=[spec] * 5,
        out_shape=[jax.ShapeDtypeStruct((rows, width), jnp.bfloat16)] * 5,
        scratch_shapes=back_scratch(rows),
        compiler_params=pltpu.CompilerParams(vmem_limit_bytes=48 * MIB),
        cost_estimate=pl.CostEstimate(
            flops=5 * 2 * rows * rows * width, bytes_accessed=24 * rows * width, transcendentals=0
        ),
        name="attend_back",
    )(q, kb, vb, ko, vo, o, do, lse, meta, cosine, sine)


F1, OUT, F2, P0, P1, P2, N = range(7)
TAIL_STREAMS = (
    ("lyxh", 1024), ("xylh", 384), ("yxlh", 1024), ("xylh", 384), ("xylh", 384), ("ylhx", 384), ("lyhx", 128),
)
TAIL_FAR = 3
FEEDS = (F1, F2)
TAIL_TICKS = {
    (0, 3): [(F2, 0)],
    (1, 1): [(OUT, 0)],
    (1, 2): [(F1, 0)],
    (2, 2): [(OUT, 1), (P0, 0)],
    (3, 3): [(F2, 1)],
    (3, 5): [(OUT, 2), (P0, 1)],
    (4, 1): [(F1, 1)],
    (4, 2): [(P1, 0)],
    (4, 3): [(OUT, 3)],
    (5, 1): [(P0, 2), (F2, 2)],
    (5, 3): [(OUT, 4)],
    (5, 5): [(P0, 3), (P1, 1), (F1, 2)],
}
TAIL_POST = {
    0: [(F2, 3)],
    1: [(P2, 0)],
    2: [(P0, 4)],
    3: [(P1, 2)],
    4: [(F1, 3)],
    5: [(F2, 4), (N, 0), (P1, 3)],
    6: [(P2, 1), (N, 1), (F1, 4), (P1, 4), (N, 2), (P2, 2)],
    7: [(N, 3), (P2, 3), (N, 4)],
    8: [(P2, 4)],
}


def normalized(x):
    x = x.astype(jnp.float32)
    centre = x - jnp.mean(x, axis=-1, keepdims=True)
    inverse = lax.rsqrt(jnp.mean(centre * centre, axis=-1, keepdims=True) + epsilon)
    return centre * inverse, inverse


def normal_back(grad, gain, n, inverse):
    e = grad * gain
    return inverse * (
        e - jnp.mean(e, axis=-1, keepdims=True) - n * jnp.mean(e * n, axis=-1, keepdims=True)
    )


def tail_kernel(
    rows, score_scale, q_ref, kb_ref, vb_ref, ko_ref, vo_ref, o_ref, do_ref, lse_ref, meta_ref, cos_ref, sin_ref,
    h1t_ref, h1bt_ref, vectors_ref, norm_ref, first_ref, *refs,
):
    pair = pl.program_id(0)
    hbm, refs = refs[:6], refs[6:]
    ff_ref, go_ref, refs = refs[0], refs[1], refs[2:]
    out_ref, up_out, down_out, head_out, norm_out, refs = *refs[:5], refs[5:]
    scratch, refs = refs[:7], refs[7:]
    bias, (diag, dk_sum, dv_sum) = scratch[:4], scratch[4:]
    dq, dkb, dvb, dko, dvo, refs = *refs[:5], refs[5:]
    held, refs = refs[:5], refs[5:]
    wq, wk, wv, x, base = held
    coming, pair_sums, norm_sums, refs = refs[0], refs[1:4], refs[4], refs[5:]
    load_sem, send_sem, recv_sem, refs = refs[0], refs[1], refs[2], refs[3:]
    sources = [(ff_ref.at[1], 0), (go_ref, 0), (ff_ref.at[2], 0)]
    sources += [(ref, 0) for ref in (*pair_sums, norm_sums)]
    scatter = Scatter(TAIL_STREAMS, sources, refs, TAIL_FAR)
    stream = lax.axis_index("stream")
    tiles = rows // TILE
    width = x.shape[1]
    loads = [
        pltpu.make_async_copy(src, dst, load_sem.at[i])
        for i, (src, dst) in enumerate(zip(hbm, (*held, out_ref)))
    ]

    def tick(slot):
        for at, moves in TAIL_TICKS.items():
            if at[1] == slot:
                @pl.when(pair == at[0])
                def _(moves=moves):
                    for number, index in moves:
                        scatter.step(number, index)

    def post(slot):
        for number, index in TAIL_POST.get(slot, ()):
            scatter.step(number, index)

    @pl.when(pair == 0)
    def _():
        scatter.greet()
        scatter.open((F2, OUT, F1))
        for load in loads:
            load.start()
        mask_back(rows, meta_ref, bias, diag)

    cols = pl.ds(pl.multiple_of(pair * LANES, LANES), LANES)
    pair_back(
        rows, score_scale, pair, cols, tick, q_ref, kb_ref, vb_ref, ko_ref, vo_ref, o_ref,
        do_ref, lse_ref, cos_ref, sin_ref, dq, dkb, dvb, dko, dvo, bias, diag, dk_sum, dv_sum,
    )

    for number, sums in enumerate(pair_sums):
        @pl.when(pair == 2 * number + 1)
        def _(number=number, sums=sums):
            both = slice(2 * number * LANES, (2 * number + 2) * LANES)
            for at, block in enumerate((
                nn(h1t_ref[...], dq[:, both]),
                nn(h1t_ref[...], dko[:, both]) + nn(h1bt_ref[...], dkb[:, both]),
                nn(h1t_ref[...], dvo[:, both]) + nn(h1bt_ref[...], dvb[:, both]),
            )):
                block = block.astype(jnp.bfloat16)
                for half in range(2):
                    sums[half, :, :, :, :, :, at * LANES : (at + 1) * LANES] = block[
                        :, half * LANES : (half + 1) * LANES
                    ].reshape(2, 2, 2, 2, RUN, LANES)
            scatter.open((P0 + number,))

    tick(tiles + 1)

    @pl.when(pair == pl.num_programs(0) - 1)
    def _():
        for load in loads:
            load.wait()
        gain = vectors_ref[0:1, :]

        def band(r):
            return slice(r * TILE, (r + 1) * TILE)

        def move(r):
            return pltpu.make_async_remote_copy(
                src_ref=dkb.at[band(r)],
                dst_ref=coming.at[band(r)],
                send_sem=send_sem.at[r],
                recv_sem=recv_sem.at[r],
                device_id=scatter.to["x"],
                device_id_type=MESH,
            )

        gain_sum = jnp.zeros((1, width), jnp.float32)
        bias_sum = jnp.zeros((1, width), jnp.float32)
        for r in range(tiles):
            at = band(r)
            grad = nt(dkb[at, :], wk[...]) + nt(dvb[at, :], wv[...])
            dkb[at, :] = grad.astype(jnp.bfloat16)
            pl.when(stream == 1)(lambda r=r: move(r).start())
            n, _ = normalized(base[at, :])
            gain_sum += jnp.sum(grad * n, axis=0, keepdims=True)
            bias_sum += jnp.sum(grad, axis=0, keepdims=True)
        post(0)
        for r in range(tiles):
            at = band(r)
            grad = nt(dq[at, :], wq[...]) + nt(dko[at, :], wk[...]) + nt(dvo[at, :], wv[...])
            n, inverse = normalized(x[at, :])
            gain_sum += jnp.sum(grad * n, axis=0, keepdims=True)
            bias_sum += jnp.sum(grad, axis=0, keepdims=True)
            grad = grad + jnp.where(stream == 0, dkb[at, :].astype(jnp.float32), 0.0)
            out_ref[at, :] += normal_back(grad, gain, n, inverse)
            post(r + 1)
        eye = jnp.where(
            lax.broadcasted_iota(jnp.int32, (8, LANES), 0)
            == lax.broadcasted_iota(jnp.int32, (8, LANES), 1),
            1.0,
            0.0,
        ).astype(jnp.bfloat16)
        zero = jnp.zeros((6, width), jnp.float32)
        for half, sums in enumerate((
            jnp.concatenate([gain_sum, bias_sum, zero], axis=0), norm_ref[...]
        )):
            block = tn(sums.astype(jnp.bfloat16), eye).astype(jnp.bfloat16)
            norm_sums[half] = block.reshape(2, 2, 2, 2, RUN, LANES)
        scatter.open((N,))
        post(tiles + 1)
        for r in range(tiles):
            at = band(r)

            @pl.when(stream == 1)
            def _(r=r):
                move(r).wait_send()

            @pl.when(stream == 0)
            def _(r=r, at=at):
                move(r).wait_recv()
                n, inverse = normalized(x[at, :])
                out_ref[at, :] += normal_back(coming[at, :].astype(jnp.float32), gain, n, inverse)

            post(tiles + 2 + r)
        scatter.finish()
        places = [sum(part for _, part in TAIL_STREAMS[:i]) for i in range(len(TAIL_STREAMS))]
        for half, out in enumerate((up_out, down_out)):
            out[:, : first_ref.shape[2]] = first_ref[half]
            low = first_ref.shape[2]
            for number in FEEDS:
                part = TAIL_STREAMS[number][1]
                out[:, low : low + part] = scatter.result(half, places[number], part)
                low += part
        middle = width // 2
        for half in range(2):
            head_out[0, :, half * middle : (half + 1) * middle] = scatter.result(
                half, places[OUT], middle
            )
            norm_out[half] = scatter.result(half, places[N], LANES)
            for number in range(len(pair_sums)):
                low = (2 * number + half) * LANES
                for at in range(3):
                    head_out[1 + at, :, low : low + LANES] = scatter.result(
                        half, places[P0 + number] + at * LANES, LANES
                    )


def tail(
    operands, h1t, h1bt, vectors, norm, first, weights, x, base, middle_grad, ff, go, score_scale
):
    rows, width = x.shape
    pairs = width // LANES
    hidden = first.shape[2] + sum(TAIL_STREAMS[number][1] for number in FEEDS)
    shapes = [(rows, width), (24, hidden), (24, hidden), (4, 24, width), (2, 24, LANES)]
    spec = pl.BlockSpec((rows, LANES), lambda j: (0, j))
    once = pl.Buffered(1)
    whole = lambda shape: pl.BlockSpec(shape, lambda j: (0,) * len(shape), pipeline_mode=once)
    flat, square = (rows, width), (width, width)
    low = jnp.bfloat16
    scratch = back_scratch(rows)
    scratch += [pltpu.VMEM(flat, low)] * 5
    scratch += [pltpu.VMEM(square, low)] * 3 + [pltpu.VMEM(flat, low)] * 2
    scratch += [pltpu.VMEM(flat, low)]
    scratch += [pltpu.VMEM((2, 2, 2, 2, 2, RUN, 3 * LANES), low)] * 3
    scratch += [pltpu.VMEM((2, 2, 2, 2, 2, RUN, LANES), low)]
    scratch += [pltpu.SemaphoreType.DMA((6,))]
    scratch += [pltpu.SemaphoreType.DMA((rows // TILE,))] * 2
    scratch += Scatter.shapes(TAIL_STREAMS, TAIL_FAR)
    return pl.pallas_call(
        functools.partial(tail_kernel, rows, score_scale),
        grid=(pairs,),
        in_specs=[spec] * 7
        + [whole(a.shape) for a in (*operands[7:], h1t, h1bt, vectors, norm, first)]
        + [pl.BlockSpec(memory_space=pl.ANY)] * 8,
        out_specs=[whole(shape) for shape in shapes],
        out_shape=[jax.ShapeDtypeStruct(shape, jnp.float32) for shape in shapes],
        scratch_shapes=scratch,
        compiler_params=pltpu.CompilerParams(
            collective_id=0, has_side_effects=True, vmem_limit_bytes=63 * MIB
        ),
        cost_estimate=pl.CostEstimate(
            flops=10 * rows * rows * width + 20 * rows * width * width,
            bytes_accessed=40 * MIB,
            transcendentals=0,
        ),
        name="tail",
    )(*operands, h1t, h1bt, vectors, norm, first, *weights, x, base, middle_grad, ff, go)


FEED_TILE = 1024
FEED_STREAMS = (("yxlh", 512), ("xylh", 512))
FEED_TICKS = {
    (1, 1): [(0, 0), (1, 0)], (1, 5): [(0, 1), (1, 1)], (2, 1): [(0, 2), (1, 2)], (2,5): [(0, 3), (1, 3)], (2,6): [(0, 4), (1, 4)],
}


def feed_kernel(
    streams, x_ref, o_ref, dy_ref, wo_ref, vectors_ref, wu_ref, wd_ref,
    y_ref, do_ref, dx_ref, norm_ref, ff_ref, go_ref, *refs,
):
    f = pl.program_id(0)
    rows, width = x_ref.shape
    scatter = None
    if streams:
        out_ref, refs = refs[0], refs[1:]
    total, normal, scale, h2s, h2t, dyt, gs, dus = refs[:8]
    if streams:
        first = refs[8]
        sources, low = [], 0
        for _, part in streams:
            sources.append((first, low))
            low += part
        scatter = Scatter(streams, sources, refs[9:], 0)

    def tick(slot):
        if scatter is None:
            return
        for at, moves in FEED_TICKS.items():
            if at[1] == slot:
                @pl.when(f == at[0])
                def _(moves=moves):
                    for stream, index in moves:
                        scatter.step(stream, index)

    def band(r):
        return pl.ds(pl.multiple_of(r * TILE, TILE), TILE)

    @pl.when(f == 0)
    def _():
        if scatter is not None:
            scatter.greet()
        norm_ref[...] = jnp.zeros_like(norm_ref)

        @pl.loop(0, rows // TILE)
        def _(r):
            at = band(r)
            x1 = x_ref[at, :].astype(jnp.float32) + nn(o_ref[at, :], wo_ref[...])
            centre = x1 - jnp.mean(x1, axis=-1, keepdims=True)
            inverse = lax.rsqrt(jnp.mean(centre * centre, axis=-1, keepdims=True) + epsilon)
            n = centre * inverse
            h2 = (n * vectors_ref[2:3, :] + vectors_ref[3:4, :]).astype(jnp.bfloat16)
            total[at, :] = x1
            normal[at, :] = n
            scale[at, :] = jnp.broadcast_to(inverse, (TILE, LANES))
            h2s[at, :] = h2
            h2t[:, at] = jnp.transpose(h2)
            dyt[:, at] = jnp.transpose(dy_ref[at, :])
            dx_ref[at, :] = jnp.zeros((TILE, width), jnp.float32)

    for r in range(rows // TILE):
        at = band(r)
        u = nn(h2s[at, :], wu_ref[...])
        square = u * u
        curve = jnp.tanh(0.7978845608028654 * u * (1.0 + 0.044715 * square))
        upper = 0.5 * (1.0 + curve)
        g = (u * upper).astype(jnp.bfloat16)
        slope = upper + u * upper * (1.0 - curve) * (
            0.7978845608028654 + 3 * 0.044715 * 0.7978845608028654 * square
        )
        gs[at, :] = g
        total[at, :] += nn(g, wd_ref[...])
        du = (nt(dy_ref[at, :], wd_ref[...]) * slope).astype(jnp.bfloat16)
        dus[at, :] = du
        dx_ref[at, :] += nt(du, wu_ref[...])
        tick(r)
    slot = rows // TILE
    for half, (left, right) in enumerate(((h2t, dus), (dyt, gs))):
        for c in range(right.shape[1] // TILE):
            cols = pl.ds(c * TILE, TILE)
            block = nn(left[...], right[:, cols]).astype(jnp.bfloat16)
            block = block.reshape(2, 2, 2, 2, RUN, TILE)
            ff_ref[0, half, :, :, :, :, :, cols] = block
        tick(slot + half)
    if scatter is not None:
        @pl.when(f == 0)
        def _():
            @pl.loop(0, 32)
            def _(i):
                at = (i // 16, i // 8 % 2, i // 4 % 2, i // 2 % 2, i % 2)
                first[at] = ff_ref[(0,) + at]

            scatter.open(range(len(streams)))

    @pl.when(f == pl.num_programs(0) - 1)
    def _():
        @pl.loop(0, rows // TILE)
        def _(r):
            at = band(r)
            y_ref[at, :] = total[at, :].astype(jnp.bfloat16)
            n = normal[at, :]
            dh2 = dx_ref[at, :]
            norm_ref[0:1, :] += jnp.sum(dh2 * n, axis=0, keepdims=True)
            norm_ref[1:2, :] += jnp.sum(dh2, axis=0, keepdims=True)
            e = dh2 * vectors_ref[2:3, :]
            e = (
                e
                - jnp.mean(e, axis=-1, keepdims=True)
                - n * jnp.mean(e * n, axis=-1, keepdims=True)
            )
            dx = dy_ref[at, :].astype(jnp.float32) + scale[at, 0:1] * e
            dx_ref[at, :] = dx
            da = dx.astype(jnp.bfloat16)
            dyt[:, at] = jnp.transpose(da)
            do_ref[at, :] = nt(da, wo_ref[...]).astype(jnp.bfloat16)

        middle = width // 2
        for half in range(2):
            block = nn(dyt[...], o_ref[:, half * middle : (half + 1) * middle])
            go_ref[half] = block.astype(jnp.bfloat16).reshape(2, 2, 2, 2, RUN, middle)
        tick(slot + 2)
        if scatter is not None:
            scatter.finish()
            for half in range(2):
                out_ref[half] = scatter.result(half, 0, out_ref.shape[2])


def feed(x, o, dy, wo, vectors, wu, wd, streams):
    rows, width = x.shape
    tiles = wu.shape[1] // FEED_TILE
    once = pl.Buffered(1)
    whole = lambda shape: pl.BlockSpec(shape, lambda f: (0,) * len(shape), pipeline_mode=once)
    flat, square = (rows, width), (width, width)
    parts = (2, 2, 2, 2, RUN)
    out_specs = [
        whole(flat),
        whole(flat),
        whole(flat),
        whole((8, width)),
        pl.BlockSpec((1, 2) + parts + (FEED_TILE,), lambda f: (f,) + (0,) * 7),
        whole((2,) + parts + (width // 2,)),
    ]
    out_shape = [
        jax.ShapeDtypeStruct(flat, jnp.bfloat16),
        jax.ShapeDtypeStruct(flat, jnp.bfloat16),
        jax.ShapeDtypeStruct(flat, jnp.float32),
        jax.ShapeDtypeStruct((8, width), jnp.float32),
        jax.ShapeDtypeStruct((tiles, 2) + parts + (FEED_TILE,), jnp.bfloat16),
        jax.ShapeDtypeStruct((2,) + parts + (width // 2,), jnp.bfloat16),
    ]
    scratch = [
        pltpu.VMEM(flat, jnp.float32),
        pltpu.VMEM(flat, jnp.float32),
        pltpu.VMEM((rows, LANES), jnp.float32),
        pltpu.VMEM(flat, jnp.bfloat16),
        pltpu.VMEM((width, rows), jnp.bfloat16),
        pltpu.VMEM((width, rows), jnp.bfloat16),
        pltpu.VMEM((rows, FEED_TILE), jnp.bfloat16),
        pltpu.VMEM((rows, FEED_TILE), jnp.bfloat16),
    ]
    options = {}
    if streams:
        out_specs += [whole((2, 24, FEED_TILE))]
        out_shape += [jax.ShapeDtypeStruct((2, 24, FEED_TILE), jnp.float32)]
        scratch += [pltpu.VMEM((2,) + parts + (FEED_TILE,), jnp.bfloat16)]
        scratch += Scatter.shapes(streams, 0)
        options = {"collective_id": 2, "has_side_effects": True}
    return pl.pallas_call(
        functools.partial(feed_kernel, streams),
        grid=(tiles,),
        in_specs=[
            whole(flat),
            whole(flat),
            whole(flat),
            whole(square),
            whole(vectors.shape),
            pl.BlockSpec((width, FEED_TILE), lambda f: (0, f)),
            pl.BlockSpec((FEED_TILE, width), lambda f: (f, 0)),
        ],
        out_specs=out_specs,
        out_shape=out_shape,
        scratch_shapes=scratch,
        compiler_params=pltpu.CompilerParams(vmem_limit_bytes=62 * MIB, **options),
        cost_estimate=pl.CostEstimate(
            flops=12 * rows * width * wu.shape[1] + 6 * rows * width * width,
            bytes_accessed=30 * MIB,
            transcendentals=0,
        ),
        name="feed",
    )(x, o, dy, wo, vectors, wu, wd)


def shards(
    tokens,
    lengths,
    pad_mask,
    first_gain,
    first_bias,
    query_weight,
    key_weight,
    value_weight,
    out_weight,
    second_gain,
    second_bias,
    up_weight,
    down_weight,
    output_grad,
):
    total_rows = tokens.shape[1]
    model_width = tokens.shape[2]
    head_width = model_width // H
    score_scale = head_width ** (-0.5)
    is_noisy = lax.axis_index("stream") == 1
    own = tokens[0]
    places, first_place = layout(lengths[0], total_rows, lengths.shape[1])
    limit = (places // BLOCK + jnp.where(is_noisy, 0, 1)) * BLOCK
    noisy_row = jnp.broadcast_to(jnp.where(is_noisy, 1, 0), places.shape)
    blank = jnp.zeros_like(places)
    meta = jnp.stack(
        [first_place, limit, pad_mask, noisy_row, blank, blank, blank, blank]
    ).astype(jnp.float32)
    cosine, sine = angle_tables(places - first_place, head_width)
    vectors = jnp.stack([first_gain, first_bias, second_gain, second_bias])
    vectors = jnp.concatenate([vectors, jnp.zeros_like(vectors)])
    weights = (query_weight, key_weight, value_weight)
    ring = lax.axis_size("dp") == 16 and lax.axis_size("stream") == 2
    if ring:
        base, h1t, h1bt, q, kb, vb, ko, vo, mixed_low, lse = front(
            own, vectors, cosine, sine, weights, meta, score_scale
        )
    else:
        far = lax.ppermute(own, "stream", [(0, 1)])
        base = jnp.where(is_noisy, far, own)
        h1t, q, ko, vo = project(own, vectors, cosine, sine, weights, score_scale)
        h1bt, kb, vb = project(base, vectors, cosine, sine, weights[1:], score_scale)
        mixed_low, lse = attend(q, kb, vb, ko, vo, meta)

    fed = feed(
        own, mixed_low, output_grad[0], out_weight, vectors, up_weight, down_weight, FEED_STREAMS if ring else (),
    )
    layer_output, mixed_grad, middle_grad, norm_sums, ff_part, out_part = fed[:6]
    layer_output = layer_output[None]
    operands = (q, kb, vb, ko, vo, mixed_low, mixed_grad, lse, meta, cosine, sine)
    if ring:
        tokens_grad, up_grad, down_grad, heads, norms = tail(
            operands, h1t, h1bt, vectors, norm_sums, fed[6], weights, own, base, middle_grad, ff_part,
            out_part, score_scale,
        )
        tokens_grad = tokens_grad[None]
        out_grad, query_grad, key_grad, value_grad = heads
        first_grads, second_grads = norms[0, :, :2].T, norms[1, :, :2].T
    else:
        dq, dkb, dvb, dko, dvo = attend_back(*operands, score_scale)
        base_grad = nt(dkb, key_weight) + nt(dvb, value_weight)
        back = lax.ppermute(base_grad.astype(jnp.bfloat16), "stream", [(1, 0)])
        normed_grad = (
            nt(dq, query_weight)
            + nt(dko, key_weight)
            + nt(dvo, value_weight)
            + jnp.where(is_noisy, 0.0, base_grad + back.astype(jnp.float32))
        )
        inputs = own.astype(jnp.float32)
        first_pull = jax.vjp(layer_norm, inputs, first_gain, first_bias)[1]
        input_part, first_gain_part, first_bias_part = first_pull(normed_grad)
        tokens_grad = (middle_grad + input_part)[None]
        ff_part = ff_part.reshape(-1, 2, model_width, FEED_TILE)
        out_part = out_part.reshape(2, model_width, model_width // 2)
        norm_part = jnp.stack(
            [first_gain_part, first_bias_part, norm_sums[0], norm_sums[1]], axis=1
        )
        part = jnp.concatenate(
            [ff_part[f, i] for i in range(2) for f in range(ff_part.shape[0])]
            + [out_part[0], out_part[1], nn(h1t, dq).astype(jnp.bfloat16)]
            + [(nn(h1t, dko) + nn(h1bt, dkb)).astype(jnp.bfloat16)]
            + [(nn(h1t, dvo) + nn(h1bt, dvb)).astype(jnp.bfloat16)]
            + [jnp.pad(norm_part, ((0, 0), (0, LANES - 4))).astype(jnp.bfloat16)],
            axis=1,
        )
        part = lax.psum_scatter(part, ("stream", "dp"), scatter_dimension=0, tiled=True)
        part = part.astype(jnp.float32)
        hidden_width = up_weight.shape[1]
        cuts = (hidden_width, hidden_width) + (model_width,) * 4 + (LANES,)
        pieces, low = [], 0
        for cut in cuts:
            pieces.append(part[:, low : low + cut])
            low += cut
        up_grad, down_grad, out_grad, query_grad, key_grad, value_grad, norms = pieces
        first_grads, second_grads = norms[:, :2].T, norms[:, 2:4].T
    return (
        layer_output,
        tokens_grad,
        first_grads,
        query_grad,
        key_grad,
        value_grad,
        out_grad.T,
        second_grads,
        up_grad,
        down_grad.T,
    )


def solution(mesh):
    placed = (
        P("stream", "dp", None),
        P("dp", None),
        P("dp"),
        P(),
        P(),
        P(),
        P(),
        P(),
        P(),
        P(),
        P(),
        P(),
        P(),
        P("stream", "dp", None),
    )
    return jax.shard_map(
        shards,
        mesh=mesh,
        in_specs=placed,
        out_specs=(
            P("stream", "dp", None),
            P("stream", "dp", None),
            P(None, ("stream", "dp")),
            P(("stream", "dp"), None),
            P(("stream", "dp"), None),
            P(("stream", "dp"), None),
            P(None, ("stream", "dp")),
            P(None, ("stream", "dp")),
            P(("stream", "dp"), None),
            P(None, ("stream", "dp")),
        ),
        check_vma=False,
    )
```

```python
import functools
import math

import jax
import jax.numpy as jnp
from jax import lax
from jax.experimental import pallas as pl
from jax.experimental.pallas import tpu as pltpu
from jax.sharding import PartitionSpec as P

H = 12
BLOCK = 16
TILE = 256
SUB = 128
LANES = 128

epsilon = 1e-05
masked_score = -1e30
MIB = 1024 * 1024


def layer_norm(values, gain_row, bias_row):
    centre = values - jnp.mean(values, axis=-1, keepdims=True)
    spread = jnp.mean(centre * centre, axis=-1, keepdims=True)
    return centre * lax.rsqrt(spread + epsilon) * gain_row + bias_row


def layout(lengths_row, total_rows, doc_slots):
    places = jnp.arange(total_rows, dtype=jnp.int32)
    end_places = jnp.cumsum(lengths_row)
    starts = end_places - lengths_row
    document = jnp.sum((places[:, None] >= end_places[None, :]).astype(jnp.int32), axis=1)
    picked = document[:, None] == jnp.arange(doc_slots, dtype=jnp.int32)[None, :]
    first_place = jnp.sum(jnp.where(picked, starts[None, :], 0), axis=1)
    return (places, first_place)


def angle_tables(position, head_width):
    half_width = head_width // 2
    freq_index = (jnp.arange(half_width)).astype(jnp.float32)
    frequency = jnp.exp(freq_index * (-2.0 * math.log(10000.0) / head_width))
    turned = position.astype(jnp.float32)[:, None] * frequency[None, :]
    cosine, sine = jnp.cos(turned), jnp.sin(turned)
    return (
        jnp.concatenate([cosine] * 4, axis=1),
        jnp.concatenate([-sine, sine, -sine, sine], axis=1),
    )


def turn(values, cosine, sine):
    lane = lax.broadcasted_iota(jnp.int32, values.shape, 1)
    low = lax.rem(lane, 64) < 32
    partner = jnp.where(low, pltpu.roll(values, LANES - 32, 1), pltpu.roll(values, 32, 1))
    return values * cosine + partner * sine


def nt(left, right):
    return lax.dot_general(
        left, right, (((1,), (1,)), ((), ())), preferred_element_type=jnp.float32
    )


def tn(left, right):
    return lax.dot_general(
        left, right, (((0,), (0,)), ((), ())), preferred_element_type=jnp.float32
    )


def nn(left, right):
    return jnp.dot(left, right, preferred_element_type=jnp.float32)


MESH = pl.DeviceIdType.MESH
RUN = 48


class Scatter:
    @staticmethod
    def shapes(streams, far):
        total = sum(width for _, width in streams)
        shapes = [
            pltpu.VMEM((2, 2, 2, 2, RUN, total), jnp.bfloat16),
            pltpu.VMEM((2, 24, total), jnp.float32),
            pltpu.VMEM((24, total), jnp.float32),
        ]
        for number, (order, width) in enumerate(streams):
            if number < far:
                shapes += [pltpu.VMEM((2, 2, 2, 2, RUN, width), jnp.bfloat16)]
            for left in range(len(order) - 1, -1, -1):
                shapes += [pltpu.VMEM((2,) * left + (RUN, width), jnp.bfloat16)]
        count = sum(1 + len(order) for order, _ in streams) + 1
        return shapes + [
            pltpu.SemaphoreType.DMA((count,)),
            pltpu.SemaphoreType.DMA((count,)),
            pltpu.SemaphoreType.DMA((len(streams),)),
        ]

    def __init__(self, streams, sources, refs, far):
        self.far = far
        self.sib, self.fin, self.other = refs[:3]
        self.bufs = list(refs[3:-3])
        self.send, self.recv, self.local = refs[-3:]
        s, d = lax.axis_index("stream"), lax.axis_index("dp")
        self.core = d % 2
        self.mine = {"x": s, "y": d // 2 % 2, "l": d // 4 % 2, "h": d // 8}
        self.to = {
            "x": {"stream": 1 - s},
            "y": {"dp": d + 2 - 4 * self.mine["y"]},
            "l": {"dp": d + 4 - 8 * self.mine["l"]},
            "h": {"dp": d + 8 - 16 * self.mine["h"]},
            "core": {"dp": d + 1 - 2 * self.core},
        }
        self.used = 0
        self.streams = []
        place = 0
        for (order, width), (source, low) in zip(streams, sources):
            self.streams.append(self.stream(order, place, width, source, low))
            place += width
        self.last = self.take()

    def take(self):
        self.used += 1
        return self.used - 1

    def copy(self, src, dst, k, to):
        return pltpu.make_async_remote_copy(
            src_ref=src,
            dst_ref=dst,
            send_sem=self.send.at[k],
            recv_sem=self.recv.at[k],
            device_id=self.to[to],
            device_id_type=MESH,
        )

    def greet(self):
        barrier = pltpu.get_barrier_semaphore()
        for to in self.to.values():
            pl.semaphore_signal(barrier, inc=1, device_id=to, device_id_type=MESH)
        pl.semaphore_wait(barrier, len(self.to))

    @staticmethod
    def add(dst, left, right):
        lead = dst.shape[:-2]
        count = math.prod(lead)

        def one(index):
            at = []
            for size in reversed(lead):
                at.append(index % size)
                index = index // size
            at = tuple(reversed(at))
            dst[at] = left[at] + right[at]

        if count == 1:
            one(0)
        else:
            pl.loop(0, count, unroll=min(count, 4))(one)

    def stream(self, order, place, width, source, low):
        number = len(self.streams)
        cols = pl.ds(place, width)
        every = (slice(None),) * 5
        src = self.sib.at[every + (cols,)]
        k = self.take()
        part = lambda core: source.at[(core,) + every + (pl.ds(low, width),)]
        swap = lambda src=src, k=k: self.copy(part(1 - self.core), src, k, "core")
        near = None
        if number < self.far:
            held = self.bufs.pop(0)
            near = lambda: pltpu.make_async_copy(part(self.core), held, self.local.at[number])

        def opening(src=src):
            swap().wait()
            if near is None:
                self.add(src, src, part(self.core))
            else:
                near().wait()
                self.add(src, src, held)

        steps = []
        pending = opening
        names = ["x", "h", "l", "y"]
        for axis in order:
            at = names.index(axis)
            names.pop(at)
            buf = self.bufs.pop(0)
            k = self.take()
            pick = lambda index, src=src, at=at: src.at[(slice(None),) * at + (index,)]
            make = lambda pick=pick, buf=buf, k=k, axis=axis: self.copy(
                pick(1 - self.mine[axis]), buf, k, axis
            )

            def begin(before=pending, make=make):
                before()
                make().start()

            def end(pick=pick, buf=buf, make=make, axis=axis):
                make().wait()
                self.add(buf, buf, pick(self.mine[axis]))

            steps.append(begin)
            pending = end
            src = buf

        def close(before=pending, src=src):
            before()
            for core in range(2):
                self.fin[core, :, cols] = src[24 * core : 24 * core + 24, :].astype(jnp.float32)

        steps.append(close)
        return (swap, near, steps)

    def open(self, order):
        for index in order:
            swap, near, _ = self.streams[index]
            swap().start()
            if near is not None:
                near().start()

    def step(self, stream, index):
        self.streams[stream][2][index]()

    def finish(self):
        last = self.copy(self.fin.at[1 - self.core], self.other, self.last, "core")
        last.start()
        last.wait()

    def result(self, half, place, width):
        cols = slice(place, place + width)
        return jnp.where(self.core == half, self.fin[half, :, cols], self.other[:, cols])


def project_kernel(score_scale, x_ref, gain_ref, shift_ref, cos_ref, sin_ref, *refs):
    count = (len(refs) - 1) // 2
    weights, outs = refs[:count], refs[count:]
    gain, shift = (ref[...].reshape(1, x_ref.shape[1]) for ref in (gain_ref, shift_ref))
    h1 = layer_norm(x_ref[...].astype(jnp.float32), gain, shift).astype(jnp.bfloat16)
    outs[0][...] = jnp.transpose(h1)
    cosine, sine = cos_ref[...], sin_ref[...]
    for index, (weight, out) in enumerate(zip(weights, outs[1:])):
        product = nn(h1, weight[...])
        is_value = index == count - 1
        is_query = count == 3 and index == 0
        if is_value:
            out[...] = product.astype(jnp.bfloat16)
            continue
        for pair in range(product.shape[1] // LANES):
            columns = slice(pair * LANES, (pair + 1) * LANES)
            turned = turn(product[:, columns], cosine, sine)
            if is_query:
                turned = turned * score_scale
            out[:, columns] = turned.astype(jnp.bfloat16)


def project(x, gain, shift, cosine, sine, weights, score_scale):
    rows, width = x.shape
    count = len(weights)
    row_spec = pl.BlockSpec((TILE, width), lambda i: (i, 0))
    table_spec = pl.BlockSpec((TILE, LANES), lambda i: (i, 0))
    whole = pl.BlockSpec((width, width), lambda i: (0, 0))
    line = pl.BlockSpec(gain.shape, lambda i: (0,))
    return pl.pallas_call(
        functools.partial(project_kernel, score_scale),
        grid=(rows // TILE,),
        in_specs=[row_spec, line, line, table_spec, table_spec] + [whole] * count,
        out_specs=[pl.BlockSpec((width, TILE), lambda i: (0, i))] + [row_spec] * count,
        out_shape=[jax.ShapeDtypeStruct((width, rows), jnp.bfloat16)]
        + [jax.ShapeDtypeStruct((rows, width), jnp.bfloat16)] * count,
        compiler_params=pltpu.CompilerParams(vmem_limit_bytes=40 * MIB),
        cost_estimate=pl.CostEstimate(
            flops=2 * rows * width * width * count,
            bytes_accessed=2 * (rows + count * (width + rows)) * width,
            transcendentals=0,
        ),
        name="project%d" % count,
    )(x, gain, shift, cosine, sine, *weights)


def two_heads(block):
    lane = lax.broadcasted_iota(jnp.int32, block.shape, 1)
    zero = jnp.zeros_like(block)
    return jnp.concatenate(
        [jnp.where(lane < 64, block, zero), jnp.where(lane < 64, zero, block)], axis=0
    )


def one_row(both):
    rows = both.shape[0] // 2
    lane = lax.broadcasted_iota(jnp.int32, (rows, LANES), 1)
    return jnp.where(lane < 64, both[:rows], both[rows:])


def subs(both, sub):
    low = sub * SUB
    return jnp.concatenate([both[low : low + SUB], both[TILE + low : TILE + low + SUB]], axis=0)


def mask_front(rows, meta_ref, bias, diag):
    columns = jnp.transpose(meta_ref[...])
    noisy = columns[:, 3:4]
    for i in range(rows // TILE):
        band = slice(i * TILE, (i + 1) * TILE)
        n = (i + 1) * TILE
        start, limit = columns[band, 0:1], columns[band, 1:2]
        key = lax.broadcasted_iota(jnp.int32, (TILE, n), 1)
        query = lax.broadcasted_iota(jnp.int32, (TILE, n), 0) + i * TILE
        usable = (meta_ref[2:3, :n] == 1.0) | (key == query)
        place = key.astype(jnp.float32)
        seen = (place >= start) & (place < limit) & usable
        bias[i][...] = jnp.where(seen, 0.0, masked_score)
        for sub in range(TILE // SUB):
            low = i * TILE + sub * SUB
            key = lax.broadcasted_iota(jnp.int32, (SUB, SUB), 1) + low
            query = lax.broadcasted_iota(jnp.int32, (SUB, SUB), 0) + low
            usable = (meta_ref[2:3, low : low + SUB] == 1.0) | (key == query)
            same = (key // BLOCK == query // BLOCK) & (
                key.astype(jnp.float32) >= columns[low : low + SUB, 0:1]
            )
            seen = same & usable & (noisy[low : low + SUB] == 1.0)
            diag[low : low + SUB, :] = jnp.where(seen, 0.0, masked_score)


def tile_front(i, pair, cols, q_ref, kb_ref, vb_ref, ko_ref, vo_ref, o_ref, bias, diag, lse):
    band = slice(i * TILE, (i + 1) * TILE)
    n = (i + 1) * TILE
    lane = lax.broadcasted_iota(jnp.int32, (TILE, LANES), 1)
    q2 = two_heads(q_ref[band, cols])
    b = bias[i][...]
    s = nt(q2, kb_ref[:n, cols]) + jnp.concatenate([b, b], axis=0)
    d = diag[band, :]

    def apart(sub):
        return slice(i * TILE + sub * SUB, i * TILE + (sub + 1) * SUB)

    def merge(parts):
        return jnp.concatenate(
            [parts[0][:SUB], parts[1][:SUB], parts[0][SUB:], parts[1][SUB:]], axis=0
        )

    parts = [nt(subs(q2, sub), ko_ref[apart(sub), cols]) for sub in range(TILE // SUB)]
    sd = merge(parts) + jnp.concatenate([d, d], axis=0)
    top = jnp.maximum(jnp.max(s, axis=1, keepdims=True), jnp.max(sd, axis=1, keepdims=True))
    p = jnp.exp(s - top)
    pd = jnp.exp(sd - top)
    total = jnp.sum(p, axis=1, keepdims=True) + jnp.sum(pd, axis=1, keepdims=True)
    pd_low = pd.astype(jnp.bfloat16)
    o = nn(p.astype(jnp.bfloat16), vb_ref[:n, cols])
    parts = [nn(subs(pd_low, sub), vo_ref[apart(sub), cols]) for sub in range(TILE // SUB)]
    o = (o + merge(parts)) * (1.0 / total)
    o_ref[band, cols] = one_row(o).astype(o_ref.dtype)
    level = top + jnp.log(total)
    old = lse[band, :]
    lse[band, :] = jnp.where(
        lane == 2 * pair, level[:TILE], jnp.where(lane == 2 * pair + 1, level[TILE:], old)
    )


def attend_kernel(rows, q_ref, kb_ref, vb_ref, ko_ref, vo_ref, meta_ref, o_ref, lse_ref, *refs):
    bias, diag, lse = refs[:-2], refs[-2], refs[-1]
    pair = pl.program_id(0)
    pl.when(pair == 0)(lambda: mask_front(rows, meta_ref, bias, diag))
    for i in range(rows // TILE):
        tile_front(
            i, pair, slice(None), q_ref, kb_ref, vb_ref, ko_ref, vo_ref, o_ref, bias, diag, lse
        )

    @pl.when(pair == pl.num_programs(0) - 1)
    def _():
        lse_ref[...] = jnp.transpose(lse[...])[: lse_ref.shape[0], :]


def front_scratch(rows):
    return [pltpu.VMEM((TILE, (i + 1) * TILE), jnp.float32) for i in range(rows // TILE)] + [
        pltpu.VMEM((rows, SUB), jnp.float32),
        pltpu.VMEM((rows, LANES), jnp.float32),
    ]


def front_kernel(
    score_scale, x_ref, gain_ref, shift_ref, lengths_ref, pad_ref, wq_ref, wk_ref, wv_ref,
    base_ref, h1t_ref, h1bt_ref, q_ref, kb_ref, vb_ref, ko_ref, vo_ref, o_ref, lse_ref, meta_ref, cos_ref,
    sin_ref, *refs,
):
    bias, diag, lse = refs[:4], refs[4], refs[5]
    coming, send_sem, recv_sem = refs[6:]
    rows, width = x_ref.shape
    stream = lax.axis_index("stream")
    gain, shift = gain_ref[...].reshape(1, width), shift_ref[...].reshape(1, width)
    partner = {"stream": 1 - stream}

    def move(r):
        return pltpu.make_async_remote_copy(
            src_ref=x_ref.at[r * TILE : (r + 1) * TILE],
            dst_ref=coming.at[r * TILE : (r + 1) * TILE],
            send_sem=send_sem.at[r],
            recv_sem=recv_sem.at[r],
            device_id=partner,
            device_id_type=MESH,
        )

    barrier = pltpu.get_barrier_semaphore()
    pl.semaphore_signal(barrier, inc=1, device_id=partner, device_id_type=MESH)
    pl.semaphore_wait(barrier, 1)
    tiles = rows // TILE

    @pl.when(stream == 0)
    def _():
        for r in range(tiles):
            move(r).start()

    place = lax.broadcasted_iota(jnp.int32, (1, rows), 1)
    end, start = 0, jnp.zeros((1, rows), jnp.int32)
    for slot in range(lengths_ref.shape[1]):
        end = end + lengths_ref[0, slot]
        start = jnp.where(place >= end, end, start)
    limit = (place // BLOCK + 1 - stream) * BLOCK
    lines = [start, limit, pad_ref[...], jnp.zeros_like(place) + stream]
    lines = jnp.concatenate(lines + [jnp.zeros_like(place)] * 4, axis=0).astype(jnp.float32)
    meta_ref[...] = lines
    starts = jnp.transpose(lines)[:, 0:1]
    lane = lax.broadcasted_iota(jnp.int32, (1, LANES), 1)
    index = lax.rem(lane, 32).astype(jnp.float32)
    frequency = jnp.exp(index * (-2.0 * math.log(10000.0) / (width // H)))
    sign = jnp.where(lax.rem(lane, 64) < 32, -1.0, 1.0)
    for r in range(tiles):
        at = slice(r * TILE, (r + 1) * TILE)
        within = lax.broadcasted_iota(jnp.int32, (TILE, 1), 0).astype(jnp.float32) + r * TILE
        turned = (within - starts[at]) * frequency
        cos_ref[at, :] = jnp.cos(turned)
        sin_ref[at, :] = jnp.sin(turned) * sign

    def put(product, out, at, table, scale=None):
        for pair in range(width // LANES):
            cols = slice(pair * LANES, (pair + 1) * LANES)
            turned = turn(product[:, cols], *table)
            if scale is not None:
                turned = turned * scale
            out[at, cols] = turned.astype(jnp.bfloat16)

    def lower(block):
        return layer_norm(block.astype(jnp.float32), gain, shift).astype(jnp.bfloat16)

    @pl.loop(0, tiles)
    def _(r):
        at = pl.ds(pl.multiple_of(r * TILE, TILE), TILE)
        table = cos_ref[at, :], sin_ref[at, :]
        h1 = lower(x_ref[at, :])
        h1t_ref[:, at] = jnp.transpose(h1)
        put(nn(h1, wq_ref[...]), q_ref, at, table, score_scale)
        put(nn(h1, wk_ref[...]), ko_ref, at, table)
        vo_ref[at, :] = nn(h1, wv_ref[...]).astype(jnp.bfloat16)

    mask_front(rows, meta_ref, bias, diag)
    for r in range(tiles):
        at = slice(r * TILE, (r + 1) * TILE)

        @pl.when(stream == 0)
        def _(at=at):
            base_ref[at, :] = x_ref[at, :]

        @pl.when(stream == 1)
        def _(r=r, at=at):
            move(r).wait_recv()
            base_ref[at, :] = coming[at, :]

        h1 = lower(base_ref[at, :])
        h1bt_ref[:, at] = jnp.transpose(h1)
        put(nn(h1, wk_ref[...]), kb_ref, at, (cos_ref[at, :], sin_ref[at, :]))
        vb_ref[at, :] = nn(h1, wv_ref[...]).astype(jnp.bfloat16)

        @pl.loop(0, width // LANES)
        def _(pair, r=r):
            cols = pl.ds(pl.multiple_of(pair * LANES, LANES), LANES)
            tile_front(r, pair, cols, q_ref, kb_ref, vb_ref, ko_ref, vo_ref, o_ref, bias, diag, lse)

    lse_ref[...] = jnp.transpose(lse[...])[: lse_ref.shape[0], :]

    @pl.when(stream == 0)
    def _():
        for r in range(tiles):
            move(r).wait_send()


def front(x, gain, shift, lengths, padding, weights, score_scale):
    rows, width = x.shape
    wide = lambda lines, columns: jax.ShapeDtypeStruct((lines, columns), jnp.float32)
    low = jnp.bfloat16
    flat = jax.ShapeDtypeStruct((rows, width), low)
    flipped = jax.ShapeDtypeStruct((width, rows), low)
    vmem = pl.BlockSpec(memory_space=pltpu.VMEM)
    return pl.pallas_call(
        functools.partial(front_kernel, score_scale),
        in_specs=[vmem] * 3 + [pl.BlockSpec(memory_space=pltpu.SMEM)] + [vmem] * 4,
        out_specs=[vmem] * 13,
        out_shape=[flat, flipped, flipped]
        + [flat] * 6
        + [wide(16, rows), wide(8, rows), wide(rows, LANES), wide(rows, LANES)],
        scratch_shapes=front_scratch(rows)
        + [
            pltpu.VMEM((rows, width), low),
            pltpu.SemaphoreType.DMA((rows // TILE,)),
            pltpu.SemaphoreType.DMA((rows // TILE,)),
        ],
        compiler_params=pltpu.CompilerParams(
            collective_id=1, has_side_effects=True, vmem_limit_bytes=62 * MIB
        ),
        cost_estimate=pl.CostEstimate(
            flops=4 * rows * rows * width + 10 * rows * width * width,
            bytes_accessed=20 * MIB,
            transcendentals=0,
        ),
        name="front",
    )(x, gain, shift, lengths, padding, *weights)


def attend(q, kb, vb, ko, vo, meta):
    rows, width = q.shape
    pairs = width // LANES
    spec = pl.BlockSpec((rows, LANES), lambda j: (0, j))
    return pl.pallas_call(
        functools.partial(attend_kernel, rows),
        grid=(pairs,),
        in_specs=[spec] * 5 + [pl.BlockSpec(meta.shape, lambda j: (0, 0))],
        out_specs=[spec, pl.BlockSpec((16, rows), lambda j: (0, 0))],
        out_shape=[
            jax.ShapeDtypeStruct((rows, width), jnp.bfloat16),
            jax.ShapeDtypeStruct((16, rows), jnp.float32),
        ],
        scratch_shapes=front_scratch(rows),
        compiler_params=pltpu.CompilerParams(vmem_limit_bytes=48 * MIB),
        cost_estimate=pl.CostEstimate(
            flops=2 * 2 * rows * rows * width, bytes_accessed=12 * rows * width, transcendentals=0
        ),
        name="attend",
    )(q, kb, vb, ko, vo, meta)


def mask_back(rows, meta_ref, bias, diag):
    columns = jnp.transpose(meta_ref[...])
    for i in range(rows // TILE):
        band = slice(i * TILE, (i + 1) * TILE)
        n = (i + 1) * TILE
        start, limit = meta_ref[0:1, band], meta_ref[1:2, band]
        key = lax.broadcasted_iota(jnp.int32, (n, TILE), 0)
        query = lax.broadcasted_iota(jnp.int32, (n, TILE), 1) + i * TILE
        usable = (columns[:n, 2:3] == 1.0) | (key == query)
        place = key.astype(jnp.float32)
        seen = (place >= start) & (place < limit) & usable
        bias[i][...] = jnp.where(seen, 0.0, masked_score)
        for sub in range(TILE // SUB):
            low = i * TILE + sub * SUB
            part = slice(low, low + SUB)
            key = lax.broadcasted_iota(jnp.int32, (SUB, SUB), 0) + low
            query = lax.broadcasted_iota(jnp.int32, (SUB, SUB), 1) + low
            usable = (columns[part, 2:3] == 1.0) | (key == query)
            same = (key // BLOCK == query // BLOCK) & (
                key.astype(jnp.float32) >= meta_ref[0:1, part]
            )
            seen = same & usable & (meta_ref[3:4, part] == 1.0)
            diag[:, part] = jnp.where(seen, 0.0, masked_score)


def pair_back(
    rows, score_scale, pair, out_cols, tick, q_ref, kb_ref, vb_ref, ko_ref, vo_ref, o_ref, do_ref, lse_ref,
    cos_ref, sin_ref, dq_ref, dkb_ref, dvb_ref, dko_ref, dvo_ref, bias, diag, dk_sum, dv_sum,
):
    head_lane = lax.broadcasted_iota(jnp.int32, (8, LANES), 1)
    head_row = lax.broadcasted_iota(jnp.int32, (8, LANES), 0)
    pick = jnp.where(head_lane // 64 == head_row, 1.0, 0.0).astype(jnp.bfloat16)
    for i in reversed(range(rows // TILE)):
        band = slice(i * TILE, (i + 1) * TILE)
        n = (i + 1) * TILE
        q2 = two_heads(q_ref[band, :])
        do = do_ref[band, :]
        do2 = two_heads(do)
        prod = do.astype(jnp.float32) * o_ref[band, :].astype(jnp.float32)
        high = prod.astype(jnp.bfloat16)
        rest = (prod - high.astype(jnp.float32)).astype(jnp.bfloat16)
        inner = nt(pick, high) + nt(pick, rest)
        inner = jnp.concatenate([inner[0:1], inner[1:2]], axis=1)
        level = jnp.concatenate(
            [lse_ref[pl.ds(2 * pair, 1), band], lse_ref[pl.ds(2 * pair + 1, 1), band]], axis=1
        )
        b = bias[i][...]
        s = nt(kb_ref[:n, :], q2) + jnp.concatenate([b, b], axis=1)
        p = jnp.exp(s - level)
        dp = nt(vb_ref[:n, :], do2)
        ds = (p * (dp - inner)).astype(jnp.bfloat16)
        dv = nn(p.astype(jnp.bfloat16), do2)
        dk = nn(ds, q2)
        if i == rows // TILE - 1:
            dv_sum[...] = dv
            dk_sum[...] = dk
        else:
            dv_sum[:n, :] += dv
            dk_sum[:n, :] += dk
        dq = tn(ds, kb_ref[:n, :])
        extra = []
        for sub in range(TILE // SUB):
            low = i * TILE + sub * SUB
            part = slice(low, low + SUB)
            qs, dos = subs(q2, sub), subs(do2, sub)
            d = diag[:, part]
            at = slice(sub * SUB, (sub + 1) * SUB)
            at2 = slice(TILE + sub * SUB, TILE + (sub + 1) * SUB)
            lev = jnp.concatenate([level[:, at], level[:, at2]], axis=1)
            inn = jnp.concatenate([inner[:, at], inner[:, at2]], axis=1)
            s = nt(ko_ref[part, :], qs) + jnp.concatenate([d, d], axis=1)
            p = jnp.exp(s - lev)
            dp = nt(vo_ref[part, :], dos)
            ds = (p * (dp - inn)).astype(jnp.bfloat16)
            dvo_ref[part, out_cols] = nn(p.astype(jnp.bfloat16), dos).astype(jnp.bfloat16)
            dko = nn(ds, qs)
            dko_ref[part, out_cols] = turn(dko, cos_ref[part, :], -sin_ref[part, :]).astype(jnp.bfloat16)
            extra.append(tn(ds, ko_ref[part, :]))
        dq = dq + jnp.concatenate(
            [extra[0][:SUB], extra[1][:SUB], extra[0][SUB:], extra[1][SUB:]], axis=0
        )
        dq = one_row(dq) * score_scale
        dq_ref[band, out_cols] = turn(dq, cos_ref[band, :], -sin_ref[band, :]).astype(jnp.bfloat16)
        tick(rows // TILE - i)
    dvb_ref[:, out_cols] = dv_sum[...].astype(jnp.bfloat16)
    dkb_ref[:, out_cols] = turn(dk_sum[...], cos_ref[...], -sin_ref[...]).astype(jnp.bfloat16)


def attend_back_kernel(
    rows, score_scale, q_ref, kb_ref, vb_ref, ko_ref, vo_ref, o_ref, do_ref, lse_ref, meta_ref, cos_ref, sin_ref,
    *refs,
):
    pair = pl.program_id(0)
    dq_ref, dkb_ref, dvb_ref, dko_ref, dvo_ref, *bias, diag, dk_sum, dv_sum = refs
    pl.when(pair == 0)(lambda: mask_back(rows, meta_ref, bias, diag))
    pair_back(
        rows, score_scale, pair, slice(None), lambda slot: None, q_ref, kb_ref, vb_ref, ko_ref, vo_ref, o_ref,
        do_ref, lse_ref, cos_ref, sin_ref, dq_ref, dkb_ref, dvb_ref, dko_ref, dvo_ref, bias, diag, dk_sum,
        dv_sum,
    )


def back_scratch(rows):
    return [pltpu.VMEM(((i + 1) * TILE, TILE), jnp.float32) for i in range(rows // TILE)] + [
        pltpu.VMEM((SUB, rows), jnp.float32),
        pltpu.VMEM((rows, LANES), jnp.float32),
        pltpu.VMEM((rows, LANES), jnp.float32),
    ]


def attend_back(q, kb, vb, ko, vo, o, do, lse, meta, cosine, sine, score_scale):
    rows, width = q.shape
    pairs = width // LANES
    spec = pl.BlockSpec((rows, LANES), lambda j: (0, j))
    whole = lambda a: pl.BlockSpec(a.shape, lambda j: (0, 0))
    return pl.pallas_call(
        functools.partial(attend_back_kernel, rows, score_scale),
        grid=(pairs,),
        in_specs=[spec] * 7 + [whole(lse), whole(meta), whole(cosine), whole(sine)],
        out_specs=[spec] * 5,
        out_shape=[jax.ShapeDtypeStruct((rows, width), jnp.bfloat16)] * 5,
        scratch_shapes=back_scratch(rows),
        compiler_params=pltpu.CompilerParams(vmem_limit_bytes=48 * MIB),
        cost_estimate=pl.CostEstimate(
            flops=5 * 2 * rows * rows * width, bytes_accessed=24 * rows * width, transcendentals=0
        ),
        name="attend_back",
    )(q, kb, vb, ko, vo, o, do, lse, meta, cosine, sine)


F1, OUT, F2, P0, P1, P2, N = range(7)
TAIL_STREAMS = (
    ("lyxh", 1024), ("xylh", 384), ("yxlh", 1024), ("xylh", 384), ("xylh", 384), ("ylhx", 384), ("lyhx", 128),
)
TAIL_FAR = 3
FEEDS = (F1, F2)
TAIL_TICKS = {
    (0, 3): [(F2, 0)],
    (1, 1): [(OUT, 0)],
    (1, 2): [(F1, 0)],
    (2, 2): [(OUT, 1), (P0, 0)],
    (3, 3): [(F2, 1)],
    (3, 5): [(OUT, 2), (P0, 1)],
    (4, 1): [(F1, 1)],
    (4, 2): [(P1, 0)],
    (4, 3): [(OUT, 3)],
    (5, 1): [(P0, 2), (F2, 2)],
    (5, 3): [(OUT, 4)],
    (5, 5): [(P0, 3), (P1, 1), (F1, 2)],
}
TAIL_POST = {
    0: [(F2, 3)],
    1: [(P2, 0)],
    2: [(P0, 4)],
    3: [(P1, 2)],
    4: [(F1, 3)],
    5: [(F2, 4), (N, 0), (P1, 3)],
    6: [(P2, 1), (N, 1), (F1, 4), (P1, 4), (N, 2), (P2, 2)],
    7: [(N, 3), (P2, 3), (N, 4)],
    8: [(P2, 4)],
}


def normalized(x):
    x = x.astype(jnp.float32)
    centre = x - jnp.mean(x, axis=-1, keepdims=True)
    inverse = lax.rsqrt(jnp.mean(centre * centre, axis=-1, keepdims=True) + epsilon)
    return centre * inverse, inverse


def normal_back(grad, gain, n, inverse):
    e = grad * gain
    return inverse * (
        e - jnp.mean(e, axis=-1, keepdims=True) - n * jnp.mean(e * n, axis=-1, keepdims=True)
    )


def tail_kernel(
    rows, score_scale, q_ref, kb_ref, vb_ref, ko_ref, vo_ref, o_ref, do_ref, lse_ref, meta_ref, cos_ref, sin_ref,
    h1t_ref, h1bt_ref, gain_ref, norm_ref, first_ref, *refs,
):
    pair = pl.program_id(0)
    hbm, refs = refs[:6], refs[6:]
    ff_ref, go_ref, refs = refs[0], refs[1], refs[2:]
    out_ref, up_out, down_out, head_out, norm_out, refs = *refs[:5], refs[5:]
    scratch, refs = refs[:7], refs[7:]
    bias, (diag, dk_sum, dv_sum) = scratch[:4], scratch[4:]
    dq, dkb, dvb, dko, dvo, refs = *refs[:5], refs[5:]
    held, refs = refs[:5], refs[5:]
    wq, wk, wv, x, base = held
    coming, pair_sums, norm_sums, refs = refs[0], refs[1:4], refs[4], refs[5:]
    load_sem, send_sem, recv_sem, refs = refs[0], refs[1], refs[2], refs[3:]
    sources = [(ff_ref.at[1], 0), (go_ref, 0), (ff_ref.at[2], 0)]
    sources += [(ref, 0) for ref in (*pair_sums, norm_sums)]
    scatter = Scatter(TAIL_STREAMS, sources, refs, TAIL_FAR)
    stream = lax.axis_index("stream")
    tiles = rows // TILE
    width = x.shape[1]
    loads = [
        pltpu.make_async_copy(src, dst, load_sem.at[i])
        for i, (src, dst) in enumerate(zip(hbm, (*held, out_ref)))
    ]

    def tick(slot):
        for at, moves in TAIL_TICKS.items():
            if at[1] == slot:
                @pl.when(pair == at[0])
                def _(moves=moves):
                    for number, index in moves:
                        scatter.step(number, index)

    def post(slot):
        for number, index in TAIL_POST.get(slot, ()):
            scatter.step(number, index)

    @pl.when(pair == 0)
    def _():
        scatter.greet()
        scatter.open((F2, OUT, F1))
        for load in loads:
            load.start()
        mask_back(rows, meta_ref, bias, diag)

    cols = pl.ds(pl.multiple_of(pair * LANES, LANES), LANES)
    pair_back(
        rows, score_scale, pair, cols, tick, q_ref, kb_ref, vb_ref, ko_ref, vo_ref, o_ref,
        do_ref, lse_ref, cos_ref, sin_ref, dq, dkb, dvb, dko, dvo, bias, diag, dk_sum, dv_sum,
    )

    for number, sums in enumerate(pair_sums):
        @pl.when(pair == 2 * number + 1)
        def _(number=number, sums=sums):
            both = slice(2 * number * LANES, (2 * number + 2) * LANES)
            for at, block in enumerate((
                nn(h1t_ref[...], dq[:, both]),
                nn(h1t_ref[...], dko[:, both]) + nn(h1bt_ref[...], dkb[:, both]),
                nn(h1t_ref[...], dvo[:, both]) + nn(h1bt_ref[...], dvb[:, both]),
            )):
                block = block.astype(jnp.bfloat16)
                for half in range(2):
                    sums[half, :, :, :, :, :, at * LANES : (at + 1) * LANES] = block[
                        :, half * LANES : (half + 1) * LANES
                    ].reshape(2, 2, 2, 2, RUN, LANES)
            scatter.open((P0 + number,))

    tick(tiles + 1)

    @pl.when(pair == pl.num_programs(0) - 1)
    def _():
        for load in loads:
            load.wait()
        gain = gain_ref[...].reshape(1, width)

        def band(r):
            return slice(r * TILE, (r + 1) * TILE)

        def move(r):
            return pltpu.make_async_remote_copy(
                src_ref=dkb.at[band(r)],
                dst_ref=coming.at[band(r)],
                send_sem=send_sem.at[r],
                recv_sem=recv_sem.at[r],
                device_id=scatter.to["x"],
                device_id_type=MESH,
            )

        gain_sum = jnp.zeros((1, width), jnp.float32)
        bias_sum = jnp.zeros((1, width), jnp.float32)
        for r in range(tiles):
            at = band(r)
            grad = nt(dkb[at, :], wk[...]) + nt(dvb[at, :], wv[...])
            dkb[at, :] = grad.astype(jnp.bfloat16)
            pl.when(stream == 1)(lambda r=r: move(r).start())
            n, _ = normalized(base[at, :])
            gain_sum += jnp.sum(grad * n, axis=0, keepdims=True)
            bias_sum += jnp.sum(grad, axis=0, keepdims=True)
        post(0)
        for r in range(tiles):
            at = band(r)
            grad = nt(dq[at, :], wq[...]) + nt(dko[at, :], wk[...]) + nt(dvo[at, :], wv[...])
            n, inverse = normalized(x[at, :])
            gain_sum += jnp.sum(grad * n, axis=0, keepdims=True)
            bias_sum += jnp.sum(grad, axis=0, keepdims=True)
            grad = grad + jnp.where(stream == 0, dkb[at, :].astype(jnp.float32), 0.0)
            out_ref[at, :] += normal_back(grad, gain, n, inverse)
            post(r + 1)
        eye = jnp.where(
            lax.broadcasted_iota(jnp.int32, (8, LANES), 0)
            == lax.broadcasted_iota(jnp.int32, (8, LANES), 1),
            1.0,
            0.0,
        ).astype(jnp.bfloat16)
        zero = jnp.zeros((6, width), jnp.float32)
        for half, sums in enumerate((
            jnp.concatenate([gain_sum, bias_sum, zero], axis=0), norm_ref[...]
        )):
            block = tn(sums.astype(jnp.bfloat16), eye).astype(jnp.bfloat16)
            norm_sums[half] = block.reshape(2, 2, 2, 2, RUN, LANES)
        scatter.open((N,))
        post(tiles + 1)
        for r in range(tiles):
            at = band(r)

            @pl.when(stream == 1)
            def _(r=r):
                move(r).wait_send()

            @pl.when(stream == 0)
            def _(r=r, at=at):
                move(r).wait_recv()
                n, inverse = normalized(x[at, :])
                out_ref[at, :] += normal_back(coming[at, :].astype(jnp.float32), gain, n, inverse)

            post(tiles + 2 + r)
        scatter.finish()
        places = [sum(part for _, part in TAIL_STREAMS[:i]) for i in range(len(TAIL_STREAMS))]
        for half, out in enumerate((up_out, down_out)):
            out[:, : first_ref.shape[2]] = first_ref[half]
            low = first_ref.shape[2]
            for number in FEEDS:
                part = TAIL_STREAMS[number][1]
                out[:, low : low + part] = scatter.result(half, places[number], part)
                low += part
        middle = width // 2
        for half in range(2):
            head_out[0, :, half * middle : (half + 1) * middle] = scatter.result(
                half, places[OUT], middle
            )
            norm_out[half] = scatter.result(half, places[N], LANES)
            for number in range(len(pair_sums)):
                low = (2 * number + half) * LANES
                for at in range(3):
                    head_out[1 + at, :, low : low + LANES] = scatter.result(
                        half, places[P0 + number] + at * LANES, LANES
                    )


def tail(
    operands, h1t, h1bt, gain, norm, first, weights, x, base, middle_grad, ff, go, score_scale
):
    rows, width = x.shape
    pairs = width // LANES
    hidden = first.shape[2] + sum(TAIL_STREAMS[number][1] for number in FEEDS)
    shapes = [(rows, width), (24, hidden), (24, hidden), (4, 24, width), (2, 24, LANES)]
    spec = pl.BlockSpec((rows, LANES), lambda j: (0, j))
    once = pl.Buffered(1)
    whole = lambda shape: pl.BlockSpec(shape, lambda j: (0,) * len(shape), pipeline_mode=once)
    flat, square = (rows, width), (width, width)
    low = jnp.bfloat16
    scratch = back_scratch(rows)
    scratch += [pltpu.VMEM(flat, low)] * 5
    scratch += [pltpu.VMEM(square, low)] * 3 + [pltpu.VMEM(flat, low)] * 2
    scratch += [pltpu.VMEM(flat, low)]
    scratch += [pltpu.VMEM((2, 2, 2, 2, 2, RUN, 3 * LANES), low)] * 3
    scratch += [pltpu.VMEM((2, 2, 2, 2, 2, RUN, LANES), low)]
    scratch += [pltpu.SemaphoreType.DMA((6,))]
    scratch += [pltpu.SemaphoreType.DMA((rows // TILE,))] * 2
    scratch += Scatter.shapes(TAIL_STREAMS, TAIL_FAR)
    return pl.pallas_call(
        functools.partial(tail_kernel, rows, score_scale),
        grid=(pairs,),
        in_specs=[spec] * 7
        + [whole(a.shape) for a in (*operands[7:], h1t, h1bt, gain, norm, first)]
        + [pl.BlockSpec(memory_space=pl.ANY)] * 8,
        out_specs=[whole(shape) for shape in shapes],
        out_shape=[jax.ShapeDtypeStruct(shape, jnp.float32) for shape in shapes],
        scratch_shapes=scratch,
        compiler_params=pltpu.CompilerParams(
            collective_id=0, has_side_effects=True, vmem_limit_bytes=63 * MIB
        ),
        cost_estimate=pl.CostEstimate(
            flops=10 * rows * rows * width + 20 * rows * width * width,
            bytes_accessed=40 * MIB,
            transcendentals=0,
        ),
        name="tail",
    )(*operands, h1t, h1bt, gain, norm, first, *weights, x, base, middle_grad, ff, go)


FEED_TILE = 1024
FEED_STREAMS = (("yxlh", 512), ("xylh", 512))
FEED_TICKS = {
    (1, 1): [(0, 0), (1, 0)], (1, 5): [(0, 1), (1, 1)], (2, 1): [(0, 2), (1, 2)], (2,5): [(0, 3), (1, 3)], (2,6): [(0, 4), (1, 4)],
}


def feed_kernel(
    streams, x_ref, o_ref, dy_ref, wo_ref, gain_ref, shift_ref, wu_ref, wd_ref,
    y_ref, do_ref, dx_ref, norm_ref, ff_ref, go_ref, *refs,
):
    f = pl.program_id(0)
    rows, width = x_ref.shape
    gain, shift = gain_ref[...].reshape(1, width), shift_ref[...].reshape(1, width)
    scatter = None
    if streams:
        out_ref, refs = refs[0], refs[1:]
    total, normal, scale, h2s, h2t, dyt, gs, dus = refs[:8]
    if streams:
        first = refs[8]
        sources, low = [], 0
        for _, part in streams:
            sources.append((first, low))
            low += part
        scatter = Scatter(streams, sources, refs[9:], 0)

    def tick(slot):
        if scatter is None:
            return
        for at, moves in FEED_TICKS.items():
            if at[1] == slot:
                @pl.when(f == at[0])
                def _(moves=moves):
                    for stream, index in moves:
                        scatter.step(stream, index)

    def band(r):
        return pl.ds(pl.multiple_of(r * TILE, TILE), TILE)

    @pl.when(f == 0)
    def _():
        if scatter is not None:
            scatter.greet()
        norm_ref[...] = jnp.zeros_like(norm_ref)

        @pl.loop(0, rows // TILE)
        def _(r):
            at = band(r)
            x1 = x_ref[at, :].astype(jnp.float32) + nn(o_ref[at, :], wo_ref[...])
            centre = x1 - jnp.mean(x1, axis=-1, keepdims=True)
            inverse = lax.rsqrt(jnp.mean(centre * centre, axis=-1, keepdims=True) + epsilon)
            n = centre * inverse
            h2 = (n * gain + shift).astype(jnp.bfloat16)
            total[at, :] = x1
            normal[at, :] = n
            scale[at, :] = jnp.broadcast_to(inverse, (TILE, LANES))
            h2s[at, :] = h2
            h2t[:, at] = jnp.transpose(h2)
            dyt[:, at] = jnp.transpose(dy_ref[at, :])
            dx_ref[at, :] = jnp.zeros((TILE, width), jnp.float32)

    for r in range(rows // TILE):
        at = band(r)
        u = nn(h2s[at, :], wu_ref[...])
        square = u * u
        curve = jnp.tanh(0.7978845608028654 * u * (1.0 + 0.044715 * square))
        upper = 0.5 * (1.0 + curve)
        g = (u * upper).astype(jnp.bfloat16)
        slope = upper + u * upper * (1.0 - curve) * (
            0.7978845608028654 + 3 * 0.044715 * 0.7978845608028654 * square
        )
        gs[at, :] = g
        total[at, :] += nn(g, wd_ref[...])
        du = (nt(dy_ref[at, :], wd_ref[...]) * slope).astype(jnp.bfloat16)
        dus[at, :] = du
        dx_ref[at, :] += nt(du, wu_ref[...])
        tick(r)
    slot = rows // TILE
    for half, (left, right) in enumerate(((h2t, dus), (dyt, gs))):
        for c in range(right.shape[1] // TILE):
            cols = pl.ds(c * TILE, TILE)
            block = nn(left[...], right[:, cols]).astype(jnp.bfloat16)
            block = block.reshape(2, 2, 2, 2, RUN, TILE)
            ff_ref[0, half, :, :, :, :, :, cols] = block
        tick(slot + half)
    if scatter is not None:
        @pl.when(f == 0)
        def _():
            @pl.loop(0, 32)
            def _(i):
                at = (i // 16, i // 8 % 2, i // 4 % 2, i // 2 % 2, i % 2)
                first[at] = ff_ref[(0,) + at]

            scatter.open(range(len(streams)))

    @pl.when(f == pl.num_programs(0) - 1)
    def _():
        @pl.loop(0, rows // TILE)
        def _(r):
            at = band(r)
            y_ref[at, :] = total[at, :].astype(jnp.bfloat16)
            n = normal[at, :]
            dh2 = dx_ref[at, :]
            norm_ref[0:1, :] += jnp.sum(dh2 * n, axis=0, keepdims=True)
            norm_ref[1:2, :] += jnp.sum(dh2, axis=0, keepdims=True)
            e = dh2 * gain
            e = (
                e
                - jnp.mean(e, axis=-1, keepdims=True)
                - n * jnp.mean(e * n, axis=-1, keepdims=True)
            )
            dx = dy_ref[at, :].astype(jnp.float32) + scale[at, 0:1] * e
            dx_ref[at, :] = dx
            da = dx.astype(jnp.bfloat16)
            dyt[:, at] = jnp.transpose(da)
            do_ref[at, :] = nt(da, wo_ref[...]).astype(jnp.bfloat16)

        middle = width // 2
        for half in range(2):
            block = nn(dyt[...], o_ref[:, half * middle : (half + 1) * middle])
            go_ref[half] = block.astype(jnp.bfloat16).reshape(2, 2, 2, 2, RUN, middle)
        tick(slot + 2)
        if scatter is not None:
            scatter.finish()
            for half in range(2):
                out_ref[half] = scatter.result(half, 0, out_ref.shape[2])


def feed(x, o, dy, wo, gain, shift, wu, wd, streams):
    rows, width = x.shape
    tiles = wu.shape[1] // FEED_TILE
    once = pl.Buffered(1)
    whole = lambda shape: pl.BlockSpec(shape, lambda f: (0,) * len(shape), pipeline_mode=once)
    flat, square = (rows, width), (width, width)
    parts = (2, 2, 2, 2, RUN)
    out_specs = [
        whole(flat),
        whole(flat),
        whole(flat),
        whole((8, width)),
        pl.BlockSpec((1, 2) + parts + (FEED_TILE,), lambda f: (f,) + (0,) * 7),
        whole((2,) + parts + (width // 2,)),
    ]
    out_shape = [
        jax.ShapeDtypeStruct(flat, jnp.bfloat16),
        jax.ShapeDtypeStruct(flat, jnp.bfloat16),
        jax.ShapeDtypeStruct(flat, jnp.float32),
        jax.ShapeDtypeStruct((8, width), jnp.float32),
        jax.ShapeDtypeStruct((tiles, 2) + parts + (FEED_TILE,), jnp.bfloat16),
        jax.ShapeDtypeStruct((2,) + parts + (width // 2,), jnp.bfloat16),
    ]
    scratch = [
        pltpu.VMEM(flat, jnp.float32),
        pltpu.VMEM(flat, jnp.float32),
        pltpu.VMEM((rows, LANES), jnp.float32),
        pltpu.VMEM(flat, jnp.bfloat16),
        pltpu.VMEM((width, rows), jnp.bfloat16),
        pltpu.VMEM((width, rows), jnp.bfloat16),
        pltpu.VMEM((rows, FEED_TILE), jnp.bfloat16),
        pltpu.VMEM((rows, FEED_TILE), jnp.bfloat16),
    ]
    options = {}
    if streams:
        out_specs += [whole((2, 24, FEED_TILE))]
        out_shape += [jax.ShapeDtypeStruct((2, 24, FEED_TILE), jnp.float32)]
        scratch += [pltpu.VMEM((2,) + parts + (FEED_TILE,), jnp.bfloat16)]
        scratch += Scatter.shapes(streams, 0)
        options = {"collective_id": 2, "has_side_effects": True}
    return pl.pallas_call(
        functools.partial(feed_kernel, streams),
        grid=(tiles,),
        in_specs=[
            whole(flat),
            whole(flat),
            whole(flat),
            whole(square),
            whole(gain.shape),
            whole(shift.shape),
            pl.BlockSpec((width, FEED_TILE), lambda f: (0, f)),
            pl.BlockSpec((FEED_TILE, width), lambda f: (f, 0)),
        ],
        out_specs=out_specs,
        out_shape=out_shape,
        scratch_shapes=scratch,
        compiler_params=pltpu.CompilerParams(vmem_limit_bytes=62 * MIB, **options),
        cost_estimate=pl.CostEstimate(
            flops=12 * rows * width * wu.shape[1] + 6 * rows * width * width,
            bytes_accessed=30 * MIB,
            transcendentals=0,
        ),
        name="feed",
    )(x, o, dy, wo, gain, shift, wu, wd)


def shards(
    tokens,
    lengths,
    pad_mask,
    first_gain,
    first_bias,
    query_weight,
    key_weight,
    value_weight,
    out_weight,
    second_gain,
    second_bias,
    up_weight,
    down_weight,
    output_grad,
):
    total_rows = tokens.shape[1]
    model_width = tokens.shape[2]
    head_width = model_width // H
    score_scale = head_width ** (-0.5)
    is_noisy = lax.axis_index("stream") == 1
    own = tokens[0]
    weights = (query_weight, key_weight, value_weight)
    ring = lax.axis_size("dp") == 16 and lax.axis_size("stream") == 2
    if ring:
        base, h1t, h1bt, q, kb, vb, ko, vo, mixed_low, lse, meta, cosine, sine = front(
            own, first_gain, first_bias, lengths, pad_mask[None], weights, score_scale
        )
    else:
        places, first_place = layout(lengths[0], total_rows, lengths.shape[1])
        limit = (places // BLOCK + jnp.where(is_noisy, 0, 1)) * BLOCK
        noisy_row = jnp.broadcast_to(jnp.where(is_noisy, 1, 0), places.shape)
        blank = jnp.zeros_like(places)
        meta = jnp.stack(
            [first_place, limit, pad_mask, noisy_row, blank, blank, blank, blank]
        ).astype(jnp.float32)
        cosine, sine = angle_tables(places - first_place, head_width)
        far = lax.ppermute(own, "stream", [(0, 1)])
        base = jnp.where(is_noisy, far, own)
        norms = (first_gain, first_bias)
        h1t, q, ko, vo = project(own, *norms, cosine, sine, weights, score_scale)
        h1bt, kb, vb = project(base, *norms, cosine, sine, weights[1:], score_scale)
        mixed_low, lse = attend(q, kb, vb, ko, vo, meta)

    fed = feed(
        own, mixed_low, output_grad[0], out_weight, second_gain, second_bias, up_weight, down_weight, FEED_STREAMS if ring else (),
    )
    layer_output, mixed_grad, middle_grad, norm_sums, ff_part, out_part = fed[:6]
    layer_output = layer_output[None]
    operands = (q, kb, vb, ko, vo, mixed_low, mixed_grad, lse, meta, cosine, sine)
    if ring:
        tokens_grad, up_grad, down_grad, heads, norms = tail(
            operands, h1t, h1bt, first_gain, norm_sums, fed[6], weights, own, base, middle_grad, ff_part,
            out_part, score_scale,
        )
        tokens_grad = tokens_grad[None]
        out_grad, query_grad, key_grad, value_grad = heads
        first_grads, second_grads = norms[0, :, :2].T, norms[1, :, :2].T
    else:
        dq, dkb, dvb, dko, dvo = attend_back(*operands, score_scale)
        base_grad = nt(dkb, key_weight) + nt(dvb, value_weight)
        back = lax.ppermute(base_grad.astype(jnp.bfloat16), "stream", [(1, 0)])
        normed_grad = (
            nt(dq, query_weight)
            + nt(dko, key_weight)
            + nt(dvo, value_weight)
            + jnp.where(is_noisy, 0.0, base_grad + back.astype(jnp.float32))
        )
        inputs = own.astype(jnp.float32)
        first_pull = jax.vjp(layer_norm, inputs, first_gain, first_bias)[1]
        input_part, first_gain_part, first_bias_part = first_pull(normed_grad)
        tokens_grad = (middle_grad + input_part)[None]
        ff_part = ff_part.reshape(-1, 2, model_width, FEED_TILE)
        out_part = out_part.reshape(2, model_width, model_width // 2)
        norm_part = jnp.stack(
            [first_gain_part, first_bias_part, norm_sums[0], norm_sums[1]], axis=1
        )
        part = jnp.concatenate(
            [ff_part[f, i] for i in range(2) for f in range(ff_part.shape[0])]
            + [out_part[0], out_part[1], nn(h1t, dq).astype(jnp.bfloat16)]
            + [(nn(h1t, dko) + nn(h1bt, dkb)).astype(jnp.bfloat16)]
            + [(nn(h1t, dvo) + nn(h1bt, dvb)).astype(jnp.bfloat16)]
            + [jnp.pad(norm_part, ((0, 0), (0, LANES - 4))).astype(jnp.bfloat16)],
            axis=1,
        )
        part = lax.psum_scatter(part, ("stream", "dp"), scatter_dimension=0, tiled=True)
        part = part.astype(jnp.float32)
        hidden_width = up_weight.shape[1]
        cuts = (hidden_width, hidden_width) + (model_width,) * 4 + (LANES,)
        pieces, low = [], 0
        for cut in cuts:
            pieces.append(part[:, low : low + cut])
            low += cut
        up_grad, down_grad, out_grad, query_grad, key_grad, value_grad, norms = pieces
        first_grads, second_grads = norms[:, :2].T, norms[:, 2:4].T
    return (
        layer_output,
        tokens_grad,
        first_grads,
        query_grad,
        key_grad,
        value_grad,
        out_grad.T,
        second_grads,
        up_grad,
        down_grad.T,
    )


def solution(mesh):
    placed = (
        P("stream", "dp", None),
        P("dp", None),
        P("dp"),
        P(),
        P(),
        P(),
        P(),
        P(),
        P(),
        P(),
        P(),
        P(),
        P(),
        P("stream", "dp", None),
    )
    return jax.shard_map(
        shards,
        mesh=mesh,
        in_specs=placed,
        out_specs=(
            P("stream", "dp", None),
            P("stream", "dp", None),
            P(None, ("stream", "dp")),
            P(("stream", "dp"), None),
            P(("stream", "dp"), None),
            P(("stream", "dp"), None),
            P(None, ("stream", "dp")),
            P(None, ("stream", "dp")),
            P(("stream", "dp"), None),
            P(None, ("stream", "dp")),
        ),
        check_vma=False,
    )
```

```python
import functools
import math

import jax
import jax.numpy as jnp
from jax import lax
from jax.experimental import pallas as pl
from jax.experimental.pallas import tpu as pltpu
from jax.sharding import PartitionSpec as P

H = 12
BLOCK = 16
TILE = 256
SUB = 128
LANES = 128

epsilon = 1e-05
masked_score = -1e30
MIB = 1024 * 1024


def layer_norm(values, gain_row, bias_row):
    centre = values - jnp.mean(values, axis=-1, keepdims=True)
    spread = jnp.mean(centre * centre, axis=-1, keepdims=True)
    return centre * lax.rsqrt(spread + epsilon) * gain_row + bias_row


def layout(lengths_row, total_rows, doc_slots):
    places = jnp.arange(total_rows, dtype=jnp.int32)
    end_places = jnp.cumsum(lengths_row)
    starts = end_places - lengths_row
    document = jnp.sum((places[:, None] >= end_places[None, :]).astype(jnp.int32), axis=1)
    picked = document[:, None] == jnp.arange(doc_slots, dtype=jnp.int32)[None, :]
    first_place = jnp.sum(jnp.where(picked, starts[None, :], 0), axis=1)
    return (places, first_place)


def angle_tables(position, head_width):
    half_width = head_width // 2
    freq_index = (jnp.arange(half_width)).astype(jnp.float32)
    frequency = jnp.exp(freq_index * (-2.0 * math.log(10000.0) / head_width))
    turned = position.astype(jnp.float32)[:, None] * frequency[None, :]
    cosine, sine = jnp.cos(turned), jnp.sin(turned)
    return (
        jnp.concatenate([cosine] * 4, axis=1),
        jnp.concatenate([-sine, sine, -sine, sine], axis=1),
    )


def turn(values, cosine, sine):
    lane = lax.broadcasted_iota(jnp.int32, values.shape, 1)
    low = lax.rem(lane, 64) < 32
    partner = jnp.where(low, pltpu.roll(values, LANES - 32, 1), pltpu.roll(values, 32, 1))
    return values * cosine + partner * sine


def nt(left, right):
    return lax.dot_general(
        left, right, (((1,), (1,)), ((), ())), preferred_element_type=jnp.float32
    )


def tn(left, right):
    return lax.dot_general(
        left, right, (((0,), (0,)), ((), ())), preferred_element_type=jnp.float32
    )


def nn(left, right):
    return jnp.dot(left, right, preferred_element_type=jnp.float32)


MESH = pl.DeviceIdType.MESH
RUN = 48


class Scatter:
    @staticmethod
    def shapes(streams, far):
        total = sum(width for _, width in streams)
        shapes = [
            pltpu.VMEM((2, 2, 2, 2, RUN, total), jnp.bfloat16),
            pltpu.VMEM((2, 24, total), jnp.float32),
            pltpu.VMEM((24, total), jnp.float32),
        ]
        for number, (order, width) in enumerate(streams):
            if number < far:
                shapes += [pltpu.VMEM((2, 2, 2, 2, RUN, width), jnp.bfloat16)]
            for left in range(len(order) - 1, -1, -1):
                shapes += [pltpu.VMEM((2,) * left + (RUN, width), jnp.bfloat16)]
        count = sum(1 + len(order) for order, _ in streams) + 1
        return shapes + [
            pltpu.SemaphoreType.DMA((count,)),
            pltpu.SemaphoreType.DMA((count,)),
            pltpu.SemaphoreType.DMA((len(streams),)),
        ]

    def __init__(self, streams, sources, refs, far):
        self.far = far
        self.sib, self.fin, self.other = refs[:3]
        self.bufs = list(refs[3:-3])
        self.send, self.recv, self.local = refs[-3:]
        s, d = lax.axis_index("stream"), lax.axis_index("dp")
        self.core = d % 2
        self.mine = {"x": s, "y": d // 2 % 2, "l": d // 4 % 2, "h": d // 8}
        self.to = {
            "x": {"stream": 1 - s},
            "y": {"dp": d + 2 - 4 * self.mine["y"]},
            "l": {"dp": d + 4 - 8 * self.mine["l"]},
            "h": {"dp": d + 8 - 16 * self.mine["h"]},
            "core": {"dp": d + 1 - 2 * self.core},
        }
        self.used = 0
        self.streams = []
        place = 0
        for (order, width), (source, low) in zip(streams, sources):
            self.streams.append(self.stream(order, place, width, source, low))
            place += width
        self.last = self.take()

    def take(self):
        self.used += 1
        return self.used - 1

    def copy(self, src, dst, k, to):
        return pltpu.make_async_remote_copy(
            src_ref=src,
            dst_ref=dst,
            send_sem=self.send.at[k],
            recv_sem=self.recv.at[k],
            device_id=self.to[to],
            device_id_type=MESH,
        )

    def greet(self):
        barrier = pltpu.get_barrier_semaphore()
        for to in self.to.values():
            pl.semaphore_signal(barrier, inc=1, device_id=to, device_id_type=MESH)
        pl.semaphore_wait(barrier, len(self.to))

    @staticmethod
    def add(dst, left, right):
        lead = dst.shape[:-2]
        count = math.prod(lead)

        def one(index):
            at = []
            for size in reversed(lead):
                at.append(index % size)
                index = index // size
            at = tuple(reversed(at))
            dst[at] = left[at] + right[at]

        if count == 1:
            one(0)
        else:
            pl.loop(0, count, unroll=min(count, 4))(one)

    def stream(self, order, place, width, source, low):
        number = len(self.streams)
        cols = pl.ds(place, width)
        every = (slice(None),) * 5
        src = self.sib.at[every + (cols,)]
        k = self.take()
        part = lambda core: source.at[(core,) + every + (pl.ds(low, width),)]
        swap = lambda src=src, k=k: self.copy(part(1 - self.core), src, k, "core")
        near = None
        if number < self.far:
            held = self.bufs.pop(0)
            near = lambda: pltpu.make_async_copy(part(self.core), held, self.local.at[number])

        def opening(src=src):
            swap().wait()
            if near is None:
                self.add(src, src, part(self.core))
            else:
                near().wait()
                self.add(src, src, held)

        steps = []
        pending = opening
        names = ["x", "h", "l", "y"]
        for axis in order:
            at = names.index(axis)
            names.pop(at)
            buf = self.bufs.pop(0)
            k = self.take()
            pick = lambda index, src=src, at=at: src.at[(slice(None),) * at + (index,)]
            make = lambda pick=pick, buf=buf, k=k, axis=axis: self.copy(
                pick(1 - self.mine[axis]), buf, k, axis
            )

            def begin(before=pending, make=make):
                before()
                make().start()

            def end(pick=pick, buf=buf, make=make, axis=axis):
                make().wait()
                self.add(buf, buf, pick(self.mine[axis]))

            steps.append(begin)
            pending = end
            src = buf

        def close(before=pending, src=src):
            before()
            for core in range(2):
                self.fin[core, :, cols] = src[24 * core : 24 * core + 24, :].astype(jnp.float32)

        steps.append(close)
        return (swap, near, steps)

    def open(self, order):
        for index in order:
            swap, near, _ = self.streams[index]
            swap().start()
            if near is not None:
                near().start()

    def step(self, stream, index):
        self.streams[stream][2][index]()

    def finish(self):
        last = self.copy(self.fin.at[1 - self.core], self.other, self.last, "core")
        last.start()
        last.wait()

    def result(self, half, place, width):
        cols = slice(place, place + width)
        return jnp.where(self.core == half, self.fin[half, :, cols], self.other[:, cols])


def project_kernel(score_scale, x_ref, gain_ref, shift_ref, cos_ref, sin_ref, *refs):
    count = (len(refs) - 1) // 2
    weights, outs = refs[:count], refs[count:]
    gain, shift = (ref[...].reshape(1, x_ref.shape[1]) for ref in (gain_ref, shift_ref))
    h1 = layer_norm(x_ref[...].astype(jnp.float32), gain, shift).astype(jnp.bfloat16)
    outs[0][...] = jnp.transpose(h1)
    cosine, sine = cos_ref[...], sin_ref[...]
    for index, (weight, out) in enumerate(zip(weights, outs[1:])):
        product = nn(h1, weight[...])
        is_value = index == count - 1
        is_query = count == 3 and index == 0
        if is_value:
            out[...] = product.astype(jnp.bfloat16)
            continue
        for pair in range(product.shape[1] // LANES):
            columns = slice(pair * LANES, (pair + 1) * LANES)
            turned = turn(product[:, columns], cosine, sine)
            if is_query:
                turned = turned * score_scale
            out[:, columns] = turned.astype(jnp.bfloat16)


def project(x, gain, shift, cosine, sine, weights, score_scale):
    rows, width = x.shape
    count = len(weights)
    row_spec = pl.BlockSpec((TILE, width), lambda i: (i, 0))
    table_spec = pl.BlockSpec((TILE, LANES), lambda i: (i, 0))
    whole = pl.BlockSpec((width, width), lambda i: (0, 0))
    line = pl.BlockSpec(gain.shape, lambda i: (0,))
    return pl.pallas_call(
        functools.partial(project_kernel, score_scale),
        grid=(rows // TILE,),
        in_specs=[row_spec, line, line, table_spec, table_spec] + [whole] * count,
        out_specs=[pl.BlockSpec((width, TILE), lambda i: (0, i))] + [row_spec] * count,
        out_shape=[jax.ShapeDtypeStruct((width, rows), jnp.bfloat16)]
        + [jax.ShapeDtypeStruct((rows, width), jnp.bfloat16)] * count,
        compiler_params=pltpu.CompilerParams(vmem_limit_bytes=40 * MIB),
        cost_estimate=pl.CostEstimate(
            flops=2 * rows * width * width * count,
            bytes_accessed=2 * (rows + count * (width + rows)) * width,
            transcendentals=0,
        ),
        name="project%d" % count,
    )(x, gain, shift, cosine, sine, *weights)


def two_heads(block):
    lane = lax.broadcasted_iota(jnp.int32, block.shape, 1)
    zero = jnp.zeros_like(block)
    return jnp.concatenate(
        [jnp.where(lane < 64, block, zero), jnp.where(lane < 64, zero, block)], axis=0
    )


def one_row(both):
    rows = both.shape[0] // 2
    lane = lax.broadcasted_iota(jnp.int32, (rows, LANES), 1)
    return jnp.where(lane < 64, both[:rows], both[rows:])


def subs(both, sub):
    low = sub * SUB
    return jnp.concatenate([both[low : low + SUB], both[TILE + low : TILE + low + SUB]], axis=0)


def mask_front(rows, meta_ref, bias, diag):
    columns = jnp.transpose(meta_ref[...])
    noisy = columns[:, 3:4]
    for i in range(rows // TILE):
        band = slice(i * TILE, (i + 1) * TILE)
        n = (i + 1) * TILE
        start, limit = columns[band, 0:1], columns[band, 1:2]
        key = lax.broadcasted_iota(jnp.int32, (TILE, n), 1)
        query = lax.broadcasted_iota(jnp.int32, (TILE, n), 0) + i * TILE
        usable = (meta_ref[2:3, :n] == 1.0) | (key == query)
        place = key.astype(jnp.float32)
        seen = (place >= start) & (place < limit) & usable
        bias[i][...] = jnp.where(seen, 0.0, masked_score)
        for sub in range(TILE // SUB):
            low = i * TILE + sub * SUB
            key = lax.broadcasted_iota(jnp.int32, (SUB, SUB), 1) + low
            query = lax.broadcasted_iota(jnp.int32, (SUB, SUB), 0) + low
            usable = (meta_ref[2:3, low : low + SUB] == 1.0) | (key == query)
            same = (key // BLOCK == query // BLOCK) & (
                key.astype(jnp.float32) >= columns[low : low + SUB, 0:1]
            )
            seen = same & usable & (noisy[low : low + SUB] == 1.0)
            diag[low : low + SUB, :] = jnp.where(seen, 0.0, masked_score)


def tile_front(i, pair, cols, q_ref, kb_ref, vb_ref, ko_ref, vo_ref, o_ref, bias, diag, lse):
    band = slice(i * TILE, (i + 1) * TILE)
    n = (i + 1) * TILE
    lane = lax.broadcasted_iota(jnp.int32, (TILE, LANES), 1)
    q2 = two_heads(q_ref[band, cols])
    b = bias[i][...]
    s = nt(q2, kb_ref[:n, cols]) + jnp.concatenate([b, b], axis=0)
    d = diag[band, :]

    def apart(sub):
        return slice(i * TILE + sub * SUB, i * TILE + (sub + 1) * SUB)

    def merge(parts):
        return jnp.concatenate(
            [parts[0][:SUB], parts[1][:SUB], parts[0][SUB:], parts[1][SUB:]], axis=0
        )

    parts = [nt(subs(q2, sub), ko_ref[apart(sub), cols]) for sub in range(TILE // SUB)]
    sd = merge(parts) + jnp.concatenate([d, d], axis=0)
    top = jnp.maximum(jnp.max(s, axis=1, keepdims=True), jnp.max(sd, axis=1, keepdims=True))
    p = jnp.exp(s - top)
    pd = jnp.exp(sd - top)
    total = jnp.sum(p, axis=1, keepdims=True) + jnp.sum(pd, axis=1, keepdims=True)
    pd_low = pd.astype(jnp.bfloat16)
    o = nn(p.astype(jnp.bfloat16), vb_ref[:n, cols])
    parts = [nn(subs(pd_low, sub), vo_ref[apart(sub), cols]) for sub in range(TILE // SUB)]
    o = (o + merge(parts)) * (1.0 / total)
    o_ref[band, cols] = one_row(o).astype(o_ref.dtype)
    level = top + jnp.log(total)
    old = lse[band, :]
    lse[band, :] = jnp.where(
        lane == 2 * pair, level[:TILE], jnp.where(lane == 2 * pair + 1, level[TILE:], old)
    )


def attend_kernel(rows, q_ref, kb_ref, vb_ref, ko_ref, vo_ref, meta_ref, o_ref, lse_ref, *refs):
    bias, diag, lse = refs[:-2], refs[-2], refs[-1]
    pair = pl.program_id(0)
    pl.when(pair == 0)(lambda: mask_front(rows, meta_ref, bias, diag))
    for i in range(rows // TILE):
        tile_front(
            i, pair, slice(None), q_ref, kb_ref, vb_ref, ko_ref, vo_ref, o_ref, bias, diag, lse
        )

    @pl.when(pair == pl.num_programs(0) - 1)
    def _():
        lse_ref[...] = jnp.transpose(lse[...])[: lse_ref.shape[0], :]


def front_scratch(rows):
    return [pltpu.VMEM((TILE, (i + 1) * TILE), jnp.float32) for i in range(rows // TILE)] + [
        pltpu.VMEM((rows, SUB), jnp.float32),
        pltpu.VMEM((rows, LANES), jnp.float32),
    ]


def front_kernel(
    score_scale, x_ref, gain_ref, shift_ref, lengths_ref, pad_ref, wq_ref, wk_ref, wv_ref,
    base_ref, h1t_ref, h1bt_ref, q_ref, kb_ref, vb_ref, ko_ref, vo_ref, o_ref, lse_ref, meta_ref, cos_ref,
    sin_ref, *refs,
):
    bias, diag, lse = refs[:4], refs[4], refs[5]
    coming, send_sem, recv_sem = refs[6:]
    rows, width = x_ref.shape
    stream = lax.axis_index("stream")
    gain, shift = gain_ref[...].reshape(1, width), shift_ref[...].reshape(1, width)
    partner = {"stream": 1 - stream}

    def move(r):
        return pltpu.make_async_remote_copy(
            src_ref=x_ref.at[r * TILE : (r + 1) * TILE],
            dst_ref=coming.at[r * TILE : (r + 1) * TILE],
            send_sem=send_sem.at[r],
            recv_sem=recv_sem.at[r],
            device_id=partner,
            device_id_type=MESH,
        )

    barrier = pltpu.get_barrier_semaphore()
    pl.semaphore_signal(barrier, inc=1, device_id=partner, device_id_type=MESH)
    pl.semaphore_wait(barrier, 1)
    tiles = rows // TILE

    @pl.when(stream == 0)
    def _():
        for r in range(tiles):
            move(r).start()

    place = lax.broadcasted_iota(jnp.int32, (1, rows), 1)
    end, start = 0, jnp.zeros((1, rows), jnp.int32)
    for slot in range(lengths_ref.shape[1]):
        end = end + lengths_ref[0, slot]
        start = jnp.where(place >= end, end, start)
    limit = (place // BLOCK + 1 - stream) * BLOCK
    lines = [start, limit, pad_ref[...], jnp.zeros_like(place) + stream]
    lines = jnp.concatenate(lines + [jnp.zeros_like(place)] * 4, axis=0).astype(jnp.float32)
    meta_ref[...] = lines
    starts = jnp.transpose(lines)[:, 0:1]
    lane = lax.broadcasted_iota(jnp.int32, (1, LANES), 1)
    index = lax.rem(lane, 32).astype(jnp.float32)
    frequency = jnp.exp(index * (-2.0 * math.log(10000.0) / (width // H)))
    sign = jnp.where(lax.rem(lane, 64) < 32, -1.0, 1.0)
    for r in range(tiles):
        at = slice(r * TILE, (r + 1) * TILE)
        within = lax.broadcasted_iota(jnp.int32, (TILE, 1), 0).astype(jnp.float32) + r * TILE
        turned = (within - starts[at]) * frequency
        cos_ref[at, :] = jnp.cos(turned)
        sin_ref[at, :] = jnp.sin(turned) * sign

    def put(product, out, at, table, scale=None):
        for pair in range(width // LANES):
            cols = slice(pair * LANES, (pair + 1) * LANES)
            turned = turn(product[:, cols], *table)
            if scale is not None:
                turned = turned * scale
            out[at, cols] = turned.astype(jnp.bfloat16)

    def lower(block):
        return layer_norm(block.astype(jnp.float32), gain, shift).astype(jnp.bfloat16)

    @pl.loop(0, tiles)
    def _(r):
        at = pl.ds(pl.multiple_of(r * TILE, TILE), TILE)
        table = cos_ref[at, :], sin_ref[at, :]
        h1 = lower(x_ref[at, :])
        h1t_ref[:, at] = jnp.transpose(h1)
        put(nn(h1, wq_ref[...]), q_ref, at, table, score_scale)
        put(nn(h1, wk_ref[...]), ko_ref, at, table)
        vo_ref[at, :] = nn(h1, wv_ref[...]).astype(jnp.bfloat16)

    mask_front(rows, meta_ref, bias, diag)
    for r in range(tiles):
        at = slice(r * TILE, (r + 1) * TILE)

        @pl.when(stream == 0)
        def _(at=at):
            base_ref[at, :] = x_ref[at, :]

        @pl.when(stream == 1)
        def _(r=r, at=at):
            move(r).wait_recv()
            base_ref[at, :] = coming[at, :]

        h1 = lower(base_ref[at, :])
        h1bt_ref[:, at] = jnp.transpose(h1)
        put(nn(h1, wk_ref[...]), kb_ref, at, (cos_ref[at, :], sin_ref[at, :]))
        vb_ref[at, :] = nn(h1, wv_ref[...]).astype(jnp.bfloat16)

        @pl.loop(0, width // LANES)
        def _(pair, r=r):
            cols = pl.ds(pl.multiple_of(pair * LANES, LANES), LANES)
            tile_front(r, pair, cols, q_ref, kb_ref, vb_ref, ko_ref, vo_ref, o_ref, bias, diag, lse)

    lse_ref[...] = jnp.transpose(lse[...])[: lse_ref.shape[0], :]

    @pl.when(stream == 0)
    def _():
        for r in range(tiles):
            move(r).wait_send()


def front(x, gain, shift, lengths, padding, weights, score_scale):
    rows, width = x.shape
    wide = lambda lines, columns: jax.ShapeDtypeStruct((lines, columns), jnp.float32)
    low = jnp.bfloat16
    flat = jax.ShapeDtypeStruct((rows, width), low)
    flipped = jax.ShapeDtypeStruct((width, rows), low)
    vmem = pl.BlockSpec(memory_space=pltpu.VMEM)
    return pl.pallas_call(
        functools.partial(front_kernel, score_scale),
        in_specs=[vmem] * 3 + [pl.BlockSpec(memory_space=pltpu.SMEM)] + [vmem] * 4,
        out_specs=[vmem] * 13,
        out_shape=[flat, flipped, flipped]
        + [flat] * 6
        + [wide(16, rows), wide(8, rows), wide(rows, LANES), wide(rows, LANES)],
        scratch_shapes=front_scratch(rows)
        + [
            pltpu.VMEM((rows, width), low),
            pltpu.SemaphoreType.DMA((rows // TILE,)),
            pltpu.SemaphoreType.DMA((rows // TILE,)),
        ],
        compiler_params=pltpu.CompilerParams(
            collective_id=1, has_side_effects=True, vmem_limit_bytes=62 * MIB
        ),
        cost_estimate=pl.CostEstimate(
            flops=4 * rows * rows * width + 10 * rows * width * width,
            bytes_accessed=20 * MIB,
            transcendentals=0,
        ),
        name="front",
    )(x, gain, shift, lengths, padding, *weights)


def attend(q, kb, vb, ko, vo, meta):
    rows, width = q.shape
    pairs = width // LANES
    spec = pl.BlockSpec((rows, LANES), lambda j: (0, j))
    return pl.pallas_call(
        functools.partial(attend_kernel, rows),
        grid=(pairs,),
        in_specs=[spec] * 5 + [pl.BlockSpec(meta.shape, lambda j: (0, 0))],
        out_specs=[spec, pl.BlockSpec((16, rows), lambda j: (0, 0))],
        out_shape=[
            jax.ShapeDtypeStruct((rows, width), jnp.bfloat16),
            jax.ShapeDtypeStruct((16, rows), jnp.float32),
        ],
        scratch_shapes=front_scratch(rows),
        compiler_params=pltpu.CompilerParams(vmem_limit_bytes=48 * MIB),
        cost_estimate=pl.CostEstimate(
            flops=2 * 2 * rows * rows * width, bytes_accessed=12 * rows * width, transcendentals=0
        ),
        name="attend",
    )(q, kb, vb, ko, vo, meta)


def mask_back(rows, meta_ref, bias, diag):
    columns = jnp.transpose(meta_ref[...])
    for i in range(rows // TILE):
        band = slice(i * TILE, (i + 1) * TILE)
        n = (i + 1) * TILE
        start, limit = meta_ref[0:1, band], meta_ref[1:2, band]
        key = lax.broadcasted_iota(jnp.int32, (n, TILE), 0)
        query = lax.broadcasted_iota(jnp.int32, (n, TILE), 1) + i * TILE
        usable = (columns[:n, 2:3] == 1.0) | (key == query)
        place = key.astype(jnp.float32)
        seen = (place >= start) & (place < limit) & usable
        bias[i][...] = jnp.where(seen, 0.0, masked_score)
        for sub in range(TILE // SUB):
            low = i * TILE + sub * SUB
            part = slice(low, low + SUB)
            key = lax.broadcasted_iota(jnp.int32, (SUB, SUB), 0) + low
            query = lax.broadcasted_iota(jnp.int32, (SUB, SUB), 1) + low
            usable = (columns[part, 2:3] == 1.0) | (key == query)
            same = (key // BLOCK == query // BLOCK) & (
                key.astype(jnp.float32) >= meta_ref[0:1, part]
            )
            seen = same & usable & (meta_ref[3:4, part] == 1.0)
            diag[:, part] = jnp.where(seen, 0.0, masked_score)


def pair_back(
    rows, score_scale, pair, out_cols, tick, q_ref, kb_ref, vb_ref, ko_ref, vo_ref, o_ref, do_ref, lse_ref,
    cos_ref, sin_ref, dq_ref, dkb_ref, dvb_ref, dko_ref, dvo_ref, bias, diag, dk_sum, dv_sum,
):
    head_lane = lax.broadcasted_iota(jnp.int32, (8, LANES), 1)
    head_row = lax.broadcasted_iota(jnp.int32, (8, LANES), 0)
    pick = jnp.where(head_lane // 64 == head_row, 1.0, 0.0).astype(jnp.bfloat16)
    for i in reversed(range(rows // TILE)):
        band = slice(i * TILE, (i + 1) * TILE)
        n = (i + 1) * TILE
        q2 = two_heads(q_ref[band, :])
        do = do_ref[band, :]
        do2 = two_heads(do)
        prod = do.astype(jnp.float32) * o_ref[band, :].astype(jnp.float32)
        high = prod.astype(jnp.bfloat16)
        rest = (prod - high.astype(jnp.float32)).astype(jnp.bfloat16)
        inner = nt(pick, high) + nt(pick, rest)
        inner = jnp.concatenate([inner[0:1], inner[1:2]], axis=1)
        level = jnp.concatenate(
            [lse_ref[pl.ds(2 * pair, 1), band], lse_ref[pl.ds(2 * pair + 1, 1), band]], axis=1
        )
        b = bias[i][...]
        s = nt(kb_ref[:n, :], q2) + jnp.concatenate([b, b], axis=1)
        p = jnp.exp(s - level)
        dp = nt(vb_ref[:n, :], do2)
        ds = (p * (dp - inner)).astype(jnp.bfloat16)
        dv = nn(p.astype(jnp.bfloat16), do2)
        dk = nn(ds, q2)
        if i == rows // TILE - 1:
            dv_sum[...] = dv
            dk_sum[...] = dk
        else:
            dv_sum[:n, :] += dv
            dk_sum[:n, :] += dk
        dq = tn(ds, kb_ref[:n, :])
        extra = []
        for sub in range(TILE // SUB):
            low = i * TILE + sub * SUB
            part = slice(low, low + SUB)
            qs, dos = subs(q2, sub), subs(do2, sub)
            d = diag[:, part]
            at = slice(sub * SUB, (sub + 1) * SUB)
            at2 = slice(TILE + sub * SUB, TILE + (sub + 1) * SUB)
            lev = jnp.concatenate([level[:, at], level[:, at2]], axis=1)
            inn = jnp.concatenate([inner[:, at], inner[:, at2]], axis=1)
            s = nt(ko_ref[part, :], qs) + jnp.concatenate([d, d], axis=1)
            p = jnp.exp(s - lev)
            dp = nt(vo_ref[part, :], dos)
            ds = (p * (dp - inn)).astype(jnp.bfloat16)
            dvo_ref[part, out_cols] = nn(p.astype(jnp.bfloat16), dos).astype(jnp.bfloat16)
            dko = nn(ds, qs)
            dko_ref[part, out_cols] = turn(dko, cos_ref[part, :], -sin_ref[part, :]).astype(jnp.bfloat16)
            extra.append(tn(ds, ko_ref[part, :]))
        dq = dq + jnp.concatenate(
            [extra[0][:SUB], extra[1][:SUB], extra[0][SUB:], extra[1][SUB:]], axis=0
        )
        dq = one_row(dq) * score_scale
        dq_ref[band, out_cols] = turn(dq, cos_ref[band, :], -sin_ref[band, :]).astype(jnp.bfloat16)
        tick(rows // TILE - i)
    dvb_ref[:, out_cols] = dv_sum[...].astype(jnp.bfloat16)
    dkb_ref[:, out_cols] = turn(dk_sum[...], cos_ref[...], -sin_ref[...]).astype(jnp.bfloat16)


def attend_back_kernel(
    rows, score_scale, q_ref, kb_ref, vb_ref, ko_ref, vo_ref, o_ref, do_ref, lse_ref, meta_ref, cos_ref, sin_ref,
    *refs,
):
    pair = pl.program_id(0)
    dq_ref, dkb_ref, dvb_ref, dko_ref, dvo_ref, *bias, diag, dk_sum, dv_sum = refs
    pl.when(pair == 0)(lambda: mask_back(rows, meta_ref, bias, diag))
    pair_back(
        rows, score_scale, pair, slice(None), lambda slot: None, q_ref, kb_ref, vb_ref, ko_ref, vo_ref, o_ref,
        do_ref, lse_ref, cos_ref, sin_ref, dq_ref, dkb_ref, dvb_ref, dko_ref, dvo_ref, bias, diag, dk_sum,
        dv_sum,
    )


def back_scratch(rows):
    return [pltpu.VMEM(((i + 1) * TILE, TILE), jnp.float32) for i in range(rows // TILE)] + [
        pltpu.VMEM((SUB, rows), jnp.float32),
        pltpu.VMEM((rows, LANES), jnp.float32),
        pltpu.VMEM((rows, LANES), jnp.float32),
    ]


def attend_back(q, kb, vb, ko, vo, o, do, lse, meta, cosine, sine, score_scale):
    rows, width = q.shape
    pairs = width // LANES
    spec = pl.BlockSpec((rows, LANES), lambda j: (0, j))
    whole = lambda a: pl.BlockSpec(a.shape, lambda j: (0, 0))
    return pl.pallas_call(
        functools.partial(attend_back_kernel, rows, score_scale),
        grid=(pairs,),
        in_specs=[spec] * 7 + [whole(lse), whole(meta), whole(cosine), whole(sine)],
        out_specs=[spec] * 5,
        out_shape=[jax.ShapeDtypeStruct((rows, width), jnp.bfloat16)] * 5,
        scratch_shapes=back_scratch(rows),
        compiler_params=pltpu.CompilerParams(vmem_limit_bytes=48 * MIB),
        cost_estimate=pl.CostEstimate(
            flops=5 * 2 * rows * rows * width, bytes_accessed=24 * rows * width, transcendentals=0
        ),
        name="attend_back",
    )(q, kb, vb, ko, vo, o, do, lse, meta, cosine, sine)


F1, OUT, F2, P0, P1, P2, N = range(7)
TAIL_STREAMS = (
    ("lyxh", 1024), ("xylh", 384), ("yxlh", 1024), ("xylh", 384), ("xylh", 384), ("ylhx", 384), ("lyhx", 128),
)
TAIL_FAR = 3
FEEDS = (F1, F2)
TAIL_TICKS = {
    (0, 3): [(F2, 0)],
    (1, 1): [(OUT, 0)],
    (1, 2): [(F1, 0)],
    (2, 2): [(OUT, 1), (P0, 0)],
    (3, 3): [(F2, 1)],
    (3, 5): [(OUT, 2), (P0, 1)],
    (4, 1): [(F1, 1)],
    (4, 2): [(P1, 0)],
    (4, 3): [(OUT, 3)],
    (5, 1): [(P0, 2), (F2, 2)],
    (5, 3): [(OUT, 4)],
    (5, 5): [(P0, 3), (P1, 1), (F1, 2)],
}
TAIL_POST = {
    0: [(F2, 3)],
    1: [(P2, 0)],
    2: [(P0, 4)],
    3: [(P1, 2)],
    4: [(F1, 3)],
    5: [(F2, 4), (N, 0), (P1, 3)],
    6: [(P2, 1), (N, 1), (F1, 4), (P1, 4), (N, 2), (P2, 2)],
    7: [(N, 3), (P2, 3), (N, 4)],
    8: [(P2, 4)],
}


def normalized(x):
    x = x.astype(jnp.float32)
    centre = x - jnp.mean(x, axis=-1, keepdims=True)
    inverse = lax.rsqrt(jnp.mean(centre * centre, axis=-1, keepdims=True) + epsilon)
    return centre * inverse, inverse


def normal_back(grad, gain, n, inverse):
    e = grad * gain
    return inverse * (
        e - jnp.mean(e, axis=-1, keepdims=True) - n * jnp.mean(e * n, axis=-1, keepdims=True)
    )


def tail_kernel(
    rows, score_scale, q_ref, kb_ref, vb_ref, ko_ref, vo_ref, o_ref, do_ref, lse_ref, meta_ref, cos_ref, sin_ref,
    h1t_ref, h1bt_ref, gain_ref, norm_ref, first_ref, *refs,
):
    pair = pl.program_id(0)
    hbm, refs = refs[:6], refs[6:]
    ff_ref, go_ref, refs = refs[0], refs[1], refs[2:]
    out_ref, up_out, down_out, head_out, norm_out, refs = *refs[:5], refs[5:]
    scratch, refs = refs[:7], refs[7:]
    bias, (diag, dk_sum, dv_sum) = scratch[:4], scratch[4:]
    dq, dkb, dvb, dko, dvo, refs = *refs[:5], refs[5:]
    held, refs = refs[:5], refs[5:]
    wq, wk, wv, x, base = held
    coming, pair_sums, norm_sums, refs = refs[0], refs[1:4], refs[4], refs[5:]
    load_sem, send_sem, recv_sem, refs = refs[0], refs[1], refs[2], refs[3:]
    sources = [(ff_ref.at[1], 0), (go_ref, 0), (ff_ref.at[2], 0)]
    sources += [(ref, 0) for ref in (*pair_sums, norm_sums)]
    scatter = Scatter(TAIL_STREAMS, sources, refs, TAIL_FAR)
    stream = lax.axis_index("stream")
    tiles = rows // TILE
    width = x.shape[1]
    loads = [
        pltpu.make_async_copy(src, dst, load_sem.at[i])
        for i, (src, dst) in enumerate(zip(hbm, (*held, out_ref)))
    ]

    def tick(slot):
        for at, moves in TAIL_TICKS.items():
            if at[1] == slot:
                @pl.when(pair == at[0])
                def _(moves=moves):
                    for number, index in moves:
                        scatter.step(number, index)

    def post(slot):
        for number, index in TAIL_POST.get(slot, ()):
            scatter.step(number, index)

    @pl.when(pair == 0)
    def _():
        scatter.greet()
        scatter.open((F2, OUT, F1))
        for load in loads:
            load.start()
        mask_back(rows, meta_ref, bias, diag)

    cols = pl.ds(pl.multiple_of(pair * LANES, LANES), LANES)
    pair_back(
        rows, score_scale, pair, cols, tick, q_ref, kb_ref, vb_ref, ko_ref, vo_ref, o_ref,
        do_ref, lse_ref, cos_ref, sin_ref, dq, dkb, dvb, dko, dvo, bias, diag, dk_sum, dv_sum,
    )

    for number, sums in enumerate(pair_sums):
        @pl.when(pair == 2 * number + 1)
        def _(number=number, sums=sums):
            both = slice(2 * number * LANES, (2 * number + 2) * LANES)
            for at, block in enumerate((
                nn(h1t_ref[...], dq[:, both]),
                nn(h1t_ref[...], dko[:, both]) + nn(h1bt_ref[...], dkb[:, both]),
                nn(h1t_ref[...], dvo[:, both]) + nn(h1bt_ref[...], dvb[:, both]),
            )):
                block = block.astype(jnp.bfloat16)
                for half in range(2):
                    sums[half, :, :, :, :, :, at * LANES : (at + 1) * LANES] = block[
                        :, half * LANES : (half + 1) * LANES
                    ].reshape(2, 2, 2, 2, RUN, LANES)
            scatter.open((P0 + number,))

    tick(tiles + 1)

    @pl.when(pair == pl.num_programs(0) - 1)
    def _():
        for load in loads:
            load.wait()
        gain = gain_ref[...].reshape(1, width)

        def band(r):
            return slice(r * TILE, (r + 1) * TILE)

        def move(r):
            return pltpu.make_async_remote_copy(
                src_ref=dkb.at[band(r)],
                dst_ref=coming.at[band(r)],
                send_sem=send_sem.at[r],
                recv_sem=recv_sem.at[r],
                device_id=scatter.to["x"],
                device_id_type=MESH,
            )

        gain_sum = jnp.zeros((1, width), jnp.float32)
        bias_sum = jnp.zeros((1, width), jnp.float32)
        for r in range(tiles):
            at = band(r)
            grad = nt(dkb[at, :], wk[...]) + nt(dvb[at, :], wv[...])
            dkb[at, :] = grad.astype(jnp.bfloat16)
            pl.when(stream == 1)(lambda r=r: move(r).start())
            n, _ = normalized(base[at, :])
            gain_sum += jnp.sum(grad * n, axis=0, keepdims=True)
            bias_sum += jnp.sum(grad, axis=0, keepdims=True)
        post(0)
        for r in range(tiles):
            at = band(r)
            grad = nt(dq[at, :], wq[...]) + nt(dko[at, :], wk[...]) + nt(dvo[at, :], wv[...])
            n, inverse = normalized(x[at, :])
            gain_sum += jnp.sum(grad * n, axis=0, keepdims=True)
            bias_sum += jnp.sum(grad, axis=0, keepdims=True)
            grad = grad + jnp.where(stream == 0, dkb[at, :].astype(jnp.float32), 0.0)
            out_ref[at, :] += normal_back(grad, gain, n, inverse)
            post(r + 1)
        eye = jnp.where(
            lax.broadcasted_iota(jnp.int32, (8, LANES), 0)
            == lax.broadcasted_iota(jnp.int32, (8, LANES), 1),
            1.0,
            0.0,
        ).astype(jnp.bfloat16)
        zero = jnp.zeros((6, width), jnp.float32)
        for half, sums in enumerate((
            jnp.concatenate([gain_sum, bias_sum, zero], axis=0), norm_ref[...]
        )):
            block = tn(sums.astype(jnp.bfloat16), eye).astype(jnp.bfloat16)
            norm_sums[half] = block.reshape(2, 2, 2, 2, RUN, LANES)
        scatter.open((N,))
        post(tiles + 1)
        for r in range(tiles):
            at = band(r)

            @pl.when(stream == 1)
            def _(r=r):
                move(r).wait_send()

            @pl.when(stream == 0)
            def _(r=r, at=at):
                move(r).wait_recv()
                n, inverse = normalized(x[at, :])
                out_ref[at, :] += normal_back(coming[at, :].astype(jnp.float32), gain, n, inverse)

            post(tiles + 2 + r)
        scatter.finish()
        places = [sum(part for _, part in TAIL_STREAMS[:i]) for i in range(len(TAIL_STREAMS))]
        for half, out in enumerate((up_out, down_out)):
            out[:, : first_ref.shape[2]] = first_ref[half]
            low = first_ref.shape[2]
            for number in FEEDS:
                part = TAIL_STREAMS[number][1]
                out[:, low : low + part] = scatter.result(half, places[number], part)
                low += part
        middle = width // 2
        for half in range(2):
            head_out[0, :, half * middle : (half + 1) * middle] = scatter.result(
                half, places[OUT], middle
            )
            norm_out[half] = scatter.result(half, places[N], LANES)
            for number in range(len(pair_sums)):
                low = (2 * number + half) * LANES
                for at in range(3):
                    head_out[1 + at, :, low : low + LANES] = scatter.result(
                        half, places[P0 + number] + at * LANES, LANES
                    )


def tail(
    operands, h1t, h1bt, gain, norm, first, weights, x, base, middle_grad, ff, go, score_scale
):
    rows, width = x.shape
    pairs = width // LANES
    hidden = first.shape[2] + sum(TAIL_STREAMS[number][1] for number in FEEDS)
    shapes = [(rows, width), (24, hidden), (24, hidden), (4, 24, width), (2, 24, LANES)]
    spec = pl.BlockSpec((rows, LANES), lambda j: (0, j))
    once = pl.Buffered(1)
    whole = lambda shape: pl.BlockSpec(shape, lambda j: (0,) * len(shape), pipeline_mode=once)
    flat, square = (rows, width), (width, width)
    low = jnp.bfloat16
    scratch = back_scratch(rows)
    scratch += [pltpu.VMEM(flat, low)] * 5
    scratch += [pltpu.VMEM(square, low)] * 3 + [pltpu.VMEM(flat, low)] * 2
    scratch += [pltpu.VMEM(flat, low)]
    scratch += [pltpu.VMEM((2, 2, 2, 2, 2, RUN, 3 * LANES), low)] * 3
    scratch += [pltpu.VMEM((2, 2, 2, 2, 2, RUN, LANES), low)]
    scratch += [pltpu.SemaphoreType.DMA((6,))]
    scratch += [pltpu.SemaphoreType.DMA((rows // TILE,))] * 2
    scratch += Scatter.shapes(TAIL_STREAMS, TAIL_FAR)
    return pl.pallas_call(
        functools.partial(tail_kernel, rows, score_scale),
        grid=(pairs,),
        in_specs=[spec] * 7
        + [whole(a.shape) for a in (*operands[7:], h1t, h1bt, gain, norm, first)]
        + [pl.BlockSpec(memory_space=pl.ANY)] * 8,
        out_specs=[whole(shape) for shape in shapes],
        out_shape=[jax.ShapeDtypeStruct(shape, jnp.float32) for shape in shapes],
        scratch_shapes=scratch,
        compiler_params=pltpu.CompilerParams(
            collective_id=0, has_side_effects=True, vmem_limit_bytes=63 * MIB
        ),
        cost_estimate=pl.CostEstimate(
            flops=10 * rows * rows * width + 20 * rows * width * width,
            bytes_accessed=40 * MIB,
            transcendentals=0,
        ),
        name="tail",
    )(*operands, h1t, h1bt, gain, norm, first, *weights, x, base, middle_grad, ff, go)


FEED_TILE = 1024
FEED_STREAMS = (("yxlh", 512), ("xylh", 512))
FEED_TICKS = {
    (1, 1): [(0, 0), (1, 0)], (1, 5): [(0, 1), (1, 1)], (2, 1): [(0, 2), (1, 2)], (2,5): [(0, 3), (1, 3)], (2,6): [(0, 4), (1, 4)],
}


def feed_kernel(
    streams, x_ref, o_ref, dy_ref, wo_ref, gain_ref, shift_ref, wu_ref, wd_ref,
    y_ref, do_ref, dx_ref, norm_ref, ff_ref, go_ref, *refs,
):
    f = pl.program_id(0)
    rows, width = x_ref.shape
    gain, shift = gain_ref[...].reshape(1, width), shift_ref[...].reshape(1, width)
    scatter = None
    if streams:
        out_ref, refs = refs[0], refs[1:]
    total, normal, scale, h2s, h2t, dyt, gs, dus = refs[:8]
    if streams:
        first = refs[8]
        sources, low = [], 0
        for _, part in streams:
            sources.append((first, low))
            low += part
        scatter = Scatter(streams, sources, refs[9:], 0)

    def tick(slot):
        if scatter is None:
            return
        for at, moves in FEED_TICKS.items():
            if at[1] == slot:
                @pl.when(f == at[0])
                def _(moves=moves):
                    for stream, index in moves:
                        scatter.step(stream, index)

    def band(r):
        return pl.ds(pl.multiple_of(r * TILE, TILE), TILE)

    @pl.when(f == 0)
    def _():
        if scatter is not None:
            scatter.greet()
        norm_ref[...] = jnp.zeros_like(norm_ref)

        @pl.loop(0, rows // TILE)
        def _(r):
            at = band(r)
            x1 = x_ref[at, :].astype(jnp.float32) + nn(o_ref[at, :], wo_ref[...])
            centre = x1 - jnp.mean(x1, axis=-1, keepdims=True)
            inverse = lax.rsqrt(jnp.mean(centre * centre, axis=-1, keepdims=True) + epsilon)
            n = centre * inverse
            h2 = (n * gain + shift).astype(jnp.bfloat16)
            total[at, :] = x1
            normal[at, :] = n
            scale[at, :] = jnp.broadcast_to(inverse, (TILE, LANES))
            h2s[at, :] = h2
            h2t[:, at] = jnp.transpose(h2)
            dyt[:, at] = jnp.transpose(dy_ref[at, :])
            dx_ref[at, :] = jnp.zeros((TILE, width), jnp.float32)

    for r in range(rows // TILE):
        at = band(r)
        u = nn(h2s[at, :], wu_ref[...])
        square = u * u
        curve = jnp.tanh(0.7978845608028654 * u * (1.0 + 0.044715 * square))
        upper = 0.5 * (1.0 + curve)
        g = (u * upper).astype(jnp.bfloat16)
        slope = upper + u * upper * (1.0 - curve) * (
            0.7978845608028654 + 3 * 0.044715 * 0.7978845608028654 * square
        )
        gs[at, :] = g
        total[at, :] += nn(g, wd_ref[...])
        du = (nt(dy_ref[at, :], wd_ref[...]) * slope).astype(jnp.bfloat16)
        dus[at, :] = du
        dx_ref[at, :] += nt(du, wu_ref[...])
        tick(r)
    slot = rows // TILE
    for half, (left, right) in enumerate(((h2t, dus), (dyt, gs))):
        for c in range(right.shape[1] // TILE):
            cols = pl.ds(c * TILE, TILE)
            block = nn(left[...], right[:, cols]).astype(jnp.bfloat16)
            block = block.reshape(2, 2, 2, 2, RUN, TILE)
            ff_ref[0, half, :, :, :, :, :, cols] = block
        tick(slot + half)
    if scatter is not None:
        @pl.when(f == 0)
        def _():
            @pl.loop(0, 32)
            def _(i):
                at = (i // 16, i // 8 % 2, i // 4 % 2, i // 2 % 2, i % 2)
                first[at] = ff_ref[(0,) + at]

            scatter.open(range(len(streams)))

    @pl.when(f == pl.num_programs(0) - 1)
    def _():
        @pl.loop(0, rows // TILE)
        def _(r):
            at = band(r)
            y_ref[at, :] = total[at, :].astype(jnp.bfloat16)
            n = normal[at, :]
            dh2 = dx_ref[at, :]
            norm_ref[0:1, :] += jnp.sum(dh2 * n, axis=0, keepdims=True)
            norm_ref[1:2, :] += jnp.sum(dh2, axis=0, keepdims=True)
            e = dh2 * gain
            e = (
                e
                - jnp.mean(e, axis=-1, keepdims=True)
                - n * jnp.mean(e * n, axis=-1, keepdims=True)
            )
            dx = dy_ref[at, :].astype(jnp.float32) + scale[at, 0:1] * e
            dx_ref[at, :] = dx
            da = dx.astype(jnp.bfloat16)
            dyt[:, at] = jnp.transpose(da)
            do_ref[at, :] = nt(da, wo_ref[...]).astype(jnp.bfloat16)

        middle = width // 2
        for half in range(2):
            block = nn(dyt[...], o_ref[:, half * middle : (half + 1) * middle])
            go_ref[half] = block.astype(jnp.bfloat16).reshape(2, 2, 2, 2, RUN, middle)
        tick(slot + 2)
        if scatter is not None:
            scatter.finish()
            for half in range(2):
                out_ref[half] = scatter.result(half, 0, out_ref.shape[2])


def feed(x, o, dy, wo, gain, shift, wu, wd, streams):
    rows, width = x.shape
    tiles = wu.shape[1] // FEED_TILE
    once = pl.Buffered(1)
    whole = lambda shape: pl.BlockSpec(shape, lambda f: (0,) * len(shape), pipeline_mode=once)
    flat, square = (rows, width), (width, width)
    parts = (2, 2, 2, 2, RUN)
    out_specs = [
        whole(flat),
        whole(flat),
        whole(flat),
        whole((8, width)),
        pl.BlockSpec((1, 2) + parts + (FEED_TILE,), lambda f: (f,) + (0,) * 7),
        whole((2,) + parts + (width // 2,)),
    ]
    out_shape = [
        jax.ShapeDtypeStruct(flat, jnp.bfloat16),
        jax.ShapeDtypeStruct(flat, jnp.bfloat16),
        jax.ShapeDtypeStruct(flat, jnp.float32),
        jax.ShapeDtypeStruct((8, width), jnp.float32),
        jax.ShapeDtypeStruct((tiles, 2) + parts + (FEED_TILE,), jnp.bfloat16),
        jax.ShapeDtypeStruct((2,) + parts + (width // 2,), jnp.bfloat16),
    ]
    scratch = [
        pltpu.VMEM(flat, jnp.float32),
        pltpu.VMEM(flat, jnp.float32),
        pltpu.VMEM((rows, LANES), jnp.float32),
        pltpu.VMEM(flat, jnp.bfloat16),
        pltpu.VMEM((width, rows), jnp.bfloat16),
        pltpu.VMEM((width, rows), jnp.bfloat16),
        pltpu.VMEM((rows, FEED_TILE), jnp.bfloat16),
        pltpu.VMEM((rows, FEED_TILE), jnp.bfloat16),
    ]
    options = {}
    if streams:
        out_specs += [whole((2, 24, FEED_TILE))]
        out_shape += [jax.ShapeDtypeStruct((2, 24, FEED_TILE), jnp.float32)]
        scratch += [pltpu.VMEM((2,) + parts + (FEED_TILE,), jnp.bfloat16)]
        scratch += Scatter.shapes(streams, 0)
        options = {"collective_id": 2, "has_side_effects": True}
    return pl.pallas_call(
        functools.partial(feed_kernel, streams),
        grid=(tiles,),
        in_specs=[
            whole(flat),
            whole(flat),
            whole(flat),
            whole(square),
            whole(gain.shape),
            whole(shift.shape),
            pl.BlockSpec((width, FEED_TILE), lambda f: (0, f)),
            pl.BlockSpec((FEED_TILE, width), lambda f: (f, 0)),
        ],
        out_specs=out_specs,
        out_shape=out_shape,
        scratch_shapes=scratch,
        compiler_params=pltpu.CompilerParams(vmem_limit_bytes=62 * MIB, **options),
        cost_estimate=pl.CostEstimate(
            flops=12 * rows * width * wu.shape[1] + 6 * rows * width * width,
            bytes_accessed=30 * MIB,
            transcendentals=0,
        ),
        name="feed",
    )(x, o, dy, wo, gain, shift, wu, wd)


def settle_kernel(y, t, up, heads, norms, *refs):
    y_out, t_out, first, q, k, v, second, up_out = refs
    y_out[...] = y[...]
    t_out[...] = t[...]

    @pl.when(pl.program_id(0) == 0)
    def _():
        up_out[...] = up[...]
        for number, ref in enumerate((q, k, v)):
            ref[...] = heads[1 + number]
        first[...] = jnp.transpose(norms[0])[:2, :]
        second[...] = jnp.transpose(norms[1])[:2, :]


def settle(y, t, up, heads, norms):
    wide = lambda *shape: jax.ShapeDtypeStruct(shape, jnp.float32)
    lines = up.shape[0]
    rows, width = y.shape
    band = pl.BlockSpec((rows // 4, width), lambda r: (r, 0))
    whole = lambda shape: pl.BlockSpec(shape, lambda r: (0,) * len(shape))
    head = wide(lines, width)
    pair = wide(2, lines)
    small = [pair, head, head, head, pair, wide(*up.shape)]
    return pl.pallas_call(
        settle_kernel,
        grid=(4,),
        in_specs=[band, band, whole(up.shape), whole(heads.shape), whole(norms.shape)],
        out_specs=[band, band] + [whole(part.shape) for part in small],
        out_shape=[jax.ShapeDtypeStruct(y.shape, y.dtype), wide(rows, width)] + small,
        compiler_params=pltpu.CompilerParams(vmem_limit_bytes=63 * MIB),
        name="settle",
    )(y, t, up, heads, norms)


def shards(
    tokens,
    lengths,
    pad_mask,
    first_gain,
    first_bias,
    query_weight,
    key_weight,
    value_weight,
    out_weight,
    second_gain,
    second_bias,
    up_weight,
    down_weight,
    output_grad,
):
    total_rows = tokens.shape[1]
    model_width = tokens.shape[2]
    head_width = model_width // H
    score_scale = head_width ** (-0.5)
    is_noisy = lax.axis_index("stream") == 1
    own = tokens[0]
    weights = (query_weight, key_weight, value_weight)
    ring = lax.axis_size("dp") == 16 and lax.axis_size("stream") == 2
    if ring:
        base, h1t, h1bt, q, kb, vb, ko, vo, mixed_low, lse, meta, cosine, sine = front(
            own, first_gain, first_bias, lengths, pad_mask[None], weights, score_scale
        )
    else:
        places, first_place = layout(lengths[0], total_rows, lengths.shape[1])
        limit = (places // BLOCK + jnp.where(is_noisy, 0, 1)) * BLOCK
        noisy_row = jnp.broadcast_to(jnp.where(is_noisy, 1, 0), places.shape)
        blank = jnp.zeros_like(places)
        meta = jnp.stack(
            [first_place, limit, pad_mask, noisy_row, blank, blank, blank, blank]
        ).astype(jnp.float32)
        cosine, sine = angle_tables(places - first_place, head_width)
        far = lax.ppermute(own, "stream", [(0, 1)])
        base = jnp.where(is_noisy, far, own)
        norms = (first_gain, first_bias)
        h1t, q, ko, vo = project(own, *norms, cosine, sine, weights, score_scale)
        h1bt, kb, vb = project(base, *norms, cosine, sine, weights[1:], score_scale)
        mixed_low, lse = attend(q, kb, vb, ko, vo, meta)

    fed = feed(
        own, mixed_low, output_grad[0], out_weight, second_gain, second_bias, up_weight, down_weight, FEED_STREAMS if ring else (),
    )
    layer_output, mixed_grad, middle_grad, norm_sums, ff_part, out_part = fed[:6]
    layer_output = layer_output[None]
    operands = (q, kb, vb, ko, vo, mixed_low, mixed_grad, lse, meta, cosine, sine)
    if ring:
        tokens_grad, up_grad, down_grad, heads, norms = tail(
            operands, h1t, h1bt, first_gain, norm_sums, fed[6], weights, own, base, middle_grad, ff_part,
            out_part, score_scale,
        )
        y, t, first, q, k, v, second, up = settle(fed[0], tokens_grad, up_grad, heads, norms)
        return (y[None], t[None], first, q, k, v, heads[0].T, second, up, down_grad.T)
    else:
        dq, dkb, dvb, dko, dvo = attend_back(*operands, score_scale)
        base_grad = nt(dkb, key_weight) + nt(dvb, value_weight)
        back = lax.ppermute(base_grad.astype(jnp.bfloat16), "stream", [(1, 0)])
        normed_grad = (
            nt(dq, query_weight)
            + nt(dko, key_weight)
            + nt(dvo, value_weight)
            + jnp.where(is_noisy, 0.0, base_grad + back.astype(jnp.float32))
        )
        inputs = own.astype(jnp.float32)
        first_pull = jax.vjp(layer_norm, inputs, first_gain, first_bias)[1]
        input_part, first_gain_part, first_bias_part = first_pull(normed_grad)
        tokens_grad = (middle_grad + input_part)[None]
        ff_part = ff_part.reshape(-1, 2, model_width, FEED_TILE)
        out_part = out_part.reshape(2, model_width, model_width // 2)
        norm_part = jnp.stack(
            [first_gain_part, first_bias_part, norm_sums[0], norm_sums[1]], axis=1
        )
        part = jnp.concatenate(
            [ff_part[f, i] for i in range(2) for f in range(ff_part.shape[0])]
            + [out_part[0], out_part[1], nn(h1t, dq).astype(jnp.bfloat16)]
            + [(nn(h1t, dko) + nn(h1bt, dkb)).astype(jnp.bfloat16)]
            + [(nn(h1t, dvo) + nn(h1bt, dvb)).astype(jnp.bfloat16)]
            + [jnp.pad(norm_part, ((0, 0), (0, LANES - 4))).astype(jnp.bfloat16)],
            axis=1,
        )
        part = lax.psum_scatter(part, ("stream", "dp"), scatter_dimension=0, tiled=True)
        part = part.astype(jnp.float32)
        hidden_width = up_weight.shape[1]
        cuts = (hidden_width, hidden_width) + (model_width,) * 4 + (LANES,)
        pieces, low = [], 0
        for cut in cuts:
            pieces.append(part[:, low : low + cut])
            low += cut
        up_grad, down_grad, out_grad, query_grad, key_grad, value_grad, norms = pieces
        first_grads, second_grads = norms[:, :2].T, norms[:, 2:4].T
    return (
        layer_output,
        tokens_grad,
        first_grads,
        query_grad,
        key_grad,
        value_grad,
        out_grad.T,
        second_grads,
        up_grad,
        down_grad.T,
    )


def solution(mesh):
    placed = (
        P("stream", "dp", None),
        P("dp", None),
        P("dp"),
        P(),
        P(),
        P(),
        P(),
        P(),
        P(),
        P(),
        P(),
        P(),
        P(),
        P("stream", "dp", None),
    )
    return jax.shard_map(
        shards,
        mesh=mesh,
        in_specs=placed,
        out_specs=(
            P("stream", "dp", None),
            P("stream", "dp", None),
            P(None, ("stream", "dp")),
            P(("stream", "dp"), None),
            P(("stream", "dp"), None),
            P(("stream", "dp"), None),
            P(None, ("stream", "dp")),
            P(None, ("stream", "dp")),
            P(("stream", "dp"), None),
            P(None, ("stream", "dp")),
        ),
        check_vma=False,
    )
```

```python
import functools
import math

import jax
import jax.numpy as jnp
from jax import lax
from jax.experimental import pallas as pl
from jax.experimental.pallas import tpu as pltpu
from jax.sharding import PartitionSpec as P

H = 12
BLOCK = 16
TILE = 256
SUB = 128
LANES = 128

epsilon = 1e-05
masked_score = -1e30
MIB = 1024 * 1024


def layer_norm(values, gain_row, bias_row):
    centre = values - jnp.mean(values, axis=-1, keepdims=True)
    spread = jnp.mean(centre * centre, axis=-1, keepdims=True)
    return centre * lax.rsqrt(spread + epsilon) * gain_row + bias_row


def layout(lengths_row, total_rows, doc_slots):
    places = jnp.arange(total_rows, dtype=jnp.int32)
    end_places = jnp.cumsum(lengths_row)
    starts = end_places - lengths_row
    document = jnp.sum((places[:, None] >= end_places[None, :]).astype(jnp.int32), axis=1)
    picked = document[:, None] == jnp.arange(doc_slots, dtype=jnp.int32)[None, :]
    first_place = jnp.sum(jnp.where(picked, starts[None, :], 0), axis=1)
    return (places, first_place)


def angle_tables(position, head_width):
    half_width = head_width // 2
    freq_index = (jnp.arange(half_width)).astype(jnp.float32)
    frequency = jnp.exp(freq_index * (-2.0 * math.log(10000.0) / head_width))
    turned = position.astype(jnp.float32)[:, None] * frequency[None, :]
    cosine, sine = jnp.cos(turned), jnp.sin(turned)
    return (
        jnp.concatenate([cosine] * 4, axis=1),
        jnp.concatenate([-sine, sine, -sine, sine], axis=1),
    )


def turn(values, cosine, sine):
    lane = lax.broadcasted_iota(jnp.int32, values.shape, 1)
    low = lax.rem(lane, 64) < 32
    partner = jnp.where(low, pltpu.roll(values, LANES - 32, 1), pltpu.roll(values, 32, 1))
    return values * cosine + partner * sine


def nt(left, right):
    return lax.dot_general(
        left, right, (((1,), (1,)), ((), ())), preferred_element_type=jnp.float32
    )


def tn(left, right):
    return lax.dot_general(
        left, right, (((0,), (0,)), ((), ())), preferred_element_type=jnp.float32
    )


def nn(left, right):
    return jnp.dot(left, right, preferred_element_type=jnp.float32)


MESH = pl.DeviceIdType.MESH
RUN = 48


class Scatter:
    @staticmethod
    def shapes(streams, far):
        total = sum(width for _, width in streams)
        shapes = [
            pltpu.VMEM((2, 2, 2, 2, RUN, total), jnp.bfloat16),
            pltpu.VMEM((2, 24, total), jnp.float32),
            pltpu.VMEM((24, total), jnp.float32),
        ]
        for number, (order, width) in enumerate(streams):
            if number < far:
                shapes += [pltpu.VMEM((2, 2, 2, 2, RUN, width), jnp.bfloat16)]
            for left in range(len(order) - 1, -1, -1):
                shapes += [pltpu.VMEM((2,) * left + (RUN, width), jnp.bfloat16)]
        count = sum(1 + len(order) for order, _ in streams) + 1
        return shapes + [
            pltpu.SemaphoreType.DMA((count,)),
            pltpu.SemaphoreType.DMA((count,)),
            pltpu.SemaphoreType.DMA((len(streams),)),
        ]

    def __init__(self, streams, sources, refs, far):
        self.far = far
        self.sib, self.fin, self.other = refs[:3]
        self.bufs = list(refs[3:-3])
        self.send, self.recv, self.local = refs[-3:]
        s, d = lax.axis_index("stream"), lax.axis_index("dp")
        self.core = d % 2
        self.mine = {"x": s, "y": d // 2 % 2, "l": d // 4 % 2, "h": d // 8}
        self.to = {
            "x": {"stream": 1 - s},
            "y": {"dp": d + 2 - 4 * self.mine["y"]},
            "l": {"dp": d + 4 - 8 * self.mine["l"]},
            "h": {"dp": d + 8 - 16 * self.mine["h"]},
            "core": {"dp": d + 1 - 2 * self.core},
        }
        self.used = 0
        self.streams = []
        place = 0
        for (order, width), (source, low) in zip(streams, sources):
            self.streams.append(self.stream(order, place, width, source, low))
            place += width
        self.last = self.take()

    def take(self):
        self.used += 1
        return self.used - 1

    def copy(self, src, dst, k, to):
        return pltpu.make_async_remote_copy(
            src_ref=src,
            dst_ref=dst,
            send_sem=self.send.at[k],
            recv_sem=self.recv.at[k],
            device_id=self.to[to],
            device_id_type=MESH,
        )

    def greet(self):
        barrier = pltpu.get_barrier_semaphore()
        for to in self.to.values():
            pl.semaphore_signal(barrier, inc=1, device_id=to, device_id_type=MESH)
        pl.semaphore_wait(barrier, len(self.to))

    @staticmethod
    def add(dst, left, right):
        lead = dst.shape[:-2]
        count = math.prod(lead)

        def one(index):
            at = []
            for size in reversed(lead):
                at.append(index % size)
                index = index // size
            at = tuple(reversed(at))
            dst[at] = left[at] + right[at]

        if count == 1:
            one(0)
        else:
            pl.loop(0, count, unroll=min(count, 4))(one)

    def stream(self, order, place, width, source, low):
        number = len(self.streams)
        cols = pl.ds(place, width)
        every = (slice(None),) * 5
        src = self.sib.at[every + (cols,)]
        k = self.take()
        part = lambda core: source.at[(core,) + every + (pl.ds(low, width),)]
        swap = lambda src=src, k=k: self.copy(part(1 - self.core), src, k, "core")
        near = None
        if number < self.far:
            held = self.bufs.pop(0)
            near = lambda: pltpu.make_async_copy(part(self.core), held, self.local.at[number])

        def opening(src=src):
            swap().wait()
            if near is None:
                self.add(src, src, part(self.core))
            else:
                near().wait()
                self.add(src, src, held)

        steps = []
        pending = opening
        names = ["x", "h", "l", "y"]
        for axis in order:
            at = names.index(axis)
            names.pop(at)
            buf = self.bufs.pop(0)
            k = self.take()
            pick = lambda index, src=src, at=at: src.at[(slice(None),) * at + (index,)]
            make = lambda pick=pick, buf=buf, k=k, axis=axis: self.copy(
                pick(1 - self.mine[axis]), buf, k, axis
            )

            def begin(before=pending, make=make):
                before()
                make().start()

            def end(pick=pick, buf=buf, make=make, axis=axis):
                make().wait()
                self.add(buf, buf, pick(self.mine[axis]))

            steps.append(begin)
            pending = end
            src = buf

        def close(before=pending, src=src):
            before()
            for core in range(2):
                self.fin[core, :, cols] = src[24 * core : 24 * core + 24, :].astype(jnp.float32)

        steps.append(close)
        return (swap, near, steps)

    def open(self, order):
        for index in order:
            swap, near, _ = self.streams[index]
            swap().start()
            if near is not None:
                near().start()

    def step(self, stream, index):
        self.streams[stream][2][index]()

    def finish(self):
        last = self.copy(self.fin.at[1 - self.core], self.other, self.last, "core")
        last.start()
        last.wait()

    def result(self, half, place, width):
        cols = slice(place, place + width)
        return jnp.where(self.core == half, self.fin[half, :, cols], self.other[:, cols])


def project_kernel(score_scale, x_ref, gain_ref, shift_ref, cos_ref, sin_ref, *refs):
    count = (len(refs) - 1) // 2
    weights, outs = refs[:count], refs[count:]
    gain, shift = (ref[...].reshape(1, x_ref.shape[1]) for ref in (gain_ref, shift_ref))
    h1 = layer_norm(x_ref[...].astype(jnp.float32), gain, shift).astype(jnp.bfloat16)
    outs[0][...] = jnp.transpose(h1)
    cosine, sine = cos_ref[...], sin_ref[...]
    for index, (weight, out) in enumerate(zip(weights, outs[1:])):
        product = nn(h1, weight[...])
        is_value = index == count - 1
        is_query = count == 3 and index == 0
        if is_value:
            out[...] = product.astype(jnp.bfloat16)
            continue
        for pair in range(product.shape[1] // LANES):
            columns = slice(pair * LANES, (pair + 1) * LANES)
            turned = turn(product[:, columns], cosine, sine)
            if is_query:
                turned = turned * score_scale
            out[:, columns] = turned.astype(jnp.bfloat16)


def project(x, gain, shift, cosine, sine, weights, score_scale):
    rows, width = x.shape
    count = len(weights)
    row_spec = pl.BlockSpec((TILE, width), lambda i: (i, 0))
    table_spec = pl.BlockSpec((TILE, LANES), lambda i: (i, 0))
    whole = pl.BlockSpec((width, width), lambda i: (0, 0))
    line = pl.BlockSpec(gain.shape, lambda i: (0,))
    return pl.pallas_call(
        functools.partial(project_kernel, score_scale),
        grid=(rows // TILE,),
        in_specs=[row_spec, line, line, table_spec, table_spec] + [whole] * count,
        out_specs=[pl.BlockSpec((width, TILE), lambda i: (0, i))] + [row_spec] * count,
        out_shape=[jax.ShapeDtypeStruct((width, rows), jnp.bfloat16)]
        + [jax.ShapeDtypeStruct((rows, width), jnp.bfloat16)] * count,
        compiler_params=pltpu.CompilerParams(vmem_limit_bytes=40 * MIB),
        cost_estimate=pl.CostEstimate(
            flops=2 * rows * width * width * count,
            bytes_accessed=2 * (rows + count * (width + rows)) * width,
            transcendentals=0,
        ),
        name="project%d" % count,
    )(x, gain, shift, cosine, sine, *weights)


def two_heads(block):
    lane = lax.broadcasted_iota(jnp.int32, block.shape, 1)
    zero = jnp.zeros_like(block)
    return jnp.concatenate(
        [jnp.where(lane < 64, block, zero), jnp.where(lane < 64, zero, block)], axis=0
    )


def one_row(both):
    rows = both.shape[0] // 2
    lane = lax.broadcasted_iota(jnp.int32, (rows, LANES), 1)
    return jnp.where(lane < 64, both[:rows], both[rows:])


def subs(both, sub):
    low = sub * SUB
    return jnp.concatenate([both[low : low + SUB], both[TILE + low : TILE + low + SUB]], axis=0)


def front_tiles(rows):
    tiles = [(low, TILE) for low in range(0, rows - TILE, TILE)]
    return tiles + [(rows - TILE, SUB), (rows - SUB, SUB)]


def mask_front(rows, meta_ref, bias, diag):
    columns = jnp.transpose(meta_ref[...])
    noisy = columns[:, 3:4]
    for i, (first, size) in enumerate(front_tiles(rows)):
        band = slice(first, first + size)
        n = first + size
        start, limit = columns[band, 0:1], columns[band, 1:2]
        key = lax.broadcasted_iota(jnp.int32, (size, n), 1)
        query = lax.broadcasted_iota(jnp.int32, (size, n), 0) + first
        usable = (meta_ref[2:3, :n] == 1.0) | (key == query)
        place = key.astype(jnp.float32)
        seen = (place >= start) & (place < limit) & usable
        bias[i][...] = jnp.where(seen, 0.0, masked_score)
        for low in range(first, first + size, SUB):
            key = lax.broadcasted_iota(jnp.int32, (SUB, SUB), 1) + low
            query = lax.broadcasted_iota(jnp.int32, (SUB, SUB), 0) + low
            usable = (meta_ref[2:3, low : low + SUB] == 1.0) | (key == query)
            same = (key // BLOCK == query // BLOCK) & (
                key.astype(jnp.float32) >= columns[low : low + SUB, 0:1]
            )
            seen = same & usable & (noisy[low : low + SUB] == 1.0)
            diag[low : low + SUB, :] = jnp.where(seen, 0.0, masked_score)


def tile_front(i, pair, cols, q_ref, kb_ref, vb_ref, ko_ref, vo_ref, o_ref, bias, diag, lse):
    first, size = front_tiles(o_ref.shape[0])[i]
    band = slice(first, first + size)
    n = first + size
    lane = lax.broadcasted_iota(jnp.int32, (size, LANES), 1)
    q2 = two_heads(q_ref[band, cols])
    b = bias[i][...]
    s = nt(q2, kb_ref[:n, cols]) + jnp.concatenate([b, b], axis=0)
    d = diag[band, :]

    def apart(sub):
        return slice(first + sub * SUB, first + (sub + 1) * SUB)

    def merge(parts):
        return jnp.concatenate([p[:SUB] for p in parts] + [p[SUB:] for p in parts], axis=0)

    def of(both, sub):
        low = sub * SUB
        return jnp.concatenate(
            [both[low : low + SUB], both[size + low : size + low + SUB]], axis=0
        )

    parts = [nt(of(q2, sub), ko_ref[apart(sub), cols]) for sub in range(size // SUB)]
    sd = merge(parts) + jnp.concatenate([d, d], axis=0)
    top = jnp.maximum(jnp.max(s, axis=1, keepdims=True), jnp.max(sd, axis=1, keepdims=True))
    p = jnp.exp(s - top)
    pd = jnp.exp(sd - top)
    total = jnp.sum(p, axis=1, keepdims=True) + jnp.sum(pd, axis=1, keepdims=True)
    pd_low = pd.astype(jnp.bfloat16)
    o = nn(p.astype(jnp.bfloat16), vb_ref[:n, cols])
    parts = [nn(of(pd_low, sub), vo_ref[apart(sub), cols]) for sub in range(size // SUB)]
    o = (o + merge(parts)) * (1.0 / total)
    o_ref[band, cols] = one_row(o).astype(o_ref.dtype)
    level = top + jnp.log(total)
    old = lse[band, :]
    lse[band, :] = jnp.where(
        lane == 2 * pair, level[:size], jnp.where(lane == 2 * pair + 1, level[size:], old)
    )


def attend_kernel(rows, q_ref, kb_ref, vb_ref, ko_ref, vo_ref, meta_ref, o_ref, lse_ref, *refs):
    bias, diag, lse = refs[:-2], refs[-2], refs[-1]
    pair = pl.program_id(0)
    pl.when(pair == 0)(lambda: mask_front(rows, meta_ref, bias, diag))
    for i in range(len(front_tiles(rows))):
        tile_front(
            i, pair, slice(None), q_ref, kb_ref, vb_ref, ko_ref, vo_ref, o_ref, bias, diag, lse
        )

    @pl.when(pair == pl.num_programs(0) - 1)
    def _():
        lse_ref[...] = jnp.transpose(lse[...])[: lse_ref.shape[0], :]


def front_scratch(rows):
    return [pltpu.VMEM((size, low + size), jnp.float32) for low, size in front_tiles(rows)] + [
        pltpu.VMEM((rows, SUB), jnp.float32),
        pltpu.VMEM((rows, LANES), jnp.float32),
    ]


def front_kernel(
    score_scale, x_ref, gain_ref, shift_ref, lengths_ref, pad_ref, wq_ref, wk_ref, wv_ref,
    base_ref, h1t_ref, h1bt_ref, q_ref, kb_ref, vb_ref, ko_ref, vo_ref, o_ref, lse_ref, meta_ref, cos_ref,
    sin_ref, *refs,
):
    *bias, diag, lse, coming, send_sem, recv_sem = refs
    rows, width = x_ref.shape
    stream = lax.axis_index("stream")
    gain, shift = gain_ref[...].reshape(1, width), shift_ref[...].reshape(1, width)
    partner = {"stream": 1 - stream}
    bands = front_tiles(rows)

    def move(r):
        return pltpu.make_async_remote_copy(
            src_ref=x_ref.at[pl.ds(*bands[r])],
            dst_ref=coming.at[pl.ds(*bands[r])],
            send_sem=send_sem.at[r],
            recv_sem=recv_sem.at[r],
            device_id=partner,
            device_id_type=MESH,
        )

    barrier = pltpu.get_barrier_semaphore()
    pl.semaphore_signal(barrier, inc=1, device_id=partner, device_id_type=MESH)
    pl.semaphore_wait(barrier, 1)
    tiles = rows // TILE

    pl.when(stream == 0)(lambda: move(0).start())

    place = lax.broadcasted_iota(jnp.int32, (1, rows), 1)
    end, start = 0, jnp.zeros((1, rows), jnp.int32)
    for slot in range(lengths_ref.shape[1]):
        end = end + lengths_ref[0, slot]
        start = jnp.where(place >= end, end, start)
    limit = (place // BLOCK + 1 - stream) * BLOCK
    lines = [start, limit, pad_ref[...], jnp.zeros_like(place) + stream]
    lines = jnp.concatenate(lines + [jnp.zeros_like(place)] * 4, axis=0).astype(jnp.float32)
    meta_ref[...] = lines
    starts = jnp.transpose(lines)[:, 0:1]
    lane = lax.broadcasted_iota(jnp.int32, (1, LANES), 1)
    index = lax.rem(lane, 32).astype(jnp.float32)
    frequency = jnp.exp(index * (-2.0 * math.log(10000.0) / (width // H)))
    sign = jnp.where(lax.rem(lane, 64) < 32, -1.0, 1.0)
    for r in range(tiles):
        at = slice(r * TILE, (r + 1) * TILE)
        within = lax.broadcasted_iota(jnp.int32, (TILE, 1), 0).astype(jnp.float32) + r * TILE
        turned = (within - starts[at]) * frequency
        cos_ref[at, :] = jnp.cos(turned)
        sin_ref[at, :] = jnp.sin(turned) * sign

    def put(product, out, at, table, scale=None):
        for pair in range(width // LANES):
            cols = slice(pair * LANES, (pair + 1) * LANES)
            turned = turn(product[:, cols], *table)
            if scale is not None:
                turned = turned * scale
            out[at, cols] = turned.astype(jnp.bfloat16)

    def lower(block):
        return layer_norm(block.astype(jnp.float32), gain, shift).astype(jnp.bfloat16)

    @pl.loop(0, tiles)
    def _(r):
        at = pl.ds(pl.multiple_of(r * TILE, TILE), TILE)
        table = cos_ref[at, :], sin_ref[at, :]
        h1 = lower(x_ref[at, :])
        h1t_ref[:, at] = jnp.transpose(h1)
        put(nn(h1, wq_ref[...]), q_ref, at, table, score_scale)
        put(nn(h1, wk_ref[...]), ko_ref, at, table)
        vo_ref[at, :] = nn(h1, wv_ref[...]).astype(jnp.bfloat16)

    @pl.when(stream == 0)
    def _():
        move(0).wait_send()
        move(1).start()

    mask_front(rows, meta_ref, bias, diag)
    for r, (first, size) in enumerate(bands):
        at = slice(first, first + size)

        @pl.when(stream == 0)
        def _(at=at):
            base_ref[at, :] = x_ref[at, :]

        @pl.when(stream == 1)
        def _(r=r, at=at):
            move(r).wait_recv()
            base_ref[at, :] = coming[at, :]

        h1 = lower(base_ref[at, :])
        h1bt_ref[:, at] = jnp.transpose(h1)
        put(nn(h1, wk_ref[...]), kb_ref, at, (cos_ref[at, :], sin_ref[at, :]))
        vb_ref[at, :] = nn(h1, wv_ref[...]).astype(jnp.bfloat16)

        @pl.loop(0, width // LANES)
        def _(pair, r=r):
            cols = pl.ds(pl.multiple_of(pair * LANES, LANES), LANES)
            tile_front(r, pair, cols, q_ref, kb_ref, vb_ref, ko_ref, vo_ref, o_ref, bias, diag, lse)

        if r == 0:
            pl.when(stream == 0)(lambda: move(2).start())
        if r == 1:
            @pl.when(stream == 0)
            def _():
                for later in range(3, len(bands)):
                    move(later).start()

    lse_ref[...] = jnp.transpose(lse[...])[: lse_ref.shape[0], :]

    @pl.when(stream == 0)
    def _():
        for r in range(1, len(bands)):
            move(r).wait_send()


def front(x, gain, shift, lengths, padding, weights, score_scale):
    rows, width = x.shape
    wide = lambda lines, columns: jax.ShapeDtypeStruct((lines, columns), jnp.float32)
    low = jnp.bfloat16
    flat = jax.ShapeDtypeStruct((rows, width), low)
    flipped = jax.ShapeDtypeStruct((width, rows), low)
    vmem = pl.BlockSpec(memory_space=pltpu.VMEM)
    return pl.pallas_call(
        functools.partial(front_kernel, score_scale),
        in_specs=[vmem] * 3 + [pl.BlockSpec(memory_space=pltpu.SMEM)] + [vmem] * 4,
        out_specs=[vmem] * 13,
        out_shape=[flat, flipped, flipped]
        + [flat] * 6
        + [wide(16, rows), wide(8, rows), wide(rows, LANES), wide(rows, LANES)],
        scratch_shapes=front_scratch(rows)
        + [
            pltpu.VMEM((rows, width), low),
            pltpu.SemaphoreType.DMA((len(front_tiles(rows)),)),
            pltpu.SemaphoreType.DMA((len(front_tiles(rows)),)),
        ],
        compiler_params=pltpu.CompilerParams(
            collective_id=1, has_side_effects=True, vmem_limit_bytes=62 * MIB
        ),
        cost_estimate=pl.CostEstimate(
            flops=4 * rows * rows * width + 10 * rows * width * width,
            bytes_accessed=20 * MIB,
            transcendentals=0,
        ),
        name="front",
    )(x, gain, shift, lengths, padding, *weights)


def attend(q, kb, vb, ko, vo, meta):
    rows, width = q.shape
    pairs = width // LANES
    spec = pl.BlockSpec((rows, LANES), lambda j: (0, j))
    return pl.pallas_call(
        functools.partial(attend_kernel, rows),
        grid=(pairs,),
        in_specs=[spec] * 5 + [pl.BlockSpec(meta.shape, lambda j: (0, 0))],
        out_specs=[spec, pl.BlockSpec((16, rows), lambda j: (0, 0))],
        out_shape=[
            jax.ShapeDtypeStruct((rows, width), jnp.bfloat16),
            jax.ShapeDtypeStruct((16, rows), jnp.float32),
        ],
        scratch_shapes=front_scratch(rows),
        compiler_params=pltpu.CompilerParams(vmem_limit_bytes=48 * MIB),
        cost_estimate=pl.CostEstimate(
            flops=2 * 2 * rows * rows * width, bytes_accessed=12 * rows * width, transcendentals=0
        ),
        name="attend",
    )(q, kb, vb, ko, vo, meta)


def mask_back(rows, meta_ref, bias, diag):
    columns = jnp.transpose(meta_ref[...])
    for i in range(rows // TILE):
        band = slice(i * TILE, (i + 1) * TILE)
        n = (i + 1) * TILE
        start, limit = meta_ref[0:1, band], meta_ref[1:2, band]
        key = lax.broadcasted_iota(jnp.int32, (n, TILE), 0)
        query = lax.broadcasted_iota(jnp.int32, (n, TILE), 1) + i * TILE
        usable = (columns[:n, 2:3] == 1.0) | (key == query)
        place = key.astype(jnp.float32)
        seen = (place >= start) & (place < limit) & usable
        bias[i][...] = jnp.where(seen, 0.0, masked_score)
        for sub in range(TILE // SUB):
            low = i * TILE + sub * SUB
            part = slice(low, low + SUB)
            key = lax.broadcasted_iota(jnp.int32, (SUB, SUB), 0) + low
            query = lax.broadcasted_iota(jnp.int32, (SUB, SUB), 1) + low
            usable = (columns[part, 2:3] == 1.0) | (key == query)
            same = (key // BLOCK == query // BLOCK) & (
                key.astype(jnp.float32) >= meta_ref[0:1, part]
            )
            seen = same & usable & (meta_ref[3:4, part] == 1.0)
            diag[:, part] = jnp.where(seen, 0.0, masked_score)


def pair_back(
    rows, score_scale, pair, out_cols, tick, q_ref, kb_ref, vb_ref, ko_ref, vo_ref, o_ref, do_ref, lse_ref,
    cos_ref, sin_ref, dq_ref, dkb_ref, dvb_ref, dko_ref, dvo_ref, bias, diag, dk_sum, dv_sum,
):
    head_lane = lax.broadcasted_iota(jnp.int32, (8, LANES), 1)
    head_row = lax.broadcasted_iota(jnp.int32, (8, LANES), 0)
    pick = jnp.where(head_lane // 64 == head_row, 1.0, 0.0).astype(jnp.bfloat16)
    for i in reversed(range(rows // TILE)):
        band = slice(i * TILE, (i + 1) * TILE)
        n = (i + 1) * TILE
        q2 = two_heads(q_ref[band, :])
        do = do_ref[band, :]
        do2 = two_heads(do)
        prod = do.astype(jnp.float32) * o_ref[band, :].astype(jnp.float32)
        high = prod.astype(jnp.bfloat16)
        rest = (prod - high.astype(jnp.float32)).astype(jnp.bfloat16)
        inner = nt(pick, high) + nt(pick, rest)
        inner = jnp.concatenate([inner[0:1], inner[1:2]], axis=1)
        level = jnp.concatenate(
            [lse_ref[pl.ds(2 * pair, 1), band], lse_ref[pl.ds(2 * pair + 1, 1), band]], axis=1
        )
        b = bias[i][...]
        s = nt(kb_ref[:n, :], q2) + jnp.concatenate([b, b], axis=1)
        p = jnp.exp(s - level)
        dp = nt(vb_ref[:n, :], do2)
        ds = (p * (dp - inner)).astype(jnp.bfloat16)
        dv = nn(p.astype(jnp.bfloat16), do2)
        dk = nn(ds, q2)
        if i == rows // TILE - 1:
            dv_sum[...] = dv
            dk_sum[...] = dk
        else:
            dv_sum[:n, :] += dv
            dk_sum[:n, :] += dk
        dq = tn(ds, kb_ref[:n, :])
        extra = []
        for sub in range(TILE // SUB):
            low = i * TILE + sub * SUB
            part = slice(low, low + SUB)
            qs, dos = subs(q2, sub), subs(do2, sub)
            d = diag[:, part]
            at = slice(sub * SUB, (sub + 1) * SUB)
            at2 = slice(TILE + sub * SUB, TILE + (sub + 1) * SUB)
            lev = jnp.concatenate([level[:, at], level[:, at2]], axis=1)
            inn = jnp.concatenate([inner[:, at], inner[:, at2]], axis=1)
            s = nt(ko_ref[part, :], qs) + jnp.concatenate([d, d], axis=1)
            p = jnp.exp(s - lev)
            dp = nt(vo_ref[part, :], dos)
            ds = (p * (dp - inn)).astype(jnp.bfloat16)
            dvo_ref[part, out_cols] = nn(p.astype(jnp.bfloat16), dos).astype(jnp.bfloat16)
            dko = nn(ds, qs)
            dko_ref[part, out_cols] = turn(dko, cos_ref[part, :], -sin_ref[part, :]).astype(jnp.bfloat16)
            extra.append(tn(ds, ko_ref[part, :]))
        dq = dq + jnp.concatenate(
            [extra[0][:SUB], extra[1][:SUB], extra[0][SUB:], extra[1][SUB:]], axis=0
        )
        dq = one_row(dq) * score_scale
        dq_ref[band, out_cols] = turn(dq, cos_ref[band, :], -sin_ref[band, :]).astype(jnp.bfloat16)
        tick(rows // TILE - i)
    dvb_ref[:, out_cols] = dv_sum[...].astype(jnp.bfloat16)
    dkb_ref[:, out_cols] = turn(dk_sum[...], cos_ref[...], -sin_ref[...]).astype(jnp.bfloat16)


def attend_back_kernel(
    rows, score_scale, q_ref, kb_ref, vb_ref, ko_ref, vo_ref, o_ref, do_ref, lse_ref, meta_ref, cos_ref, sin_ref,
    *refs,
):
    pair = pl.program_id(0)
    dq_ref, dkb_ref, dvb_ref, dko_ref, dvo_ref, *bias, diag, dk_sum, dv_sum = refs
    pl.when(pair == 0)(lambda: mask_back(rows, meta_ref, bias, diag))
    pair_back(
        rows, score_scale, pair, slice(None), lambda slot: None, q_ref, kb_ref, vb_ref, ko_ref, vo_ref, o_ref,
        do_ref, lse_ref, cos_ref, sin_ref, dq_ref, dkb_ref, dvb_ref, dko_ref, dvo_ref, bias, diag, dk_sum,
        dv_sum,
    )


def back_scratch(rows):
    return [pltpu.VMEM(((i + 1) * TILE, TILE), jnp.float32) for i in range(rows // TILE)] + [
        pltpu.VMEM((SUB, rows), jnp.float32),
        pltpu.VMEM((rows, LANES), jnp.float32),
        pltpu.VMEM((rows, LANES), jnp.float32),
    ]


def attend_back(q, kb, vb, ko, vo, o, do, lse, meta, cosine, sine, score_scale):
    rows, width = q.shape
    pairs = width // LANES
    spec = pl.BlockSpec((rows, LANES), lambda j: (0, j))
    whole = lambda a: pl.BlockSpec(a.shape, lambda j: (0, 0))
    return pl.pallas_call(
        functools.partial(attend_back_kernel, rows, score_scale),
        grid=(pairs,),
        in_specs=[spec] * 7 + [whole(lse), whole(meta), whole(cosine), whole(sine)],
        out_specs=[spec] * 5,
        out_shape=[jax.ShapeDtypeStruct((rows, width), jnp.bfloat16)] * 5,
        scratch_shapes=back_scratch(rows),
        compiler_params=pltpu.CompilerParams(vmem_limit_bytes=48 * MIB),
        cost_estimate=pl.CostEstimate(
            flops=5 * 2 * rows * rows * width, bytes_accessed=24 * rows * width, transcendentals=0
        ),
        name="attend_back",
    )(q, kb, vb, ko, vo, o, do, lse, meta, cosine, sine)


F1, OUT, F2, P0, P1, P2, N = range(7)
TAIL_STREAMS = (
    ("lyxh", 1024), ("xylh", 384), ("yxlh", 1024), ("xylh", 384), ("xylh", 384), ("ylhx", 384), ("lyhx", 128),
)
TAIL_FAR = 3
FEEDS = (F1, F2)
TAIL_TICKS = {
    (0, 3): [(F2, 0)],
    (1, 1): [(OUT, 0)],
    (1, 2): [(F1, 0)],
    (2, 2): [(OUT, 1), (P0, 0)],
    (3, 3): [(F2, 1)],
    (3, 5): [(OUT, 2), (P0, 1)],
    (4, 1): [(F1, 1)],
    (4, 2): [(P1, 0)],
    (4, 3): [(OUT, 3)],
    (5, 1): [(P0, 2), (F2, 2)],
    (5, 3): [(OUT, 4)],
    (5, 5): [(P0, 3), (P1, 1), (F1, 2)],
}
TAIL_POST = {
    0: [(F2, 3)],
    1: [(P2, 0)],
    2: [(P0, 4)],
    3: [(P1, 2)],
    4: [(F1, 3)],
    5: [(F2, 4), (N, 0), (P1, 3)],
    6: [(P2, 1), (N, 1), (F1, 4), (P1, 4), (N, 2), (P2, 2)],
    7: [(N, 3), (P2, 3), (N, 4)],
    8: [(P2, 4)],
}


def normalized(x):
    x = x.astype(jnp.float32)
    centre = x - jnp.mean(x, axis=-1, keepdims=True)
    inverse = lax.rsqrt(jnp.mean(centre * centre, axis=-1, keepdims=True) + epsilon)
    return centre * inverse, inverse


def normal_back(grad, gain, n, inverse):
    e = grad * gain
    return inverse * (
        e - jnp.mean(e, axis=-1, keepdims=True) - n * jnp.mean(e * n, axis=-1, keepdims=True)
    )


def tail_kernel(
    rows, score_scale, q_ref, kb_ref, vb_ref, ko_ref, vo_ref, o_ref, do_ref, lse_ref, meta_ref, cos_ref, sin_ref,
    h1t_ref, h1bt_ref, gain_ref, norm_ref, first_ref, *refs,
):
    pair = pl.program_id(0)
    hbm, refs = refs[:6], refs[6:]
    ff_ref, go_ref, refs = refs[0], refs[1], refs[2:]
    out_ref, up_out, down_out, head_out, norm_out, refs = *refs[:5], refs[5:]
    scratch, refs = refs[:7], refs[7:]
    bias, (diag, dk_sum, dv_sum) = scratch[:4], scratch[4:]
    dq, dkb, dvb, dko, dvo, refs = *refs[:5], refs[5:]
    held, refs = refs[:5], refs[5:]
    wq, wk, wv, x, base = held
    coming, pair_sums, norm_sums, refs = refs[0], refs[1:4], refs[4], refs[5:]
    load_sem, send_sem, recv_sem, refs = refs[0], refs[1], refs[2], refs[3:]
    sources = [(ff_ref.at[1], 0), (go_ref, 0), (ff_ref.at[2], 0)]
    sources += [(ref, 0) for ref in (*pair_sums, norm_sums)]
    scatter = Scatter(TAIL_STREAMS, sources, refs, TAIL_FAR)
    stream = lax.axis_index("stream")
    tiles = rows // TILE
    width = x.shape[1]
    loads = [
        pltpu.make_async_copy(src, dst, load_sem.at[i])
        for i, (src, dst) in enumerate(zip(hbm, (*held, out_ref)))
    ]

    def tick(slot):
        for at, moves in TAIL_TICKS.items():
            if at[1] == slot:
                @pl.when(pair == at[0])
                def _(moves=moves):
                    for number, index in moves:
                        scatter.step(number, index)

    def post(slot):
        for number, index in TAIL_POST.get(slot, ()):
            scatter.step(number, index)

    @pl.when(pair == 0)
    def _():
        scatter.greet()
        scatter.open((F2, OUT, F1))
        for load in loads:
            load.start()
        mask_back(rows, meta_ref, bias, diag)

    cols = pl.ds(pl.multiple_of(pair * LANES, LANES), LANES)
    pair_back(
        rows, score_scale, pair, cols, tick, q_ref, kb_ref, vb_ref, ko_ref, vo_ref, o_ref,
        do_ref, lse_ref, cos_ref, sin_ref, dq, dkb, dvb, dko, dvo, bias, diag, dk_sum, dv_sum,
    )

    for number, sums in enumerate(pair_sums):
        @pl.when(pair == 2 * number + 1)
        def _(number=number, sums=sums):
            both = slice(2 * number * LANES, (2 * number + 2) * LANES)
            for at, block in enumerate((
                nn(h1t_ref[...], dq[:, both]),
                nn(h1t_ref[...], dko[:, both]) + nn(h1bt_ref[...], dkb[:, both]),
                nn(h1t_ref[...], dvo[:, both]) + nn(h1bt_ref[...], dvb[:, both]),
            )):
                block = block.astype(jnp.bfloat16)
                for half in range(2):
                    sums[half, :, :, :, :, :, at * LANES : (at + 1) * LANES] = block[
                        :, half * LANES : (half + 1) * LANES
                    ].reshape(2, 2, 2, 2, RUN, LANES)
            scatter.open((P0 + number,))

    tick(tiles + 1)

    @pl.when(pair == pl.num_programs(0) - 1)
    def _():
        for load in loads:
            load.wait()
        gain = gain_ref[...].reshape(1, width)

        def band(r):
            return slice(r * TILE, (r + 1) * TILE)

        def move(r):
            return pltpu.make_async_remote_copy(
                src_ref=dkb.at[band(r)],
                dst_ref=coming.at[band(r)],
                send_sem=send_sem.at[r],
                recv_sem=recv_sem.at[r],
                device_id=scatter.to["x"],
                device_id_type=MESH,
            )

        gain_sum = jnp.zeros((1, width), jnp.float32)
        bias_sum = jnp.zeros((1, width), jnp.float32)
        for r in range(tiles):
            at = band(r)
            grad = nt(dkb[at, :], wk[...]) + nt(dvb[at, :], wv[...])
            dkb[at, :] = grad.astype(jnp.bfloat16)
            pl.when(stream == 1)(lambda r=r: move(r).start())
            n, _ = normalized(base[at, :])
            gain_sum += jnp.sum(grad * n, axis=0, keepdims=True)
            bias_sum += jnp.sum(grad, axis=0, keepdims=True)
        post(0)
        for r in range(tiles):
            at = band(r)
            grad = nt(dq[at, :], wq[...]) + nt(dko[at, :], wk[...]) + nt(dvo[at, :], wv[...])
            n, inverse = normalized(x[at, :])
            gain_sum += jnp.sum(grad * n, axis=0, keepdims=True)
            bias_sum += jnp.sum(grad, axis=0, keepdims=True)
            grad = grad + jnp.where(stream == 0, dkb[at, :].astype(jnp.float32), 0.0)
            out_ref[at, :] += normal_back(grad, gain, n, inverse)
            post(r + 1)
        eye = jnp.where(
            lax.broadcasted_iota(jnp.int32, (8, LANES), 0)
            == lax.broadcasted_iota(jnp.int32, (8, LANES), 1),
            1.0,
            0.0,
        ).astype(jnp.bfloat16)
        zero = jnp.zeros((6, width), jnp.float32)
        for half, sums in enumerate((
            jnp.concatenate([gain_sum, bias_sum, zero], axis=0), norm_ref[...]
        )):
            block = tn(sums.astype(jnp.bfloat16), eye).astype(jnp.bfloat16)
            norm_sums[half] = block.reshape(2, 2, 2, 2, RUN, LANES)
        scatter.open((N,))
        post(tiles + 1)
        for r in range(tiles):
            at = band(r)

            @pl.when(stream == 1)
            def _(r=r):
                move(r).wait_send()

            @pl.when(stream == 0)
            def _(r=r, at=at):
                move(r).wait_recv()
                n, inverse = normalized(x[at, :])
                out_ref[at, :] += normal_back(coming[at, :].astype(jnp.float32), gain, n, inverse)

            post(tiles + 2 + r)
        scatter.finish()
        places = [sum(part for _, part in TAIL_STREAMS[:i]) for i in range(len(TAIL_STREAMS))]
        for half, out in enumerate((up_out, down_out)):
            out[:, : first_ref.shape[2]] = first_ref[half]
            low = first_ref.shape[2]
            for number in FEEDS:
                part = TAIL_STREAMS[number][1]
                out[:, low : low + part] = scatter.result(half, places[number], part)
                low += part
        middle = width // 2
        for half in range(2):
            head_out[0, :, half * middle : (half + 1) * middle] = scatter.result(
                half, places[OUT], middle
            )
            norm_out[half] = scatter.result(half, places[N], LANES)
            for number in range(len(pair_sums)):
                low = (2 * number + half) * LANES
                for at in range(3):
                    head_out[1 + at, :, low : low + LANES] = scatter.result(
                        half, places[P0 + number] + at * LANES, LANES
                    )


def tail(
    operands, h1t, h1bt, gain, norm, first, weights, x, base, middle_grad, ff, go, score_scale
):
    rows, width = x.shape
    pairs = width // LANES
    hidden = first.shape[2] + sum(TAIL_STREAMS[number][1] for number in FEEDS)
    shapes = [(rows, width), (24, hidden), (24, hidden), (4, 24, width), (2, 24, LANES)]
    spec = pl.BlockSpec((rows, LANES), lambda j: (0, j))
    once = pl.Buffered(1)
    whole = lambda shape: pl.BlockSpec(shape, lambda j: (0,) * len(shape), pipeline_mode=once)
    flat, square = (rows, width), (width, width)
    low = jnp.bfloat16
    scratch = back_scratch(rows)
    scratch += [pltpu.VMEM(flat, low)] * 5
    scratch += [pltpu.VMEM(square, low)] * 3 + [pltpu.VMEM(flat, low)] * 2
    scratch += [pltpu.VMEM(flat, low)]
    scratch += [pltpu.VMEM((2, 2, 2, 2, 2, RUN, 3 * LANES), low)] * 3
    scratch += [pltpu.VMEM((2, 2, 2, 2, 2, RUN, LANES), low)]
    scratch += [pltpu.SemaphoreType.DMA((6,))]
    scratch += [pltpu.SemaphoreType.DMA((rows // TILE,))] * 2
    scratch += Scatter.shapes(TAIL_STREAMS, TAIL_FAR)
    return pl.pallas_call(
        functools.partial(tail_kernel, rows, score_scale),
        grid=(pairs,),
        in_specs=[spec] * 7
        + [whole(a.shape) for a in (*operands[7:], h1t, h1bt, gain, norm, first)]
        + [pl.BlockSpec(memory_space=pl.ANY)] * 8,
        out_specs=[whole(shape) for shape in shapes],
        out_shape=[jax.ShapeDtypeStruct(shape, jnp.float32) for shape in shapes],
        scratch_shapes=scratch,
        compiler_params=pltpu.CompilerParams(
            collective_id=0, has_side_effects=True, vmem_limit_bytes=63 * MIB
        ),
        cost_estimate=pl.CostEstimate(
            flops=10 * rows * rows * width + 20 * rows * width * width,
            bytes_accessed=40 * MIB,
            transcendentals=0,
        ),
        name="tail",
    )(*operands, h1t, h1bt, gain, norm, first, *weights, x, base, middle_grad, ff, go)


FEED_TILE = 1024
FEED_STREAMS = (("yxlh", 512), ("xylh", 512))
FEED_TICKS = {
    (1, 1): [(0, 0), (1, 0)], (1, 5): [(0, 1), (1, 1)], (2, 1): [(0, 2), (1, 2)], (2,5): [(0, 3), (1, 3)], (2,6): [(0, 4), (1, 4)],
}


def feed_kernel(
    streams, x_ref, o_ref, dy_ref, wo_ref, gain_ref, shift_ref, wu_ref, wd_ref,
    y_ref, do_ref, dx_ref, norm_ref, ff_ref, go_ref, *refs,
):
    f = pl.program_id(0)
    rows, width = x_ref.shape
    gain, shift = gain_ref[...].reshape(1, width), shift_ref[...].reshape(1, width)
    scatter = None
    if streams:
        out_ref, refs = refs[0], refs[1:]
    total, normal, scale, h2s, h2t, dyt, gs, dus = refs[:8]
    if streams:
        first = refs[8]
        sources, low = [], 0
        for _, part in streams:
            sources.append((first, low))
            low += part
        scatter = Scatter(streams, sources, refs[9:], 0)

    def tick(slot):
        if scatter is None:
            return
        for at, moves in FEED_TICKS.items():
            if at[1] == slot:
                @pl.when(f == at[0])
                def _(moves=moves):
                    for stream, index in moves:
                        scatter.step(stream, index)

    def band(r):
        return pl.ds(pl.multiple_of(r * TILE, TILE), TILE)

    @pl.when(f == 0)
    def _():
        if scatter is not None:
            scatter.greet()
        norm_ref[...] = jnp.zeros_like(norm_ref)

        @pl.loop(0, rows // TILE)
        def _(r):
            at = band(r)
            x1 = x_ref[at, :].astype(jnp.float32) + nn(o_ref[at, :], wo_ref[...])
            centre = x1 - jnp.mean(x1, axis=-1, keepdims=True)
            inverse = lax.rsqrt(jnp.mean(centre * centre, axis=-1, keepdims=True) + epsilon)
            n = centre * inverse
            h2 = (n * gain + shift).astype(jnp.bfloat16)
            total[at, :] = x1
            normal[at, :] = n
            scale[at, :] = jnp.broadcast_to(inverse, (TILE, LANES))
            h2s[at, :] = h2
            h2t[:, at] = jnp.transpose(h2)
            dyt[:, at] = jnp.transpose(dy_ref[at, :])
            dx_ref[at, :] = jnp.zeros((TILE, width), jnp.float32)

    for r in range(rows // TILE):
        at = band(r)
        u = nn(h2s[at, :], wu_ref[...])
        square = u * u
        curve = jnp.tanh(0.7978845608028654 * u * (1.0 + 0.044715 * square))
        upper = 0.5 * (1.0 + curve)
        g = (u * upper).astype(jnp.bfloat16)
        slope = upper + u * upper * (1.0 - curve) * (
            0.7978845608028654 + 3 * 0.044715 * 0.7978845608028654 * square
        )
        gs[at, :] = g
        total[at, :] += nn(g, wd_ref[...])
        du = (nt(dy_ref[at, :], wd_ref[...]) * slope).astype(jnp.bfloat16)
        dus[at, :] = du
        dx_ref[at, :] += nt(du, wu_ref[...])
        tick(r)
    slot = rows // TILE
    for half, (left, right) in enumerate(((h2t, dus), (dyt, gs))):
        for c in range(right.shape[1] // TILE):
            cols = pl.ds(c * TILE, TILE)
            block = nn(left[...], right[:, cols]).astype(jnp.bfloat16)
            block = block.reshape(2, 2, 2, 2, RUN, TILE)
            ff_ref[0, half, :, :, :, :, :, cols] = block
        tick(slot + half)
    if scatter is not None:
        @pl.when(f == 0)
        def _():
            @pl.loop(0, 32)
            def _(i):
                at = (i // 16, i // 8 % 2, i // 4 % 2, i // 2 % 2, i % 2)
                first[at] = ff_ref[(0,) + at]

            scatter.open(range(len(streams)))

    @pl.when(f == pl.num_programs(0) - 1)
    def _():
        @pl.loop(0, rows // TILE)
        def _(r):
            at = band(r)
            y_ref[at, :] = total[at, :].astype(jnp.bfloat16)
            n = normal[at, :]
            dh2 = dx_ref[at, :]
            norm_ref[0:1, :] += jnp.sum(dh2 * n, axis=0, keepdims=True)
            norm_ref[1:2, :] += jnp.sum(dh2, axis=0, keepdims=True)
            e = dh2 * gain
            e = (
                e
                - jnp.mean(e, axis=-1, keepdims=True)
                - n * jnp.mean(e * n, axis=-1, keepdims=True)
            )
            dx = dy_ref[at, :].astype(jnp.float32) + scale[at, 0:1] * e
            dx_ref[at, :] = dx
            da = dx.astype(jnp.bfloat16)
            dyt[:, at] = jnp.transpose(da)
            do_ref[at, :] = nt(da, wo_ref[...]).astype(jnp.bfloat16)

        middle = width // 2
        for half in range(2):
            block = nn(dyt[...], o_ref[:, half * middle : (half + 1) * middle])
            go_ref[half] = block.astype(jnp.bfloat16).reshape(2, 2, 2, 2, RUN, middle)
        tick(slot + 2)
        if scatter is not None:
            scatter.finish()
            for half in range(2):
                out_ref[half] = scatter.result(half, 0, out_ref.shape[2])


def feed(x, o, dy, wo, gain, shift, wu, wd, streams):
    rows, width = x.shape
    tiles = wu.shape[1] // FEED_TILE
    once = pl.Buffered(1)
    whole = lambda shape: pl.BlockSpec(shape, lambda f: (0,) * len(shape), pipeline_mode=once)
    flat, square = (rows, width), (width, width)
    parts = (2, 2, 2, 2, RUN)
    out_specs = [
        whole(flat),
        whole(flat),
        whole(flat),
        whole((8, width)),
        pl.BlockSpec((1, 2) + parts + (FEED_TILE,), lambda f: (f,) + (0,) * 7),
        whole((2,) + parts + (width // 2,)),
    ]
    out_shape = [
        jax.ShapeDtypeStruct(flat, jnp.bfloat16),
        jax.ShapeDtypeStruct(flat, jnp.bfloat16),
        jax.ShapeDtypeStruct(flat, jnp.float32),
        jax.ShapeDtypeStruct((8, width), jnp.float32),
        jax.ShapeDtypeStruct((tiles, 2) + parts + (FEED_TILE,), jnp.bfloat16),
        jax.ShapeDtypeStruct((2,) + parts + (width // 2,), jnp.bfloat16),
    ]
    scratch = [
        pltpu.VMEM(flat, jnp.float32),
        pltpu.VMEM(flat, jnp.float32),
        pltpu.VMEM((rows, LANES), jnp.float32),
        pltpu.VMEM(flat, jnp.bfloat16),
        pltpu.VMEM((width, rows), jnp.bfloat16),
        pltpu.VMEM((width, rows), jnp.bfloat16),
        pltpu.VMEM((rows, FEED_TILE), jnp.bfloat16),
        pltpu.VMEM((rows, FEED_TILE), jnp.bfloat16),
    ]
    options = {}
    if streams:
        out_specs += [whole((2, 24, FEED_TILE))]
        out_shape += [jax.ShapeDtypeStruct((2, 24, FEED_TILE), jnp.float32)]
        scratch += [pltpu.VMEM((2,) + parts + (FEED_TILE,), jnp.bfloat16)]
        scratch += Scatter.shapes(streams, 0)
        options = {"collective_id": 2, "has_side_effects": True}
    return pl.pallas_call(
        functools.partial(feed_kernel, streams),
        grid=(tiles,),
        in_specs=[
            whole(flat),
            whole(flat),
            whole(flat),
            whole(square),
            whole(gain.shape),
            whole(shift.shape),
            pl.BlockSpec((width, FEED_TILE), lambda f: (0, f)),
            pl.BlockSpec((FEED_TILE, width), lambda f: (f, 0)),
        ],
        out_specs=out_specs,
        out_shape=out_shape,
        scratch_shapes=scratch,
        compiler_params=pltpu.CompilerParams(vmem_limit_bytes=62 * MIB, **options),
        cost_estimate=pl.CostEstimate(
            flops=12 * rows * width * wu.shape[1] + 6 * rows * width * width,
            bytes_accessed=30 * MIB,
            transcendentals=0,
        ),
        name="feed",
    )(x, o, dy, wo, gain, shift, wu, wd)


def settle_kernel(y, t, up, heads, norms, *refs):
    y_out, t_out, first, q, k, v, second, up_out = refs
    y_out[...] = y[...]
    t_out[...] = t[...]

    @pl.when(pl.program_id(0) == 0)
    def _():
        up_out[...] = up[...]
        for number, ref in enumerate((q, k, v)):
            ref[...] = heads[1 + number]
        first[...] = jnp.transpose(norms[0])[:2, :]
        second[...] = jnp.transpose(norms[1])[:2, :]


def settle(y, t, up, heads, norms):
    wide = lambda *shape: jax.ShapeDtypeStruct(shape, jnp.float32)
    lines = up.shape[0]
    rows, width = y.shape
    band = pl.BlockSpec((rows // 4, width), lambda r: (r, 0))
    whole = lambda shape: pl.BlockSpec(shape, lambda r: (0,) * len(shape))
    head = wide(lines, width)
    pair = wide(2, lines)
    small = [pair, head, head, head, pair, wide(*up.shape)]
    return pl.pallas_call(
        settle_kernel,
        grid=(4,),
        in_specs=[band, band, whole(up.shape), whole(heads.shape), whole(norms.shape)],
        out_specs=[band, band] + [whole(part.shape) for part in small],
        out_shape=[jax.ShapeDtypeStruct(y.shape, y.dtype), wide(rows, width)] + small,
        compiler_params=pltpu.CompilerParams(vmem_limit_bytes=63 * MIB),
        name="settle",
    )(y, t, up, heads, norms)


def shards(
    tokens,
    lengths,
    pad_mask,
    first_gain,
    first_bias,
    query_weight,
    key_weight,
    value_weight,
    out_weight,
    second_gain,
    second_bias,
    up_weight,
    down_weight,
    output_grad,
):
    total_rows = tokens.shape[1]
    model_width = tokens.shape[2]
    head_width = model_width // H
    score_scale = head_width ** (-0.5)
    is_noisy = lax.axis_index("stream") == 1
    own = tokens[0]
    weights = (query_weight, key_weight, value_weight)
    ring = lax.axis_size("dp") == 16 and lax.axis_size("stream") == 2
    if ring:
        base, h1t, h1bt, q, kb, vb, ko, vo, mixed_low, lse, meta, cosine, sine = front(
            own, first_gain, first_bias, lengths, pad_mask[None], weights, score_scale
        )
    else:
        places, first_place = layout(lengths[0], total_rows, lengths.shape[1])
        limit = (places // BLOCK + jnp.where(is_noisy, 0, 1)) * BLOCK
        noisy_row = jnp.broadcast_to(jnp.where(is_noisy, 1, 0), places.shape)
        blank = jnp.zeros_like(places)
        meta = jnp.stack(
            [first_place, limit, pad_mask, noisy_row, blank, blank, blank, blank]
        ).astype(jnp.float32)
        cosine, sine = angle_tables(places - first_place, head_width)
        far = lax.ppermute(own, "stream", [(0, 1)])
        base = jnp.where(is_noisy, far, own)
        norms = (first_gain, first_bias)
        h1t, q, ko, vo = project(own, *norms, cosine, sine, weights, score_scale)
        h1bt, kb, vb = project(base, *norms, cosine, sine, weights[1:], score_scale)
        mixed_low, lse = attend(q, kb, vb, ko, vo, meta)

    fed = feed(
        own, mixed_low, output_grad[0], out_weight, second_gain, second_bias, up_weight, down_weight, FEED_STREAMS if ring else (),
    )
    layer_output, mixed_grad, middle_grad, norm_sums, ff_part, out_part = fed[:6]
    layer_output = layer_output[None]
    operands = (q, kb, vb, ko, vo, mixed_low, mixed_grad, lse, meta, cosine, sine)
    if ring:
        tokens_grad, up_grad, down_grad, heads, norms = tail(
            operands, h1t, h1bt, first_gain, norm_sums, fed[6], weights, own, base, middle_grad, ff_part,
            out_part, score_scale,
        )
        y, t, first, q, k, v, second, up = settle(fed[0], tokens_grad, up_grad, heads, norms)
        return (y[None], t[None], first, q, k, v, heads[0].T, second, up, down_grad.T)
    else:
        dq, dkb, dvb, dko, dvo = attend_back(*operands, score_scale)
        base_grad = nt(dkb, key_weight) + nt(dvb, value_weight)
        back = lax.ppermute(base_grad.astype(jnp.bfloat16), "stream", [(1, 0)])
        normed_grad = (
            nt(dq, query_weight)
            + nt(dko, key_weight)
            + nt(dvo, value_weight)
            + jnp.where(is_noisy, 0.0, base_grad + back.astype(jnp.float32))
        )
        inputs = own.astype(jnp.float32)
        first_pull = jax.vjp(layer_norm, inputs, first_gain, first_bias)[1]
        input_part, first_gain_part, first_bias_part = first_pull(normed_grad)
        tokens_grad = (middle_grad + input_part)[None]
        ff_part = ff_part.reshape(-1, 2, model_width, FEED_TILE)
        out_part = out_part.reshape(2, model_width, model_width // 2)
        norm_part = jnp.stack(
            [first_gain_part, first_bias_part, norm_sums[0], norm_sums[1]], axis=1
        )
        part = jnp.concatenate(
            [ff_part[f, i] for i in range(2) for f in range(ff_part.shape[0])]
            + [out_part[0], out_part[1], nn(h1t, dq).astype(jnp.bfloat16)]
            + [(nn(h1t, dko) + nn(h1bt, dkb)).astype(jnp.bfloat16)]
            + [(nn(h1t, dvo) + nn(h1bt, dvb)).astype(jnp.bfloat16)]
            + [jnp.pad(norm_part, ((0, 0), (0, LANES - 4))).astype(jnp.bfloat16)],
            axis=1,
        )
        part = lax.psum_scatter(part, ("stream", "dp"), scatter_dimension=0, tiled=True)
        part = part.astype(jnp.float32)
        hidden_width = up_weight.shape[1]
        cuts = (hidden_width, hidden_width) + (model_width,) * 4 + (LANES,)
        pieces, low = [], 0
        for cut in cuts:
            pieces.append(part[:, low : low + cut])
            low += cut
        up_grad, down_grad, out_grad, query_grad, key_grad, value_grad, norms = pieces
        first_grads, second_grads = norms[:, :2].T, norms[:, 2:4].T
    return (
        layer_output,
        tokens_grad,
        first_grads,
        query_grad,
        key_grad,
        value_grad,
        out_grad.T,
        second_grads,
        up_grad,
        down_grad.T,
    )


def solution(mesh):
    placed = (
        P("stream", "dp", None),
        P("dp", None),
        P("dp"),
        P(),
        P(),
        P(),
        P(),
        P(),
        P(),
        P(),
        P(),
        P(),
        P(),
        P("stream", "dp", None),
    )
    return jax.shard_map(
        shards,
        mesh=mesh,
        in_specs=placed,
        out_specs=(
            P("stream", "dp", None),
            P("stream", "dp", None),
            P(None, ("stream", "dp")),
            P(("stream", "dp"), None),
            P(("stream", "dp"), None),
            P(("stream", "dp"), None),
            P(None, ("stream", "dp")),
            P(None, ("stream", "dp")),
            P(("stream", "dp"), None),
            P(None, ("stream", "dp")),
        ),
        check_vma=False,
    )
```
